32 devices in a mesh: freq: 2 (over x), tm: 8 (over z, core), batch: 2 (over y).
Axes of the slice: x: 2, y: 2, z: 4, core: 2. Of those that a mesh axis runs over, the one named last changes fastest.
Arguments:
- patches: bfloat16 [16, 8, 256, 384], P('batch', 'freq', 'tm'), may hold values from -6 to 6
- patch_mask: int32 [16, 8, 256], P('batch', 'freq', 'tm'), may hold values 0 or 1
- clip_lengths: int32 [16], P('batch'), may hold values from 1 to 256
- target_index: int32 [16, 8, 256], P('batch', 'freq', 'tm'), may hold values from 0 to 127
- targets: bfloat16 [16, 128, 384], P('batch'), may hold values from -0.41992188 to 0.41992188
- out_grad: bfloat16 [16, 8, 256, 384], P('batch', 'freq', 'tm'), may hold values from -6 to 6
- mask_embed: bfloat16 [384], replicated, may hold values from -4 to 4
- ln1_gain: bfloat16 [384], replicated, may hold values from 0.25 to 1.75
- ln1_shift: bfloat16 [384], replicated, may hold values from -1.5 to 1.5
- w_qkv: bfloat16 [384, 1152], replicated, may hold values from -0.3125 to 0.3125
- bias_q: bfloat16 [384], replicated, may hold values from -1.5 to 1.5
- bias_v: bfloat16 [384], replicated, may hold values from -0.25 to 0.25
- w_out: bfloat16 [384, 384], replicated, may hold values from -1.5 to 1.5
- bias_out: bfloat16 [384], replicated, may hold values from -1.5 to 1.5
- ln2_gain: bfloat16 [384], replicated, may hold values from 0.25 to 1.75
- ln2_shift: bfloat16 [384], replicated, may hold values from -1.5 to 1.5
- w_up: bfloat16 [384, 1536], replicated, may hold values from -0.3125 to 0.3125
- bias_up: bfloat16 [1536], replicated, may hold values from -1.5 to 1.5
- w_down: bfloat16 [1536, 384], replicated, may hold values from -0.15625 to 0.15625
- bias_down: bfloat16 [384], replicated, may hold values from -1.5 to 1.5
Outputs:
- block_out: bfloat16 [16, 8, 256, 384], P('batch', 'freq', 'tm')
- input_grad: bfloat16 [16, 8, 256, 384], P('batch', 'freq', 'tm')
- grad_mask_embed: float32 [384], replicated
- grad_ln1_gain: float32 [384], replicated
- grad_ln1_shift: float32 [384], replicated
- grad_w_qkv: float32 [384, 1152], replicated
- grad_bias_q: float32 [384], replicated
- grad_bias_v: float32 [384], replicated
- grad_w_out: float32 [384, 384], replicated
- grad_bias_out: float32 [384], replicated
- grad_ln2_gain: float32 [384], replicated
- grad_ln2_shift: float32 [384], replicated
- grad_w_up: float32 [384, 1536], replicated
- grad_bias_up: float32 [1536], replicated
- grad_w_down: float32 [1536, 384], replicated
- grad_bias_down: float32 [384], replicated
- soft_accuracy: float32 [16], P('batch')
The draws below stay inside these ranges and needn't reach their ends.
All inputs are finite; a program needn't handle non-finite values. No bound on the sum of `patch_mask` on one device may be relied on, other than what follows from the above.
Results may differ from the reference program's by a relative error of at most 0.014.
Values may be sent and summed in bfloat16 or wider, within the bound.
A program may use at most 256 MiB of HBM per device.

```python
import jax
import jax.numpy as jnp
from jax import lax

D = 384
HEADS = 6
HEAD_DIM = 64
FF = 1536
NF = 8
T_LEN = 256
NCAND = 128
CLIPS = 16


def draw_clip_lengths(key, part):
    first, second, third = jax.random.split(key, 3)
    left_draw = jax.random.randint(first, (CLIPS,), 1, T_LEN + 1)
    right_draw = jax.random.randint(second, (CLIPS,), 1, T_LEN + 1)
    shorter = jnp.maximum(left_draw * right_draw // T_LEN, 1)
    chosen = jax.random.randint(third, (CLIPS // 4,), 0, 4)
    within = jnp.arange(CLIPS) % 4
    longest = within == jnp.repeat(chosen, 4)
    return jnp.where(longest, T_LEN, shorter).astype(jnp.int32)


def with_ends(array, own_key, least, high):
    dims = array.shape
    place = [jax.random.randint(jax.random.fold_in(own_key, axis), (), 0, dims[axis]) for axis in range(len(dims))]
    array = array.at[tuple(place)].set(least)
    longest = dims.index(max(dims))
    place[longest] = (place[longest] + 1) % dims[longest]
    return array.at[tuple(place)].set(high)


def block_scale(rng, shape, cuts, smallest, high):
    loudness = 1.0
    for dim, blocks in cuts:
        draws = jax.random.uniform(jax.random.fold_in(jax.random.fold_in(rng, 6), dim), (blocks,), jnp.float32, smallest / len(cuts), high / len(cuts))
        loudness = loudness * jnp.repeat(jnp.exp(draws), shape[dim] // blocks).reshape((-1,) + (1,) * (len(shape) - 1 - dim))
    return loudness


def scatter_about(own_key, shape, scale, bound, shards=(), kind=jnp.bfloat16):
    drawn = jax.random.normal(own_key, shape, jnp.float32) * scale
    if len(shards) > 0:
        drawn = block_scale(own_key, shape, shards, -0.22, 0.18) * drawn
    return jnp.clip(drawn, min=-bound, max=bound).astype(kind)


def setup_inputs(seed: int = 0) -> dict:
    key_of = jax.random.split(jax.random.key(seed), 21)
    patches = scatter_about(key_of[0], (CLIPS, NF, T_LEN, D), 1.0, 6.0, ((0, 2), (1, 2), (2, 8)))
    patch_mask = with_ends((jax.random.randint(key_of[1], (CLIPS, NF, T_LEN), 0, 5) < 2).astype(jnp.int32), jax.random.fold_in(key_of[1], 1), 0, 1)
    clip_lengths = draw_clip_lengths(jax.random.fold_in(key_of[20], 71), 0)
    target_index = with_ends(jax.random.randint(key_of[3], (CLIPS, NF, T_LEN), 0, NCAND), jax.random.fold_in(key_of[3], 1), 0, NCAND - 1).astype(jnp.int32)
    targets = scatter_about(key_of[4], (CLIPS, NCAND, D), 0.07, 0.41992188, ((0, 2),))
    out_grad = scatter_about(key_of[5], (CLIPS, NF, T_LEN, D), 1.0, 6.0, ((0, 2), (1, 2), (2, 8)))
    mask_embed = scatter_about(key_of[6], (D,), 1.0, 4.0)
    ln1_gain = jnp.clip(1.0 + 0.15 * jax.random.normal(key_of[7], (D,), jnp.float32), 0.25, 1.75).astype(jnp.bfloat16)
    ln1_shift = scatter_about(key_of[8], (D,), 0.3, 1.5)
    w_qkv = scatter_about(key_of[9], (D, 3 * D), D ** -0.5, 0.3125)
    bias_q = scatter_about(key_of[10], (D,), 0.3, 1.5)
    bias_v = scatter_about(key_of[11], (D,), 0.05, 0.25)
    w_out = scatter_about(key_of[12], (D, D), 16 ** -0.5, 1.5)
    bias_out = scatter_about(key_of[13], (D,), 0.3, 1.5)
    ln2_gain = jnp.clip(1.0 + 0.15 * jax.random.normal(key_of[14], (D,), jnp.float32), 0.25, 1.75).astype(jnp.bfloat16)
    ln2_shift = scatter_about(key_of[15], (D,), 0.3, 1.5)
    w_up = scatter_about(key_of[16], (D, FF), D ** -0.5, 0.3125)
    bias_up = scatter_about(key_of[17], (FF,), 0.3, 1.5)
    w_down = scatter_about(key_of[18], (FF, D), FF ** -0.5, 0.15625)
    bias_down = scatter_about(key_of[19], (D,), 0.3, 1.5)
    return {"patches": patches, "patch_mask": patch_mask, "clip_lengths": clip_lengths, "target_index": target_index, "targets": targets, "out_grad": out_grad, "mask_embed": mask_embed, "ln1_gain": ln1_gain, "ln1_shift": ln1_shift, "w_qkv": w_qkv, "bias_q": bias_q, "bias_v": bias_v, "w_out": w_out, "bias_out": bias_out, "ln2_gain": ln2_gain, "ln2_shift": ln2_shift, "w_up": w_up, "bias_up": bias_up, "w_down": w_down, "bias_down": bias_down}


@jax.custom_vjp
def low(v):
    return lax.optimization_barrier(v.astype(jnp.bfloat16)).astype(jnp.float32)

@jax.custom_vjp
def low_back(v):
    return v

def low_keep(v):
    return (low(v), None)

def low_pass(kept, grad):
    return (grad,)

def back_keep(v):
    return (v, None)

def back_low(kept, grad):
    return (low(grad),)
low.defvjp(low_keep, low_pass)
low_back.defvjp(back_keep, back_low)
highest = lax.Precision.HIGHEST

def layer_norm(inputs, gain_vec, shift_vec):
    center = inputs - lax.optimization_barrier(jnp.mean(inputs, axis=-1, keepdims=True))
    spread = lax.optimization_barrier(jnp.mean(center * center, axis=-1, keepdims=True))
    return center * lax.rsqrt(spread + 1e-06) * gain_vec + shift_vec

def matmul(left_mat, right_mat):
    return jnp.dot(left_mat, right_mat, precision=highest)

def clip_forward(weights, patch_rows, mask_rows, length):
    mask_embed, ln1_gain, ln1_shift, w_qkv, bias_q, bias_v, w_out, bias_out, ln2_gain, ln2_shift, w_up, bias_up, w_down, bias_down = weights
    token_count = NF * T_LEN
    start = jnp.where(mask_rows[:, :, None] == 1, mask_embed, patch_rows).reshape(token_count, D)
    normed = low(layer_norm(start, ln1_gain, ln1_shift))
    project = matmul(normed, w_qkv)
    queries = low(low_back(project[:, :D] + bias_q)).reshape(token_count, HEADS, HEAD_DIM)
    key_rows = low(low_back(project[:, D:2 * D])).reshape(token_count, HEADS, HEAD_DIM)
    value_rows = low(low_back(project[:, 2 * D:] + bias_v)).reshape(token_count, HEADS, HEAD_DIM)
    usable = jnp.broadcast_to(jnp.arange(T_LEN)[None, :] < length, (NF, T_LEN)).reshape(token_count)
    scores = jnp.einsum('qhd,khd->hqk', queries, key_rows, precision=highest) * HEAD_DIM ** (-0.5)
    scores = low_back(jnp.where(usable[None, None, :], scores, -1000000000.0))
    row_max = lax.optimization_barrier(jnp.max(scores, axis=-1, keepdims=True))
    raised = jnp.exp(scores - row_max)
    attn_prob = raised / lax.optimization_barrier(jnp.sum(raised, axis=-1, keepdims=True))
    mixed = jnp.einsum('hqk,khd->qhd', low(attn_prob), value_rows, precision=highest)
    mixed = low(low_back(mixed)).reshape(token_count, D)
    branch = low_back(matmul(mixed, w_out) + bias_out)
    middle = start + branch
    second = low(layer_norm(middle, ln2_gain, ln2_shift))
    hidden_up = low_back(matmul(second, w_up) + bias_up)
    activated = low(jax.nn.gelu(hidden_up, approximate=False))
    down_rows = low_back(matmul(activated, w_down) + bias_down)
    return (middle + down_rows).reshape(NF, T_LEN, D)

def reference(patches, patch_mask, clip_lengths, target_index, targets, out_grad, mask_embed, ln1_gain, ln1_shift, w_qkv, bias_q, bias_v, w_out, bias_out, ln2_gain, ln2_shift, w_up, bias_up, w_down, bias_down):
    params = (mask_embed.astype(jnp.float32), ln1_gain.astype(jnp.float32), ln1_shift.astype(jnp.float32), w_qkv.astype(jnp.float32), bias_q.astype(jnp.float32), bias_v.astype(jnp.float32), w_out.astype(jnp.float32), bias_out.astype(jnp.float32), ln2_gain.astype(jnp.float32), ln2_shift.astype(jnp.float32), w_up.astype(jnp.float32), bias_up.astype(jnp.float32), w_down.astype(jnp.float32), bias_down.astype(jnp.float32))
    clip_step = jax.checkpoint(clip_forward)

    def forward(inputs, weights):
        return lax.map(lambda element: clip_step(weights, element[0], element[1], element[2]), (inputs, patch_mask, clip_lengths))
    layer_value, pullback = jax.vjp(forward, patches.astype(jnp.float32), params)
    input_grad, weight_grads = pullback(out_grad.astype(jnp.float32))
    grad_mask_embed, grad_ln1_gain, grad_ln1_shift, grad_w_qkv, grad_bias_q, grad_bias_v, grad_w_out, grad_bias_out, grad_ln2_gain, grad_ln2_shift, grad_w_up, grad_bias_up, grad_w_down, grad_bias_down = weight_grads
    block_out = layer_value.astype(jnp.bfloat16)
    logits = jnp.einsum('cftd,cnd->cftn', block_out.astype(jnp.float32), targets.astype(jnp.float32), precision=highest)
    logit_max = lax.optimization_barrier(jnp.max(logits, axis=-1, keepdims=True))
    raised = jnp.exp(logits - logit_max)
    cand_prob = raised / lax.optimization_barrier(jnp.sum(raised, axis=-1, keepdims=True))
    picked = lax.optimization_barrier(jnp.sum(jnp.where(jnp.arange(NCAND) == target_index[..., None], cand_prob, 0.0), axis=-1))
    live_rows = ((patch_mask == 1) & (jnp.arange(T_LEN)[None, None, :] < clip_lengths[:, None, None])).astype(jnp.float32)
    prob_sum = lax.optimization_barrier(jnp.sum(picked * live_rows, axis=(1, 2)))
    counted = lax.optimization_barrier(jnp.sum(live_rows, axis=(1, 2)))
    soft_accuracy = prob_sum / jnp.maximum(counted, 1.0)
    return (block_out, input_grad.astype(jnp.bfloat16), grad_mask_embed, grad_ln1_gain, grad_ln1_shift, grad_w_qkv, grad_bias_q, grad_bias_v, grad_w_out, grad_bias_out, grad_ln2_gain, grad_ln2_shift, grad_w_up, grad_bias_up, grad_w_down, grad_bias_down, soft_accuracy)
```

```python
import functools

import jax
import jax.numpy as jnp
from jax import lax
from jax.experimental import pallas as pl
from jax.experimental.pallas import tpu as pltpu
from jax.sharding import PartitionSpec as P

D = 384
HEADS = 6
HEAD_DIM = 64
PAIRS = HEADS // 2
PAIR = 2 * HEAD_DIM
SCALE = HEAD_DIM ** (-0.5)
DEAD = -1e9
MESH = pl.DeviceIdType.MESH
VMEM_LIMIT = 60 * 2**20


def mm(left_mat, right_mat):
    return jnp.dot(left_mat, right_mat, preferred_element_type=jnp.float32)


def mm_nt(left_mat, right_mat):
    return lax.dot_general(
        left_mat, right_mat, (((1,), (1,)), ((), ())), preferred_element_type=jnp.float32
    )


def mm_tn(left_mat, right_mat):
    return lax.dot_general(
        left_mat, right_mat, (((0,), (0,)), ((), ())), preferred_element_type=jnp.float32
    )


class Plan:
    def __init__(self, mesh, clips):
        self.freq = mesh.shape["freq"]
        self.tm = mesh.shape["tm"]
        self.clips = clips
        self.share = self.freq * self.tm // clips
        self.blocks = self.tm // self.share
        assert self.freq * self.blocks == clips and self.blocks * self.share == self.tm


def exchange_kernel(plan, count, *refs):
    ins, outs = refs[:count], refs[count : 2 * count]
    send_sem, recv_sem, local_sem = refs[2 * count :]
    time_id = lax.axis_index("tm")
    part = time_id % plan.share
    me = lax.axis_index("freq") * plan.blocks + time_id // plan.share

    def device(member):
        return {"freq": member // plan.blocks, "tm": (member % plan.blocks) * plan.share + part}

    barrier = pltpu.get_barrier_semaphore()
    for step in range(1, plan.clips):
        pl.semaphore_signal(
            barrier, inc=1, device_id=device(lax.rem(me + step, plan.clips)), device_id_type=MESH
        )
    pl.semaphore_wait(barrier, plan.clips - 1)
    copies = []
    for i in range(count):
        for step in range(1, plan.clips):
            peer = lax.rem(me + step, plan.clips)
            copy = pltpu.make_async_remote_copy(
                src_ref=ins[i].at[peer],
                dst_ref=outs[i].at[me],
                send_sem=send_sem.at[i, step],
                recv_sem=recv_sem.at[i, step],
                device_id=device(peer),
                device_id_type=MESH,
            )
            copy.start()
            copies.append(copy)
        copy = pltpu.make_async_copy(ins[i].at[me], outs[i].at[me], local_sem.at[i])
        copy.start()
        copies.append(copy)
    for copy in copies:
        copy.wait()


def exchange(plan, collective_id, *arrays):
    count = len(arrays)
    return pl.pallas_call(
        functools.partial(exchange_kernel, plan, count),
        out_shape=[jax.ShapeDtypeStruct(x.shape, x.dtype) for x in arrays],
        in_specs=[pl.BlockSpec(memory_space=pl.ANY)] * count,
        out_specs=[pl.BlockSpec(memory_space=pl.ANY)] * count,
        scratch_shapes=[
            pltpu.SemaphoreType.DMA((count, plan.clips)),
            pltpu.SemaphoreType.DMA((count, plan.clips)),
            pltpu.SemaphoreType.DMA((count,)),
        ],
        compiler_params=pltpu.CompilerParams(collective_id=collective_id, has_side_effects=True),
        name="exchange",
    )(*arrays)


def forward_kernel(q_ref, k_ref, v_ref, bias_ref, mixed_ref, total_ref):
    lane = lax.broadcasted_iota(jnp.int32, (1, PAIR), 1)
    q_pair, k_pair, v_pair, bias = q_ref[...], k_ref[...], v_ref[...], bias_ref[...]
    outs = []
    for e in range(2):
        own = (lane // HEAD_DIM) == e
        scores = mm_nt(jnp.where(own, q_pair, jnp.zeros_like(q_pair)), k_pair) + bias
        row_max = jnp.max(scores, axis=1, keepdims=True)
        raised = jnp.exp(scores - row_max)
        row_total = jnp.sum(raised, axis=1, keepdims=True)
        outs.append(mm(raised.astype(jnp.bfloat16), v_pair) / row_total)
        total_ref[0, e, :] = (row_max + jnp.log(row_total))[:, 0]
    mixed_ref[...] = jnp.where(lane < HEAD_DIM, outs[0], outs[1])


def attend_forward(queries, key_rows, value_rows, bias):
    rows, keys = queries.shape[0], key_rows.shape[0]
    block = min(256, rows)
    return pl.pallas_call(
        forward_kernel,
        grid=(PAIRS, rows // block),
        in_specs=[
            pl.BlockSpec((block, PAIR), lambda p, i: (i, p)),
            pl.BlockSpec((keys, PAIR), lambda p, i: (0, p)),
            pl.BlockSpec((keys, PAIR), lambda p, i: (0, p)),
            pl.BlockSpec((1, keys), lambda p, i: (0, 0)),
        ],
        out_specs=[
            pl.BlockSpec((block, PAIR), lambda p, i: (i, p)),
            pl.BlockSpec((1, 2, block), lambda p, i: (p, 0, i)),
        ],
        out_shape=[
            jax.ShapeDtypeStruct((rows, D), jnp.float32),
            jax.ShapeDtypeStruct((PAIRS, 2, rows), jnp.float32),
        ],
        compiler_params=pltpu.CompilerParams(vmem_limit_bytes=VMEM_LIMIT),
        name="attend_forward",
    )(queries, key_rows, value_rows, bias)


def backward_kernel(
    q_ref, k_ref, kt_ref, v_ref, do_ref, bias_ref, total_ref, center_ref,
    dqt_ref, dk_ref, dv_ref, dqt_sum,
):
    lane = lax.broadcasted_iota(jnp.int32, (1, PAIR), 1)
    step = pl.program_id(1)

    @pl.when(step == 0)
    def _():
        dqt_sum[...] = jnp.zeros_like(dqt_sum)

    q_pair, k_pair, v_pair, do_pair = q_ref[...], k_ref[...], v_ref[...], do_ref[...]
    bias = bias_ref[...]
    grad_k, grad_v = [], []
    for e in range(2):
        own = (lane // HEAD_DIM) == e
        head = slice(e * HEAD_DIM, (e + 1) * HEAD_DIM)
        q_own = jnp.where(own, q_pair, jnp.zeros_like(q_pair))
        do_own = jnp.where(own, do_pair, jnp.zeros_like(do_pair))
        prob = jnp.exp(mm_nt(k_pair, q_own) + bias - total_ref[0, e : e + 1, :])
        grad_prob = mm_nt(v_pair, do_own)
        grad_scores = (prob * (grad_prob - center_ref[0, e : e + 1, :])).astype(jnp.bfloat16)
        grad_v.append(mm(prob.astype(jnp.bfloat16), do_own))
        grad_k.append(mm(grad_scores, q_own))
        dqt_sum[head, :] += mm(kt_ref[head, :], grad_scores)
    dk_ref[...] = (grad_k[0] + grad_k[1]).astype(dk_ref.dtype)
    dv_ref[...] = (grad_v[0] + grad_v[1]).astype(dv_ref.dtype)

    @pl.when(step == pl.num_programs(1) - 1)
    def _():
        dqt_ref[...] = (dqt_sum[...] * SCALE).astype(dqt_ref.dtype)


def attend_backward(queries, key_rows, value_rows, grad_mixed, bias, total, center):
    rows, keys = queries.shape[0], key_rows.shape[0]
    block = min(512, keys)
    return pl.pallas_call(
        backward_kernel,
        grid=(PAIRS, keys // block),
        in_specs=[
            pl.BlockSpec((rows, PAIR), lambda p, i: (0, p)),
            pl.BlockSpec((block, PAIR), lambda p, i: (i, p)),
            pl.BlockSpec((PAIR, block), lambda p, i: (p, i)),
            pl.BlockSpec((block, PAIR), lambda p, i: (i, p)),
            pl.BlockSpec((rows, PAIR), lambda p, i: (0, p)),
            pl.BlockSpec((block, 1), lambda p, i: (i, 0)),
            pl.BlockSpec((1, 2, rows), lambda p, i: (p, 0, 0)),
            pl.BlockSpec((1, 2, rows), lambda p, i: (p, 0, 0)),
        ],
        out_specs=[
            pl.BlockSpec((PAIR, rows), lambda p, i: (p, 0)),
            pl.BlockSpec((block, PAIR), lambda p, i: (i, p)),
            pl.BlockSpec((block, PAIR), lambda p, i: (i, p)),
        ],
        out_shape=[
            jax.ShapeDtypeStruct((D, rows), jnp.bfloat16),
            jax.ShapeDtypeStruct((keys, D), jnp.bfloat16),
            jax.ShapeDtypeStruct((keys, D), jnp.bfloat16),
        ],
        scratch_shapes=[pltpu.VMEM((PAIR, rows), jnp.float32)],
        compiler_params=pltpu.CompilerParams(vmem_limit_bytes=VMEM_LIMIT),
        name="attend_backward",
    )(queries, key_rows, key_rows.T, value_rows, grad_mixed, bias, total, center)


def layer_norm(inputs, gain_vec, shift_vec):
    center = inputs - jnp.mean(inputs, axis=-1, keepdims=True)
    spread = jnp.mean(center * center, axis=-1, keepdims=True)
    return center * lax.rsqrt(spread + 1e-06) * gain_vec + shift_vec


def gelu_exact(inputs):
    return jax.nn.gelu(inputs, approximate=False)


def per_device(
    plan, batches,
    patches, patch_mask, clip_lengths, target_index, targets, out_grad,
    mask_embed, ln1_gain, ln1_shift, w_qkv, bias_q, bias_v, w_out, bias_out,
    ln2_gain, ln2_shift, w_up, bias_up, w_down, bias_down,
):
    f32 = jnp.float32
    clips, freq_rows, time_rows, width = patches.shape
    block_rows = freq_rows * time_rows
    tokens = clips * block_rows
    time_id = lax.axis_index("tm")
    part = time_id % plan.share
    clip = lax.axis_index("freq") * plan.blocks + time_id // plan.share
    length = lax.dynamic_index_in_dim(clip_lengths, clip, keepdims=False)
    groups = [
        [block * plan.share + j for j in range(plan.share)] for block in range(plan.blocks)
    ]

    masked_patches = jnp.where((patch_mask == 1)[..., None], mask_embed, patches)
    code = (target_index * 2 + patch_mask).reshape(clips, 1, block_rows)
    start_low, grad_low, code = exchange(plan, 0, masked_patches, out_grad, code)
    start = start_low.reshape(tokens, width).astype(f32)
    grad_down = grad_low.reshape(tokens, width)
    code = code.reshape(tokens)
    flat_mask = (code % 2 == 1)[:, None]
    target = code // 2

    def live(owner):
        shape = (clips, freq_rows, time_rows)
        blocks = lax.broadcasted_iota(jnp.int32, shape, 0) % plan.blocks
        step = lax.broadcasted_iota(jnp.int32, shape, 2)
        return (((blocks * plan.share + owner) * time_rows + step) < length).reshape(tokens)

    normed, first_back = jax.vjp(layer_norm, start, ln1_gain.astype(f32), ln1_shift.astype(f32))
    normed_low = normed.astype(jnp.bfloat16)
    project = mm(normed_low, w_qkv)
    queries = (project[:, :D] + bias_q.astype(f32)).astype(jnp.bfloat16)
    queries = (queries.astype(f32) * SCALE).astype(jnp.bfloat16)
    local_kv = jnp.concatenate(
        [project[:, D : 2 * D], project[:, 2 * D :] + bias_v.astype(f32)], axis=-1
    ).astype(jnp.bfloat16)
    full_kv = lax.all_gather(local_kv, "tm", axis=0, tiled=True, axis_index_groups=groups)
    key_rows, value_rows = full_kv[:, :D], full_kv[:, D:]
    usable = jnp.concatenate([live(j) for j in range(plan.share)])
    bias = jnp.where(usable, 0.0, DEAD).astype(f32)

    mixed_f, total = attend_forward(queries, key_rows, value_rows, bias[None, :])
    mixed = mixed_f.astype(jnp.bfloat16)
    middle = start + mm(mixed, w_out) + bias_out.astype(f32)
    second, second_back = jax.vjp(layer_norm, middle, ln2_gain.astype(f32), ln2_shift.astype(f32))
    second_low = second.astype(jnp.bfloat16)
    hidden_up = mm(second_low, w_up) + bias_up.astype(f32)
    activated_f, gelu_back = jax.vjp(gelu_exact, hidden_up)
    activated = activated_f.astype(jnp.bfloat16)
    result = middle + mm(activated, w_down) + bias_down.astype(f32)
    block_out = result.astype(jnp.bfloat16)
    grad_w_down = mm_tn(activated, grad_down)
    grad_bias_down = jnp.sum(grad_down.astype(f32), axis=0)
    grad_up = gelu_back(mm_nt(grad_down, w_down))[0].astype(jnp.bfloat16)
    grad_w_up = mm_tn(second_low, grad_up)
    grad_bias_up = jnp.sum(grad_up.astype(f32), axis=0)
    grad_middle_norm, grad_ln2_gain, grad_ln2_shift = second_back(mm_nt(grad_up, w_up))
    grad_middle = grad_down.astype(f32) + grad_middle_norm
    grad_branch = grad_middle.astype(jnp.bfloat16)
    grad_w_out = mm_tn(mixed, grad_branch)
    grad_bias_out = jnp.sum(grad_branch.astype(f32), axis=0)
    grad_mixed = mm_nt(grad_branch, w_out).astype(jnp.bfloat16)

    center = jnp.sum(
        (grad_mixed.astype(f32) * mixed_f).reshape(tokens, HEADS, HEAD_DIM), axis=-1
    ).T.reshape(PAIRS, 2, tokens)
    grad_q_t, grad_k, grad_v = attend_backward(
        queries, key_rows, value_rows, grad_mixed, bias[:, None], total, center
    )
    grad_kv = lax.psum_scatter(
        jnp.concatenate([grad_k, grad_v], axis=-1), "tm", scatter_dimension=0, tiled=True,
        axis_index_groups=groups,
    )
    grad_project = jnp.concatenate([grad_q_t.T, grad_kv], axis=-1)
    grad_w_qkv = mm_tn(normed_low, grad_project)
    grad_bias_q = jnp.sum(grad_project[:, :D].astype(f32), axis=0)
    grad_bias_v = jnp.sum(grad_project[:, 2 * D :].astype(f32), axis=0)
    grad_start_norm, grad_ln1_gain, grad_ln1_shift = first_back(mm_nt(grad_project, w_qkv))
    grad_start = grad_middle + grad_start_norm
    grad_mask_embed = jnp.sum(jnp.where(flat_mask, grad_start, 0.0), axis=0)
    input_grad = jnp.where(flat_mask, 0.0, grad_start).astype(jnp.bfloat16)

    own_targets = lax.dynamic_index_in_dim(targets, clip, keepdims=False)
    logits = mm_nt(block_out, own_targets)
    raised = jnp.exp(logits - jnp.max(logits, axis=-1, keepdims=True))
    cand_ids = lax.broadcasted_iota(jnp.int32, raised.shape, 1)
    hit = jnp.sum(jnp.where(cand_ids == target[:, None], raised, 0.0), axis=-1)
    picked = hit / jnp.sum(raised, axis=-1)
    counts = ((code % 2 == 1) & live(part)).astype(f32)
    slot = (jnp.arange(clips) == clip).astype(f32)
    score = jnp.concatenate([slot * jnp.sum(picked * counts), slot * jnp.sum(counts)])

    block_grid, input_grid = exchange(
        plan, 1, block_out.reshape(patches.shape), input_grad.reshape(patches.shape)
    )
    everywhere = ("freq", "tm", "batch")
    grad_w_out, grad_w_up, grad_w_down, grad_w_qkv = [
        g.astype(f32)
        for g in lax.psum(
            tuple(g.astype(jnp.bfloat16) for g in (grad_w_out, grad_w_up, grad_w_down, grad_w_qkv)),
            everywhere,
        )
    ]
    vectors = (
        grad_mask_embed, grad_ln1_gain, grad_ln1_shift, grad_bias_q, grad_bias_v, grad_bias_out,
        grad_ln2_gain, grad_ln2_shift, grad_bias_up, grad_bias_down,
    )
    batch_slot = (jnp.arange(batches) == lax.axis_index("batch")).astype(f32)
    packed = jnp.concatenate(vectors + ((batch_slot[:, None] * score[None, :]).reshape(-1),))
    packed = lax.psum(packed, everywhere)
    pieces, at = [], 0
    for vector in vectors:
        pieces.append(packed[at : at + vector.shape[0]])
        at += vector.shape[0]
    scores = lax.dynamic_index_in_dim(
        packed[at:].reshape(batches, 2, clips), lax.axis_index("batch"), keepdims=False
    )
    soft_accuracy = scores[0] / jnp.maximum(scores[1], 1.0)
    (grad_mask_embed, grad_ln1_gain, grad_ln1_shift, grad_bias_q, grad_bias_v, grad_bias_out,
     grad_ln2_gain, grad_ln2_shift, grad_bias_up, grad_bias_down) = pieces
    return (
        block_grid, input_grid, grad_mask_embed, grad_ln1_gain, grad_ln1_shift, grad_w_qkv,
        grad_bias_q, grad_bias_v, grad_w_out, grad_bias_out, grad_ln2_gain, grad_ln2_shift,
        grad_w_up, grad_bias_up, grad_w_down, grad_bias_down, soft_accuracy,
    )


def solution(mesh):
    rows = P("batch", "freq", "tm", None)
    whole = P()
    in_specs = (
        rows, P("batch", "freq", "tm"), P("batch"), P("batch", "freq", "tm"),
        P("batch", None, None), rows,
    ) + (whole,) * 14
    out_specs = (rows, rows) + (whole,) * 14 + (P("batch"),)

    def body(*args):
        plan = Plan(mesh, args[0].shape[0])
        return per_device(plan, mesh.shape["batch"], *args)

    return jax.shard_map(
        body, mesh=mesh, in_specs=in_specs, out_specs=out_specs, check_vma=False
    )
```

```python
import functools

import jax
import jax.numpy as jnp
from jax import lax
from jax.experimental import pallas as pl
from jax.experimental.pallas import tpu as pltpu
from jax.sharding import PartitionSpec as P

D = 384
FF = 1536
HEADS = 6
HEAD_DIM = 64
PAIRS = HEADS // 2
PAIR = 2 * HEAD_DIM
SCALE = HEAD_DIM ** (-0.5)
DEAD = -1e9
EPS = 1e-06
VEC_ROWS = 16
MESH = pl.DeviceIdType.MESH
VMEM_LIMIT = 60 * 2**20
ANY = pl.BlockSpec(memory_space=pl.ANY)
VMEM = pl.BlockSpec(memory_space=pltpu.VMEM)
BF16 = jnp.bfloat16
F32 = jnp.float32


def mm(left_mat, right_mat):
    return jnp.dot(left_mat, right_mat, preferred_element_type=F32)


def mm_nt(left_mat, right_mat):
    return lax.dot_general(
        left_mat, right_mat, (((1,), (1,)), ((), ())), preferred_element_type=F32
    )


def mm_tn(left_mat, right_mat):
    return lax.dot_general(
        left_mat, right_mat, (((0,), (0,)), ((), ())), preferred_element_type=F32
    )


def row(ref):
    return ref[...].astype(F32).reshape(1, -1)


def normalize(rows):
    center = rows - jnp.mean(rows, axis=-1, keepdims=True)
    scale = lax.rsqrt(jnp.mean(center * center, axis=-1, keepdims=True) + EPS)
    return center * scale, scale


def normalize_back(grad_hat, hat, scale):
    first = jnp.mean(grad_hat, axis=-1, keepdims=True)
    second = jnp.mean(grad_hat * hat, axis=-1, keepdims=True)
    return scale * (grad_hat - first - hat * second)


def sum_rows(rows):
    return jnp.sum(rows, axis=0, keepdims=True)


def columns(ints):
    freq_rows, time_rows = ints.shape
    shape = (time_rows, time_rows)
    eye = lax.broadcasted_iota(jnp.int32, shape, 0) == lax.broadcasted_iota(jnp.int32, shape, 1)
    parts = [
        jnp.sum(jnp.where(eye, ints[f : f + 1, :], 0), axis=1, keepdims=True)
        for f in range(freq_rows)
    ]
    return jnp.concatenate(parts, axis=0)


class Plan:
    def __init__(self, mesh, patches):
        self.freq = mesh.shape["freq"]
        self.tm = mesh.shape["tm"]
        self.batch = mesh.shape["batch"]
        self.clips, self.freq_rows, self.time_rows, _ = patches.shape
        self.share = self.freq * self.tm // self.clips
        self.blocks = self.tm // self.share
        self.block_rows = self.freq_rows * self.time_rows
        self.rows = self.clips * self.block_rows
        self.keys = self.share * self.rows
        assert self.freq * self.blocks == self.clips and self.blocks * self.share == self.tm

    def place(self):
        time_id = lax.axis_index("tm")
        return lax.axis_index("freq") * self.blocks + time_id // self.share, time_id % self.share

    def member(self, member, part):
        return {
            "freq": member // self.blocks,
            "tm": (member % self.blocks) * self.share + part,
        }

    def sharer(self, part):
        time_id = lax.axis_index("tm")
        return {"tm": time_id // self.share * self.share + part}

    def key_time(self, place):
        part = place // self.rows
        block = (place // self.block_rows) % self.clips % self.blocks
        return (block * self.share + part) * self.time_rows + place % self.time_rows


def greet(devices):
    barrier = pltpu.get_barrier_semaphore()
    for device in devices:
        pl.semaphore_signal(barrier, inc=1, device_id=device, device_id_type=MESH)
    pl.semaphore_wait(barrier, len(devices))


def remote(src, dst, send_sem, recv_sem, device):
    return pltpu.make_async_remote_copy(
        src_ref=src, dst_ref=dst, send_sem=send_sem, recv_sem=recv_sem,
        device_id=device, device_id_type=MESH,
    )


def project_kernel(
    plan, patches, mask, target, embed, gain, shift, w_ref, bias_q, bias_v,
    start_out, q_out, kv_out, mask_out, target_out,
    taken, mask_in, target_in, start_buf, q_buf, kv_buf,
    send_sem, recv_sem, local_sem, kv_send, kv_recv, out_sem,
):
    me, part = plan.place()
    n = plan.clips
    peers = [lax.rem(me + step, n) for step in range(n)]
    sharers = [lax.rem(part + step, plan.share) for step in range(plan.share)]
    greet(
        [plan.member(peers[step], part) for step in range(1, n)]
        + [plan.sharer(sharers[step]) for step in range(1, plan.share)]
    )
    streams = ((mask, mask_in), (target, target_in), (patches, taken))
    arrivals = []
    for step in range(n):
        copies = []
        for i, (src, dst) in enumerate(streams):
            if step == 0:
                copy = pltpu.make_async_copy(src.at[me], dst.at[me], local_sem.at[i])
            else:
                copy = remote(
                    src.at[peers[step]], dst.at[me], send_sem.at[i, step], recv_sem.at[i, step],
                    plan.member(peers[step], part),
                )
            copy.start()
            copies.append(copy)
        arrivals.append(copies)
    gain_row, shift_row, embed_row = row(gain), row(shift), row(embed)
    bias_q_row, bias_v_row = row(bias_q), row(bias_v)
    waits = []
    for step in range(n):
        source = lax.rem(me + n - step, n)
        for copy in arrivals[step]:
            if step == 0:
                copy.wait()
            else:
                copy.wait_recv()
        masked = columns(mask_in[source]) == 1
        rows = taken[source].astype(F32)
        start = jnp.where(masked, embed_row, rows)
        start_buf[source] = start.astype(BF16)
        hat, _ = normalize(start)
        normed = (hat * gain_row + shift_row).astype(BF16)
        project = mm(normed, w_ref[...])
        queries = (project[:, :D] + bias_q_row).astype(BF16)
        q_buf[source] = (queries.astype(F32) * SCALE).astype(BF16)
        kv_buf[source, :, :D] = project[:, D : 2 * D].astype(BF16)
        kv_buf[source, :, D:] = (project[:, 2 * D :] + bias_v_row).astype(BF16)
        for other in range(1, plan.share):
            copy = remote(
                kv_buf.at[source], kv_out.at[part, source], kv_send.at[other, step],
                kv_recv.at[other, step], plan.sharer(sharers[other]),
            )
            copy.start()
            waits.append(copy)
        for i, (src, dst) in enumerate(
            (
                (kv_buf.at[source], kv_out.at[part, source]),
                (q_buf.at[source], q_out.at[source]),
                (start_buf.at[source], start_out.at[source]),
            )
        ):
            copy = pltpu.make_async_copy(src, dst, out_sem.at[i, step])
            copy.start()
            waits.append(copy)
    for i, (src, dst) in enumerate(((mask_in, mask_out), (target_in, target_out))):
        copy = pltpu.make_async_copy(src, dst, local_sem.at[i])
        copy.start()
        waits.append(copy)
    for step in range(1, n):
        for copy in arrivals[step]:
            copy.wait_send()
    for copy in waits:
        copy.wait()


def project_rows(plan, patches, mask, target, embed, gain, shift, w_qkv, bias_q, bias_v):
    n, rows = plan.clips, plan.block_rows
    ints = jax.ShapeDtypeStruct(mask.shape, jnp.int32)
    dma = pltpu.SemaphoreType.DMA
    return pl.pallas_call(
        functools.partial(project_kernel, plan),
        out_shape=[
            jax.ShapeDtypeStruct((n, rows, D), BF16),
            jax.ShapeDtypeStruct((n, rows, D), BF16),
            jax.ShapeDtypeStruct((plan.share, n, rows, 2 * D), BF16),
            ints,
            ints,
        ],
        in_specs=[ANY] * 3 + [VMEM] * 6,
        out_specs=[ANY] * 5,
        scratch_shapes=[
            pltpu.VMEM(patches.shape, BF16),
            pltpu.VMEM(mask.shape, jnp.int32),
            pltpu.VMEM(mask.shape, jnp.int32),
            pltpu.VMEM((n, rows, D), BF16),
            pltpu.VMEM((n, rows, D), BF16),
            pltpu.VMEM((n, rows, 2 * D), BF16),
            dma((3, n)), dma((3, n)), dma((3,)),
            dma((plan.share, n)), dma((plan.share, n)), dma((3, n)),
        ],
        compiler_params=pltpu.CompilerParams(
            collective_id=0, has_side_effects=True, vmem_limit_bytes=VMEM_LIMIT
        ),
        name="project_rows",
    )(patches, mask, target, embed, gain, shift, w_qkv, bias_q, bias_v)


def forward_kernel(plan, place, q_ref, k_ref, v_ref, mixed_ref, total_ref):
    lane = lax.broadcasted_iota(jnp.int32, (1, PAIR), 1)
    q_pair, k_pair, v_pair = q_ref[...], k_ref[...], v_ref[...]
    key_id = lax.broadcasted_iota(jnp.int32, (1, plan.keys), 1)
    bias = jnp.where(plan.key_time(key_id) < place[1], 0.0, DEAD)
    outs = []
    for e in range(2):
        own = (lane // HEAD_DIM) == e
        scores = mm_nt(jnp.where(own, q_pair, jnp.zeros_like(q_pair)), k_pair) + bias
        row_max = jnp.max(scores, axis=1, keepdims=True)
        raised = jnp.exp(scores - row_max)
        row_total = jnp.sum(raised, axis=1, keepdims=True)
        outs.append(mm(raised.astype(BF16), v_pair) / row_total)
        total_ref[0, e, :] = (row_max + jnp.log(row_total))[:, 0]
    mixed_ref[...] = jnp.where(lane < HEAD_DIM, outs[0], outs[1])


def attend_forward(plan, place, queries, kv):
    rows, keys = plan.rows, plan.keys
    block = min(256, rows)
    return pl.pallas_call(
        functools.partial(forward_kernel, plan),
        grid_spec=pltpu.PrefetchScalarGridSpec(
            num_scalar_prefetch=1,
            grid=(PAIRS, rows // block),
            in_specs=[
                pl.BlockSpec((block, PAIR), lambda p, i, s: (i, p)),
                pl.BlockSpec((keys, PAIR), lambda p, i, s: (0, p)),
                pl.BlockSpec((keys, PAIR), lambda p, i, s: (0, PAIRS + p)),
            ],
            out_specs=[
                pl.BlockSpec((block, PAIR), lambda p, i, s: (i, p)),
                pl.BlockSpec((1, 2, block), lambda p, i, s: (p, 0, i)),
            ],
        ),
        out_shape=[
            jax.ShapeDtypeStruct((rows, D), F32),
            jax.ShapeDtypeStruct((PAIRS, 2, rows), F32),
        ],
        compiler_params=pltpu.CompilerParams(vmem_limit_bytes=VMEM_LIMIT),
        cost_estimate=pl.CostEstimate(
            flops=4 * rows * keys * D, bytes_accessed=8 * rows * D, transcendentals=rows * keys
        ),
        name="attend_forward",
    )(place, queries, kv, kv)


def gelu_parts(rows):
    lower = 0.5 * (1.0 + lax.erf(rows * 0.7071067811865476))
    slope = lower + rows * (jnp.exp(-0.5 * rows * rows) * 0.3989422804014327)
    return rows * lower, slope


def feed_kernel(
    plan, place, mixed, start, grad, mask, target, targets, w_out, bias_out, gain, shift,
    w_up, bias_up, w_down, bias_down,
    block_out, grad_middle, grad_mixed, center, grad_w_up, grad_w_down, grad_w_out, vec,
    middle, second, down_sum, second_sum, act_buf, up_buf,
):
    step = pl.program_id(0)
    steps = pl.num_programs(0)
    rows = plan.rows
    tile = min(256, rows)
    tiles = [slice(i * tile, (i + 1) * tile) for i in range(rows // tile)]
    gain_row, shift_row = row(gain), row(shift)

    @pl.when(step == 0)
    def _():
        vec[...] = jnp.zeros_like(vec)
        for part in tiles:
            rows_in = start[part, :].astype(F32) + mm(mixed[part, :].astype(BF16), w_out[...])
            rows_in = rows_in + row(bias_out)
            middle[part, :] = rows_in
            hat, _ = normalize(rows_in)
            second[part, :] = (hat * gain_row + shift_row).astype(BF16)
        down_sum[...] = jnp.zeros_like(down_sum)
        second_sum[...] = jnp.zeros_like(second_sum)

    bias_row = row(bias_up.at[0])
    for part in tiles:
        hidden = mm(second[part, :], w_up[...]) + bias_row
        active, slope = gelu_parts(hidden)
        active = active.astype(BF16)
        act_buf[part, :] = active
        down_sum[part, :] += mm(active, w_down[...])
        grad_up = (mm_nt(grad[part, :], w_down[...]) * slope).astype(BF16)
        up_buf[part, :] = grad_up
        second_sum[part, :] += mm_nt(grad_up, w_up[...])
    grad_w_down[...] = mm_tn(act_buf[...], grad[...])
    grad_w_up[...] = mm_tn(second[...], up_buf[...])
    vec[pl.ds(9 + step, 1), :] = sum_rows(up_buf[...].astype(F32))

    @pl.when(step == steps - 1)
    def _():
        clip, length, batch = place[0], place[1], place[2]
        head_of = lax.broadcasted_iota(jnp.int32, (8, D), 1) // HEAD_DIM
        picks = (head_of == lax.broadcasted_iota(jnp.int32, (8, D), 0)).astype(BF16)
        cand = lax.broadcasted_iota(jnp.int32, (1, targets.shape[1]), 1)
        vec[8:9, :] = sum_rows(grad[...].astype(F32))
        total_hit = jnp.zeros((1, 1), F32)
        total_count = jnp.zeros((1, 1), F32)
        per_tile = tile // plan.block_rows
        for t, part in enumerate(tiles):
            result = middle[part, :] + down_sum[part, :] + row(bias_down)
            result = result.astype(BF16)
            block_out[part, :] = result
            hat, scale = normalize(middle[part, :])
            grad_second = second_sum[part, :]
            vec[6:7, :] += sum_rows(grad_second * hat)
            vec[7:8, :] += sum_rows(grad_second)
            back = normalize_back(grad_second * gain_row, hat, scale)
            back = grad[part, :].astype(F32) + back
            grad_middle[part, :] = back
            branch = back.astype(BF16)
            act_buf[part, :] = branch
            vec[5:6, :] += sum_rows(branch.astype(F32))
            down = mm_nt(branch, w_out[...]).astype(BF16)
            grad_mixed[part, :] = down
            product = down.astype(F32) * mixed[part, :]
            high = product.astype(BF16)
            low = (product - high.astype(F32)).astype(BF16)
            center[:, part] = mm_nt(picks, high) + mm_nt(picks, low)
            logits = mm_nt(result, targets[0])
            raised = jnp.exp(logits - jnp.max(logits, axis=1, keepdims=True))
            sources = range(t * per_tile, (t + 1) * per_tile)
            target_col = jnp.concatenate([columns(target[s]) for s in sources], axis=0)
            mask_col = jnp.concatenate([columns(mask[s]) for s in sources], axis=0)
            hit = jnp.sum(jnp.where(cand == target_col, raised, 0.0), axis=1, keepdims=True)
            hit = hit / jnp.sum(raised, axis=1, keepdims=True)
            ids = lax.broadcasted_iota(jnp.int32, (tile, 1), 0) + t * tile + place[3] * rows
            counted = jnp.where((plan.key_time(ids) < length) & (mask_col == 1), 1.0, 0.0)
            total_hit += jnp.sum(hit * counted, axis=0, keepdims=True)
            total_count += jnp.sum(counted, axis=0, keepdims=True)
        grad_w_out[...] = mm_tn(mixed[...].astype(BF16), act_buf[...])
        lane = lax.broadcasted_iota(jnp.int32, (1, D), 1)
        slot = batch * 2 * plan.clips + clip
        scores = jnp.where(lane == slot, total_hit, 0.0)
        vec[13:14, :] = scores + jnp.where(lane == slot + plan.clips, total_count, 0.0)


def feed_forward(
    plan, place, mixed, start, grad, mask, target, targets, w_out, bias_out, gain, shift,
    w_up, bias_up, w_down, bias_down,
):
    rows = plan.rows
    steps = FF // D

    def full(shape):
        return pl.BlockSpec(shape, lambda i, s: (0,) * len(shape))

    return pl.pallas_call(
        functools.partial(feed_kernel, plan),
        grid_spec=pltpu.PrefetchScalarGridSpec(
            num_scalar_prefetch=1,
            grid=(steps,),
            in_specs=[
                full((rows, D)), full((rows, D)), full((rows, D)),
                full(mask.shape), full(mask.shape),
                pl.BlockSpec((1,) + targets.shape[1:], lambda i, s: (s[0], 0, 0)),
                full((D, D)), full((D,)), full((D,)), full((D,)),
                pl.BlockSpec((D, D), lambda i, s: (0, i)),
                pl.BlockSpec((1, 1, D), lambda i, s: (i, 0, 0)),
                pl.BlockSpec((D, D), lambda i, s: (i, 0)),
                full((D,)),
            ],
            out_specs=[
                full((rows, D)), full((rows, D)), full((rows, D)), full((8, rows)),
                pl.BlockSpec((D, D), lambda i, s: (0, i)),
                pl.BlockSpec((D, D), lambda i, s: (i, 0)),
                full((D, D)), full((VEC_ROWS, D)),
            ],
            scratch_shapes=[
                pltpu.VMEM((rows, D), F32), pltpu.VMEM((rows, D), BF16),
                pltpu.VMEM((rows, D), F32), pltpu.VMEM((rows, D), F32),
                pltpu.VMEM((rows, D), BF16), pltpu.VMEM((rows, D), BF16),
            ],
        ),
        out_shape=[
            jax.ShapeDtypeStruct((rows, D), BF16),
            jax.ShapeDtypeStruct((rows, D), F32),
            jax.ShapeDtypeStruct((rows, D), BF16),
            jax.ShapeDtypeStruct((8, rows), F32),
            jax.ShapeDtypeStruct((D, FF), F32),
            jax.ShapeDtypeStruct((FF, D), F32),
            jax.ShapeDtypeStruct((D, D), F32),
            jax.ShapeDtypeStruct((VEC_ROWS, D), F32),
        ],
        compiler_params=pltpu.CompilerParams(vmem_limit_bytes=VMEM_LIMIT),
        cost_estimate=pl.CostEstimate(
            flops=12 * rows * FF * D, bytes_accessed=20 * rows * D, transcendentals=2 * rows * FF
        ),
        name="feed_forward",
    )(
        place, mixed, start, grad, mask, target, targets, w_out, bias_out, gain, shift,
        w_up, bias_up.reshape(steps, 1, D), w_down, bias_down,
    )


def backward_kernel(
    plan, block, place, q_ref, k_ref, v_ref, do_ref, total_ref, center_ref,
    dq_ref, dk_ref, dv_ref, dqt_sum,
):
    lane = lax.broadcasted_iota(jnp.int32, (1, PAIR), 1)
    pair, step = pl.program_id(0), pl.program_id(1)

    @pl.when(step == 0)
    def _():
        dqt_sum[...] = jnp.zeros_like(dqt_sum)

    q_pair, k_pair, v_pair, do_pair = q_ref[...], k_ref[...], v_ref[...], do_ref[...]
    k_turned = k_pair.T
    key_id = lax.broadcasted_iota(jnp.int32, (block, 1), 0) + step * block
    bias = jnp.where(plan.key_time(key_id) < place[1], 0.0, DEAD)
    grad_k, grad_v = [], []
    for e in range(2):
        own = (lane // HEAD_DIM) == e
        head = slice(e * HEAD_DIM, (e + 1) * HEAD_DIM)
        q_own = jnp.where(own, q_pair, jnp.zeros_like(q_pair))
        do_own = jnp.where(own, do_pair, jnp.zeros_like(do_pair))
        prob = jnp.exp(mm_nt(k_pair, q_own) + bias - total_ref[0, e : e + 1, :])
        grad_prob = mm_nt(v_pair, do_own)
        center = center_ref[pl.ds(2 * pair + e, 1), :]
        grad_scores = (prob * (grad_prob - center)).astype(BF16)
        grad_v.append(mm(prob.astype(BF16), do_own))
        grad_k.append(mm(grad_scores, q_own))
        dqt_sum[head, :] += mm(k_turned[head, :], grad_scores)
    dk_ref[...] = (grad_k[0] + grad_k[1]).astype(dk_ref.dtype)
    dv_ref[...] = (grad_v[0] + grad_v[1]).astype(dv_ref.dtype)

    @pl.when(step == pl.num_programs(1) - 1)
    def _():
        dq_ref[...] = (dqt_sum[...] * SCALE).T.astype(dq_ref.dtype)


def attend_backward(plan, place, queries, kv, grad_mixed, total, center):
    rows, keys = plan.rows, plan.keys
    block = min(512, keys)
    return pl.pallas_call(
        functools.partial(backward_kernel, plan, block),
        grid_spec=pltpu.PrefetchScalarGridSpec(
            num_scalar_prefetch=1,
            grid=(PAIRS, keys // block),
            in_specs=[
                pl.BlockSpec((rows, PAIR), lambda p, i, s: (0, p)),
                pl.BlockSpec((block, PAIR), lambda p, i, s: (i, p)),
                pl.BlockSpec((block, PAIR), lambda p, i, s: (i, PAIRS + p)),
                pl.BlockSpec((rows, PAIR), lambda p, i, s: (0, p)),
                pl.BlockSpec((1, 2, rows), lambda p, i, s: (p, 0, 0)),
                pl.BlockSpec((8, rows), lambda p, i, s: (0, 0)),
            ],
            out_specs=[
                pl.BlockSpec((rows, PAIR), lambda p, i, s: (0, p)),
                pl.BlockSpec((block, PAIR), lambda p, i, s: (i, p)),
                pl.BlockSpec((block, PAIR), lambda p, i, s: (i, p)),
            ],
            scratch_shapes=[pltpu.VMEM((PAIR, rows), F32)],
        ),
        out_shape=[
            jax.ShapeDtypeStruct((rows, D), BF16),
            jax.ShapeDtypeStruct((keys, D), BF16),
            jax.ShapeDtypeStruct((keys, D), BF16),
        ],
        compiler_params=pltpu.CompilerParams(vmem_limit_bytes=VMEM_LIMIT),
        cost_estimate=pl.CostEstimate(
            flops=10 * rows * keys * D, bytes_accessed=10 * rows * D, transcendentals=rows * keys
        ),
        name="attend_backward",
    )(place, queries, kv, kv, grad_mixed, total, center)


def finish_kernel(
    plan, cut, dq, start, grad_middle, mask, dk_all, dv_all, w_ref, gain, shift, dw_out, vec,
    input_grad, reduced, vec_out,
    dk_buf, dv_buf, hat_buf, grad_buf, weight, away, core_in, plane_send, plane_in,
    depth_send, depth_in, total, rows_buf, vec_buf, vec_core, vec_plane, vec_depth,
    kv_send, kv_recv, kv_local, rows_ss, rows_rs, rows_local, core_sem, plane_ss, plane_rs,
    depth_ss, depth_rs, up_ss, up_rs, wide_ss, wide_rs, last_sem, vec_core_sem,
    vec_plane_ss, vec_plane_rs, vec_depth_ss, vec_depth_rs, out_sem,
):
    n, rows, block_rows = plan.clips, plan.rows, plan.block_rows
    half, chunk, piece = cut.half, cut.chunk, cut.piece
    me, part = plan.place()
    time_id = lax.axis_index("tm")
    core, depth = time_id % 2, time_id // 2
    n_plane, n_depth = cut.n_plane, cut.n_depth
    plane = lax.axis_index("freq") * plan.batch + lax.axis_index("batch")
    partner = {"tm": time_id + 1 - 2 * core}
    peers = [lax.rem(me + k, n) for k in range(n)]
    sharers = [lax.rem(part + k, plan.share) for k in range(plan.share)]
    planes = [lax.rem(plane + k, n_plane) for k in range(n_plane)]
    depths = [lax.rem(depth + k, n_depth) for k in range(n_depth)]
    in_plane = [{"freq": v // plan.batch, "batch": v % plan.batch} for v in planes]
    in_depth = [{"tm": v * 2 + core} for v in depths]

    def spot(first, count):
        return pl.ds(pl.multiple_of(first, 16), count)

    greet(
        [plan.member(peers[k], part) for k in range(1, n)]
        + [plan.sharer(sharers[k]) for k in range(1, plan.share)]
        + [partner]
        + in_plane[1:]
        + in_depth[1:]
    )
    kv_copies = []
    for i, (src, dst) in enumerate(((dk_all, dk_buf), (dv_all, dv_buf))):
        for k in range(1, plan.share):
            copy = remote(
                src.at[sharers[k]], dst.at[k], kv_send.at[i, k], kv_recv.at[i, k],
                plan.sharer(sharers[k]),
            )
            copy.start()
            kv_copies.append(copy)
        copy = pltpu.make_async_copy(src.at[part], dst.at[0], kv_local.at[i])
        copy.start()
        kv_copies.append(copy)

    gain_row, shift_row = row(gain), row(shift)
    tile = min(256, rows)
    normed = []
    for i in range(rows // tile):
        span = slice(i * tile, (i + 1) * tile)
        hat, _ = normalize(start[span, :].astype(F32))
        hat_buf[span, :] = hat
        normed.append((hat * gain_row + shift_row).astype(BF16))
    normed = jnp.concatenate(normed, axis=0)
    weight[3 * D :, :] = dw_out[...]
    weight[:D, :] = mm_tn(normed, dq[...])
    grad_buf[...] = mm_nt(dq[...], w_ref[:, :D])
    vec_buf[...] = vec[...]
    vec_buf[3:4, :] = sum_rows(dq[...].astype(F32))
    for copy in kv_copies:
        copy.wait()
    for i, buf in enumerate((dk_buf, dv_buf)):
        summed = buf[0].astype(F32)
        for k in range(1, plan.share):
            summed = summed + buf[k].astype(F32)
        summed = summed.astype(BF16)
        at = slice((1 + i) * D, (2 + i) * D)
        weight[at, :] = mm_tn(normed, summed)
        grad_buf[...] += mm_nt(summed, w_ref[:, at])
        if i == 1:
            vec_buf[4:5, :] = sum_rows(summed.astype(F32))

    away[...] = weight[spot((1 - core) * half, half), :].astype(BF16)
    core_copy = remote(away, core_in, core_sem.at[0], core_sem.at[1], partner)
    core_copy.start()

    row_copies = []
    grad_embed = jnp.zeros((1, D), F32)
    grad_gain = jnp.zeros((1, D), F32)
    grad_shift = jnp.zeros((1, D), F32)
    for k in range(n):
        owner = peers[k]
        span = spot(owner * block_rows, block_rows)
        _, scale = normalize(start[span, :].astype(F32))
        hat = hat_buf[span, :]
        grad_normed = grad_buf[span, :]
        grad_gain += sum_rows(grad_normed * hat)
        grad_shift += sum_rows(grad_normed)
        grad_start = grad_middle[span, :] + normalize_back(grad_normed * gain_row, hat, scale)
        masked = columns(mask[owner]) == 1
        grad_embed += sum_rows(jnp.where(masked, grad_start, 0.0))
        rows_buf[owner] = jnp.where(masked, 0.0, grad_start).astype(BF16)
        if k == 0:
            copy = pltpu.make_async_copy(rows_buf.at[owner], input_grad.at[me], rows_local)
        else:
            copy = remote(
                rows_buf.at[owner], input_grad.at[me], rows_ss.at[k], rows_rs.at[k],
                plan.member(owner, part),
            )
        copy.start()
        row_copies.append(copy)
    vec_buf[0:1, :] = grad_embed
    vec_buf[1:2, :] = grad_gain
    vec_buf[2:3, :] = grad_shift
    vec_copy = remote(vec_buf, vec_core, vec_core_sem.at[0], vec_core_sem.at[1], partner)
    vec_copy.start()

    core_copy.wait()
    plane_send[...] = (weight[spot(core * half, half), :] + core_in[...].astype(F32)).astype(BF16)
    plane_copies = []
    for k in range(1, n_plane):
        copy = remote(
            plane_send.at[spot(planes[k] * chunk, chunk)], plane_in.at[k],
            plane_ss.at[k], plane_rs.at[k], in_plane[k],
        )
        copy.start()
        plane_copies.append(copy)
    vec_copy.wait()
    vec_plane[plane] = vec_buf[...] + vec_core[...]
    vec_plane_copies = []
    for k in range(1, n_plane):
        copy = remote(
            vec_plane.at[plane], vec_plane.at[plane], vec_plane_ss.at[k], vec_plane_rs.at[k],
            in_plane[k],
        )
        copy.start()
        vec_plane_copies.append(copy)
    mine = plane_send[spot(plane * chunk, chunk), :].astype(F32)
    for k in range(1, n_plane):
        plane_copies[k - 1].wait()
        mine = mine + plane_in[k].astype(F32)

    depth_copies = []
    home = core * half + plane * chunk
    if cut.scatter:
        depth_send[...] = mine.astype(BF16)
        for k in range(1, n_depth):
            copy = remote(
                depth_send.at[spot(depths[k] * piece, piece)], depth_in.at[k],
                depth_ss.at[k], depth_rs.at[k], in_depth[k],
            )
            copy.start()
            depth_copies.append(copy)
    else:
        depth_in[depth] = mine.astype(BF16)
        for k in range(1, n_depth):
            copy = remote(
                depth_in.at[depth], depth_in.at[depth], depth_ss.at[k], depth_rs.at[k], in_depth[k]
            )
            copy.start()
            depth_copies.append(copy)
    for copy in vec_plane_copies:
        copy.wait()
    summed = vec_plane[0]
    for k in range(1, n_plane):
        summed = summed + vec_plane[k]
    vec_depth[depth] = summed
    vec_depth_copies = []
    for k in range(1, n_depth):
        copy = remote(
            vec_depth.at[depth], vec_depth.at[depth], vec_depth_ss.at[k], vec_depth_rs.at[k],
            in_depth[k],
        )
        copy.start()
        vec_depth_copies.append(copy)
    if cut.scatter:
        mine = depth_send[spot(depth * piece, piece), :].astype(F32)
        for k in range(1, n_depth):
            depth_copies[k - 1].wait()
            mine = mine + depth_in[k].astype(F32)
        own = spot(home + depth * piece, piece)
        total[own, :] = mine.astype(BF16)
        up_copies = []
        for k in range(1, n_depth):
            copy = remote(total.at[own], total.at[own], up_ss.at[k], up_rs.at[k], in_depth[k])
            copy.start()
            up_copies.append(copy)
        for copy in up_copies:
            copy.wait()
    else:
        for copy in depth_copies:
            copy.wait()
        mine = depth_in[0].astype(F32)
        for k in range(1, n_depth):
            mine = mine + depth_in[k].astype(F32)
        total[spot(home, chunk), :] = mine.astype(BF16)
    own = spot(home, chunk)
    wide_copies = []
    for k in range(1, n_plane):
        copy = remote(total.at[own], total.at[own], wide_ss.at[k], wide_rs.at[k], in_plane[k])
        copy.start()
        wide_copies.append(copy)
    for copy in vec_depth_copies:
        copy.wait()
    summed = vec_depth[0]
    for k in range(1, n_depth):
        summed = summed + vec_depth[k]
    vec_out[...] = summed
    for copy in wide_copies:
        copy.wait()
    own = spot(core * half, half)
    last = remote(total.at[own], total.at[own], last_sem.at[0], last_sem.at[1], partner)
    last.start()
    last.wait()
    copy = pltpu.make_async_copy(total, reduced, out_sem)
    copy.start()
    for other in row_copies:
        other.wait()
    copy.wait()


class Cut:
    def __init__(self, plan):
        self.rows = 4 * D
        self.n_plane = plan.freq * plan.batch
        self.n_depth = plan.tm // 2
        self.half = self.rows // 2
        self.chunk = self.half // self.n_plane
        self.piece = self.chunk // self.n_depth
        self.scatter = self.piece % 16 == 0 and self.piece * self.n_depth == self.chunk
        assert self.chunk * self.n_plane == self.half and self.chunk % 16 == 0


def finish(plan, dq, start, grad_middle, mask, dk_all, dv_all, w_qkv, gain, shift, dw_out, vec):
    n, rows = plan.clips, plan.rows
    cut = Cut(plan)
    dma = pltpu.SemaphoreType.DMA
    depth_shape = (cut.n_depth, cut.piece if cut.scatter else cut.chunk, D)
    vec_shape = (VEC_ROWS, D)
    return pl.pallas_call(
        functools.partial(finish_kernel, plan, cut),
        out_shape=[
            jax.ShapeDtypeStruct((n, plan.block_rows, D), BF16),
            jax.ShapeDtypeStruct((cut.rows, D), BF16),
            jax.ShapeDtypeStruct(vec_shape, F32),
        ],
        in_specs=[VMEM] * 4 + [ANY] * 2 + [VMEM] * 5,
        out_specs=[ANY, ANY, VMEM],
        scratch_shapes=[
            pltpu.VMEM((plan.share, rows, D), BF16),
            pltpu.VMEM((plan.share, rows, D), BF16),
            pltpu.VMEM((rows, D), F32),
            pltpu.VMEM((rows, D), F32),
            pltpu.VMEM((cut.rows, D), F32),
            pltpu.VMEM((cut.half, D), BF16),
            pltpu.VMEM((cut.half, D), BF16),
            pltpu.VMEM((cut.half, D), BF16),
            pltpu.VMEM((cut.n_plane, cut.chunk, D), BF16),
            pltpu.VMEM((cut.chunk, D), BF16),
            pltpu.VMEM(depth_shape, BF16),
            pltpu.VMEM((cut.rows, D), BF16),
            pltpu.VMEM((n, plan.block_rows, D), BF16),
            pltpu.VMEM(vec_shape, F32),
            pltpu.VMEM(vec_shape, F32),
            pltpu.VMEM((cut.n_plane,) + vec_shape, F32),
            pltpu.VMEM((cut.n_depth,) + vec_shape, F32),
            dma((2, plan.share)), dma((2, plan.share)), dma((2,)),
            dma((n,)), dma((n,)), dma(()), dma((2,)),
            dma((cut.n_plane,)), dma((cut.n_plane,)), dma((cut.n_depth,)), dma((cut.n_depth,)),
            dma((cut.n_depth,)), dma((cut.n_depth,)), dma((cut.n_plane,)), dma((cut.n_plane,)),
            dma((2,)), dma((2,)),
            dma((cut.n_plane,)), dma((cut.n_plane,)), dma((cut.n_depth,)), dma((cut.n_depth,)),
            dma(()),
        ],
        compiler_params=pltpu.CompilerParams(
            collective_id=1, has_side_effects=True, vmem_limit_bytes=VMEM_LIMIT
        ),
        name="finish",
    )(dq, start, grad_middle, mask, dk_all, dv_all, w_qkv, gain, shift, dw_out, vec)


def unpack_kernel(plan, place, reduced, vec, *outs):
    w_qkv, w_out, bias_up, soft = outs[:4]
    for p in range(3):
        w_qkv[:, p * D : (p + 1) * D] = reduced[p * D : (p + 1) * D, :].astype(F32)
    w_out[...] = reduced[3 * D :, :].astype(F32)
    for i, out in enumerate(outs[4:]):
        out[...] = vec[i, :]
    for i in range(FF // D):
        bias_up[i * D : (i + 1) * D] = vec[9 + i, :]
    scores = vec[13:14, :]
    lane = lax.broadcasted_iota(jnp.int32, (plan.clips, D), 1)
    slot = place[2] * 2 * plan.clips + lax.broadcasted_iota(jnp.int32, (plan.clips, D), 0)
    hits = jnp.sum(jnp.where(lane == slot, scores, 0.0), axis=1, keepdims=True)
    counts = jnp.sum(jnp.where(lane == slot + plan.clips, scores, 0.0), axis=1, keepdims=True)
    soft[...] = hits / jnp.maximum(counts, 1.0)


def unpack(plan, place, reduced, vec):
    vector = jax.ShapeDtypeStruct((D,), F32)
    return pl.pallas_call(
        functools.partial(unpack_kernel, plan),
        grid_spec=pltpu.PrefetchScalarGridSpec(
            num_scalar_prefetch=1, grid=(), in_specs=[VMEM] * 2, out_specs=[VMEM] * 13
        ),
        out_shape=[
            jax.ShapeDtypeStruct((D, 3 * D), F32),
            jax.ShapeDtypeStruct((D, D), F32),
            jax.ShapeDtypeStruct((FF,), F32),
            jax.ShapeDtypeStruct((plan.clips, 1), F32),
        ]
        + [vector] * 9,
        compiler_params=pltpu.CompilerParams(vmem_limit_bytes=VMEM_LIMIT),
        name="unpack",
    )(place, reduced, vec)


def per_device(
    plan,
    patches, patch_mask, clip_lengths, target_index, targets, out_grad,
    mask_embed, ln1_gain, ln1_shift, w_qkv, bias_q, bias_v, w_out, bias_out,
    ln2_gain, ln2_shift, w_up, bias_up, w_down, bias_down,
):
    n, rows, block_rows = plan.clips, plan.rows, plan.block_rows
    clip, part = plan.place()
    length = lax.dynamic_index_in_dim(clip_lengths, clip, keepdims=False)
    place = jnp.stack([clip, length, lax.axis_index("batch"), part]).astype(jnp.int32)
    members = [
        [f * plan.tm + b * plan.share + j for f in range(plan.freq) for b in range(plan.blocks)]
        for j in range(plan.share)
    ]

    def swap(blocks):
        return lax.all_to_all(
            blocks, ("freq", "tm"), 0, 0, axis_index_groups=members, tiled=True
        )

    start, queries, kv, mask, target = project_rows(
        plan, patches.reshape(n, block_rows, D), patch_mask, target_index,
        mask_embed, ln1_gain, ln1_shift, w_qkv, bias_q, bias_v,
    )
    start, out_grad = lax.optimization_barrier((start, out_grad))
    grad = swap(out_grad.reshape(n, block_rows, D)).reshape(rows, D)
    start = start.reshape(rows, D)
    queries = queries.reshape(rows, D)
    kv = kv.reshape(plan.keys, 2 * D)
    mixed, total = attend_forward(plan, place, queries, kv)
    block_out, grad_middle, grad_mixed, center, grad_w_up, grad_w_down, grad_w_out, vec = (
        feed_forward(
            plan, place, mixed, start, grad, mask, target, targets, w_out, bias_out,
            ln2_gain, ln2_shift, w_up, bias_up, w_down, bias_down,
        )
    )
    block_grid = swap(block_out.reshape(n, block_rows, D)).reshape(patches.shape)
    grad_w_up, grad_w_down = lax.psum((grad_w_up, grad_w_down), ("freq", "tm", "batch"))
    dq, dk_all, dv_all = attend_backward(plan, place, queries, kv, grad_mixed, total, center)
    input_grad, reduced, vec = finish(
        plan, dq, start, grad_middle, mask,
        dk_all.reshape(plan.share, rows, D), dv_all.reshape(plan.share, rows, D),
        w_qkv, ln1_gain, ln1_shift, grad_w_out, vec,
    )
    grad_w_qkv, grad_w_out, grad_bias_up, soft, *vectors = unpack(plan, place, reduced, vec)
    (grad_mask_embed, grad_ln1_gain, grad_ln1_shift, grad_bias_q, grad_bias_v, grad_bias_out,
     grad_ln2_gain, grad_ln2_shift, grad_bias_down) = vectors
    return (
        block_grid, input_grad.reshape(patches.shape), grad_mask_embed, grad_ln1_gain,
        grad_ln1_shift, grad_w_qkv, grad_bias_q, grad_bias_v, grad_w_out, grad_bias_out,
        grad_ln2_gain, grad_ln2_shift, grad_w_up, grad_bias_up, grad_w_down, grad_bias_down,
        soft.reshape(n),
    )


def solution(mesh):
    rows = P("batch", "freq", "tm", None)
    whole = P()
    in_specs = (
        rows, P("batch", "freq", "tm"), P("batch"), P("batch", "freq", "tm"),
        P("batch", None, None), rows,
    ) + (whole,) * 14
    out_specs = (rows, rows) + (whole,) * 14 + (P("batch"),)

    def body(*args):
        return per_device(Plan(mesh, args[0]), *args)

    return jax.shard_map(
        body, mesh=mesh, in_specs=in_specs, out_specs=out_specs, check_vma=False
    )
```

```python
import functools

import jax
import jax.numpy as jnp
from jax import lax
from jax.experimental import pallas as pl
from jax.experimental.pallas import tpu as pltpu
from jax.sharding import PartitionSpec as P

D = 384
FF = 1536
HEADS = 6
HEAD_DIM = 64
PAIRS = HEADS // 2
PAIR = 2 * HEAD_DIM
SCALE = HEAD_DIM ** (-0.5)
DEAD = -1e9
EPS = 1e-06
VEC_ROWS = 16
MESH = pl.DeviceIdType.MESH
VMEM_LIMIT = 60 * 2**20
ANY = pl.BlockSpec(memory_space=pl.ANY)
VMEM = pl.BlockSpec(memory_space=pltpu.VMEM)
BF16 = jnp.bfloat16
F32 = jnp.float32


def mm(left_mat, right_mat):
    return jnp.dot(left_mat, right_mat, preferred_element_type=F32)


def mm_nt(left_mat, right_mat):
    return lax.dot_general(
        left_mat, right_mat, (((1,), (1,)), ((), ())), preferred_element_type=F32
    )


def mm_tn(left_mat, right_mat):
    return lax.dot_general(
        left_mat, right_mat, (((0,), (0,)), ((), ())), preferred_element_type=F32
    )


def row(ref):
    return ref[...].astype(F32).reshape(1, -1)


def normalize(rows):
    center = rows - jnp.mean(rows, axis=-1, keepdims=True)
    scale = lax.rsqrt(jnp.mean(center * center, axis=-1, keepdims=True) + EPS)
    return center * scale, scale


def normalize_back(grad_hat, hat, scale):
    first = jnp.mean(grad_hat, axis=-1, keepdims=True)
    second = jnp.mean(grad_hat * hat, axis=-1, keepdims=True)
    return scale * (grad_hat - first - hat * second)


def sum_rows(rows):
    return jnp.sum(rows, axis=0, keepdims=True)


def columns(ints):
    freq_rows, time_rows = ints.shape
    shape = (time_rows, time_rows)
    eye = lax.broadcasted_iota(jnp.int32, shape, 0) == lax.broadcasted_iota(jnp.int32, shape, 1)
    parts = [
        jnp.sum(jnp.where(eye, ints[f : f + 1, :], 0), axis=1, keepdims=True)
        for f in range(freq_rows)
    ]
    return jnp.concatenate(parts, axis=0)


class Plan:
    def __init__(self, mesh, patches):
        self.freq = mesh.shape["freq"]
        self.tm = mesh.shape["tm"]
        self.batch = mesh.shape["batch"]
        self.clips, self.freq_rows, self.time_rows, _ = patches.shape
        self.share = self.freq * self.tm // self.clips
        self.blocks = self.tm // self.share
        self.block_rows = self.freq_rows * self.time_rows
        self.rows = self.clips * self.block_rows
        self.keys = self.share * self.rows
        assert self.freq * self.blocks == self.clips and self.blocks * self.share == self.tm

    def place(self):
        time_id = lax.axis_index("tm")
        return lax.axis_index("freq") * self.blocks + time_id // self.share, time_id % self.share

    def member(self, member, part):
        return {
            "freq": member // self.blocks,
            "tm": (member % self.blocks) * self.share + part,
        }

    def sharer(self, part):
        time_id = lax.axis_index("tm")
        return {"tm": time_id // self.share * self.share + part}

    def key_time(self, place):
        part = place // self.rows
        block = (place // self.block_rows) % self.clips % self.blocks
        return (block * self.share + part) * self.time_rows + place % self.time_rows


def greet(devices):
    barrier = pltpu.get_barrier_semaphore()
    for device in devices:
        pl.semaphore_signal(barrier, inc=1, device_id=device, device_id_type=MESH)
    pl.semaphore_wait(barrier, len(devices))


def remote(src, dst, send_sem, recv_sem, device):
    return pltpu.make_async_remote_copy(
        src_ref=src, dst_ref=dst, send_sem=send_sem, recv_sem=recv_sem,
        device_id=device, device_id_type=MESH,
    )


def front_kernel(
    plan, lengths, patches, mask, target, out_grad, embed, gain, shift, w_ref, bias_q, bias_v,
    start_out, q_out, qt_out, k_out, v_out, mixed_out, total_out, mask_out, target_out, grad_out,
    taken, mask_in, target_in, start_buf, q_buf, qt_buf, kv_buf, k_buf, v_buf, vt_buf,
    mixed_buf, total_buf, score_a, score_b,
    send_sem, recv_sem, local_sem, kv_send, kv_recv, grad_send, grad_recv, out_sem,
):
    me, part = plan.place()
    n, rows, keys, block_rows = plan.clips, plan.rows, plan.keys, plan.block_rows
    peers = [lax.rem(me + step, n) for step in range(n)]
    sharers = [lax.rem(part + step, plan.share) for step in range(plan.share)]
    greet(
        [plan.member(peers[step], part) for step in range(1, n)]
        + [plan.sharer(sharers[step]) for step in range(1, plan.share)]
    )
    streams = ((mask, mask_in), (target, target_in), (patches, taken))
    arrivals = []
    for step in range(n):
        copies = []
        for i, (src, dst) in enumerate(streams):
            if step == 0:
                copy = pltpu.make_async_copy(src.at[me], dst.at[me], local_sem.at[i])
            else:
                copy = remote(
                    src.at[peers[step]], dst.at[me], send_sem.at[i, step], recv_sem.at[i, step],
                    plan.member(peers[step], part),
                )
            copy.start()
            copies.append(copy)
        arrivals.append(copies)
    gain_row, shift_row, embed_row = row(gain), row(shift), row(embed)
    bias_q_row, bias_v_row = row(bias_q), row(bias_v)
    waits, shared = [], []

    def save(index, src, dst):
        copy = pltpu.make_async_copy(src, dst, out_sem.at[index])
        copy.start()
        waits.append(copy)

    for step in range(n):
        source = lax.rem(me + n - step, n)
        for copy in arrivals[step]:
            if step == 0:
                copy.wait()
            else:
                copy.wait_recv()
        masked = columns(mask_in[source]) == 1
        start = jnp.where(masked, embed_row, taken[source].astype(F32))
        start_buf[source] = start.astype(BF16)
        hat, _ = normalize(start)
        normed = (hat * gain_row + shift_row).astype(BF16)
        project = mm(normed, w_ref[...])
        queries = (project[:, :D] + bias_q_row).astype(BF16)
        q_buf[source] = (queries.astype(F32) * SCALE).astype(BF16)
        kv_buf[part, source, :, :D] = project[:, D : 2 * D].astype(BF16)
        kv_buf[part, source, :, D:] = (project[:, 2 * D :] + bias_v_row).astype(BF16)
        for other in range(1, plan.share):
            copy = remote(
                kv_buf.at[part, source], kv_buf.at[part, source], kv_send.at[other, step],
                kv_recv.at[other, step], plan.sharer(sharers[other]),
            )
            copy.start()
            shared.append(copy)
    for step in range(n):
        if step == 0:
            copy = pltpu.make_async_copy(out_grad.at[me], grad_out.at[me], local_sem.at[0])
        else:
            copy = remote(
                out_grad.at[peers[step]], grad_out.at[me], grad_send.at[step], grad_recv.at[step],
                plan.member(peers[step], part),
            )
        copy.start()
        waits.append(copy)
    save(0, start_buf, start_out)
    save(1, q_buf, q_out)
    save(2, mask_in, mask_out)
    save(3, target_in, target_out)
    for i in range(n):
        at = slice(i * block_rows, (i + 1) * block_rows)
        qt_buf[:, at] = q_buf[i].T
    save(4, qt_buf, qt_out)
    for copy in shared:
        copy.wait()
    length = lengths[me]
    first = kv_buf[0, 0, 0:1, :D]
    for i in range(plan.share):
        for b in range(n):
            begin = i * rows + b * block_rows
            at = slice(begin, begin + block_rows)
            ids = lax.broadcasted_iota(jnp.int32, (block_rows, 1), 0) + begin
            live = plan.key_time(ids) < length
            k_buf[at, :] = jnp.where(live, kv_buf[i, b, :, :D], first)
            value = kv_buf[i, b, :, D:]
            value = jnp.where(live, value, jnp.zeros_like(value))
            v_buf[at, :] = value
            turned = value.T
            ids = lax.broadcasted_iota(jnp.int32, (16, block_rows), 1) + begin
            top = lax.broadcasted_iota(jnp.int32, (16, block_rows), 0) == 0
            count = jnp.where((plan.key_time(ids) < length) & top, 1.0, 0.0).astype(BF16)
            for h in range(HEADS):
                vt_buf[h, :HEAD_DIM, at] = turned[h * HEAD_DIM : (h + 1) * HEAD_DIM, :]
                vt_buf[h, HEAD_DIM:, at] = count
    save(5, k_buf, k_out)
    save(6, v_buf, v_out)

    width = score_a.shape[1]
    spans = rows // width
    items = HEADS * spans
    lane = lax.broadcasted_iota(jnp.int32, (1, PAIR), 1)

    def score(item, buf):
        head, span = item // spans, item % spans
        pair = pl.ds(pl.multiple_of(head // 2 * PAIR, PAIR), PAIR)
        at = pl.ds(pl.multiple_of(span * width, width), width)
        k_own = jnp.where(lane // HEAD_DIM == head % 2, k_buf[:, pair], jnp.zeros((), BF16))
        scores = mm(k_own, qt_buf[pair, at])
        buf[...] = scores
        return jnp.max(scores, axis=0, keepdims=True)

    def blend(item, buf, top):
        head, span = item // spans, item % spans
        at = pl.ds(pl.multiple_of(span * width, width), width)
        raised = jnp.exp(buf[...] - top).astype(BF16)
        out = mm(vt_buf[head], raised)
        row_total = out[HEAD_DIM : HEAD_DIM + 1, :]
        into = pl.ds(pl.multiple_of(head * HEAD_DIM, HEAD_DIM), HEAD_DIM)
        mixed_buf[into, at] = (out[:HEAD_DIM, :] / row_total).astype(BF16)
        total_buf[head, :, at] = top + jnp.log(row_total)

    def two(i, top_a):
        top_b = score(2 * i + 1, score_b)
        blend(2 * i, score_a, top_a)
        top_a = score(2 * i + 2, score_a)
        blend(2 * i + 1, score_b, top_b)
        return top_a

    top_a = lax.fori_loop(0, items // 2 - 1, two, score(0, score_a))
    top_b = score(items - 1, score_b)
    blend(items - 2, score_a, top_a)
    blend(items - 1, score_b, top_b)
    save(7, mixed_buf, mixed_out)
    save(8, total_buf, total_out)
    for step in range(1, n):
        for copy in arrivals[step]:
            copy.wait_send()
    for copy in waits:
        copy.wait()


def front(plan, lengths, patches, mask, target, out_grad, embed, gain, shift, w_qkv, bias_q, bias_v):
    n, rows, keys, block_rows = plan.clips, plan.rows, plan.keys, plan.block_rows
    width = min(512, rows)
    assert HEADS * (rows // width) % 2 == 0
    dma = pltpu.SemaphoreType.DMA
    blocks = (n, block_rows, D)
    total = (HEADS, 1, rows)
    shapes = [
        (blocks, BF16), (blocks, BF16), ((D, rows), BF16), ((keys, D), BF16), ((keys, D), BF16),
        ((D, rows), BF16), (total, F32), (mask.shape, jnp.int32), (mask.shape, jnp.int32),
        (blocks, BF16),
    ]
    return pl.pallas_call(
        functools.partial(front_kernel, plan),
        out_shape=[jax.ShapeDtypeStruct(shape, kind) for shape, kind in shapes],
        in_specs=[pl.BlockSpec(memory_space=pltpu.SMEM)] + [ANY] * 4 + [VMEM] * 6,
        out_specs=[ANY] * 10,
        scratch_shapes=[
            pltpu.VMEM(blocks, BF16),
            pltpu.VMEM(mask.shape, jnp.int32),
            pltpu.VMEM(mask.shape, jnp.int32),
            pltpu.VMEM(blocks, BF16),
            pltpu.VMEM(blocks, BF16),
            pltpu.VMEM((D, rows), BF16),
            pltpu.VMEM((plan.share, n, block_rows, 2 * D), BF16),
            pltpu.VMEM((keys, D), BF16),
            pltpu.VMEM((keys, D), BF16),
            pltpu.VMEM((HEADS, HEAD_DIM + 16, keys), BF16),
            pltpu.VMEM((D, rows), BF16),
            pltpu.VMEM(total, F32),
            pltpu.VMEM((keys, width), F32),
            pltpu.VMEM((keys, width), F32),
            dma((3, n)), dma((3, n)), dma((3,)),
            dma((plan.share, n)), dma((plan.share, n)), dma((n,)), dma((n,)), dma((9,)),
        ],
        compiler_params=pltpu.CompilerParams(
            collective_id=0, has_side_effects=True, vmem_limit_bytes=VMEM_LIMIT
        ),
        name="front",
    )(lengths, patches, mask, target, out_grad, embed, gain, shift, w_qkv, bias_q, bias_v)


def gelu_parts(rows):
    lower = 0.5 * (1.0 + lax.erf(rows * 0.7071067811865476))
    slope = lower + rows * (jnp.exp(-0.5 * rows * rows) * 0.3989422804014327)
    return rows * lower, slope


def feed_kernel(
    plan, place, mixed, start, grad, mask, target, targets, w_out, bias_out, gain, shift,
    w_up, bias_up, w_down, bias_down,
    block_out, grad_middle, grad_mixed, grad_mixed_t, center, payload, grad_w_out, vec,
    middle, second, down_sum, second_sum, act_buf, up_buf,
):
    step = pl.program_id(0)
    steps = pl.num_programs(0)
    rows = plan.rows
    tile = min(256, rows)
    tiles = [slice(i * tile, (i + 1) * tile) for i in range(rows // tile)]
    gain_row, shift_row = row(gain), row(shift)

    @pl.when(step == 0)
    def _():
        vec[...] = jnp.zeros_like(vec)
        for part in tiles:
            rows_in = start[part, :].astype(F32) + mm_tn(mixed[:, part], w_out[...])
            rows_in = rows_in + row(bias_out)
            middle[part, :] = rows_in
            hat, _ = normalize(rows_in)
            second[part, :] = (hat * gain_row + shift_row).astype(BF16)
        down_sum[...] = jnp.zeros_like(down_sum)
        second_sum[...] = jnp.zeros_like(second_sum)

    bias_row = row(bias_up.at[0])
    for part in tiles:
        hidden = mm(second[part, :], w_up[...]) + bias_row
        active, slope = gelu_parts(hidden)
        active = active.astype(BF16)
        act_buf[part, :] = active
        down_sum[part, :] += mm(active, w_down[...])
        grad_up = (mm_nt(grad[part, :], w_down[...]) * slope).astype(BF16)
        up_buf[part, :] = grad_up
        second_sum[part, :] += mm_nt(grad_up, w_up[...])
    payload[0, 0] = mm_tn(act_buf[...], grad[...]).astype(BF16)
    payload[1, 0] = mm_tn(second[...], up_buf[...]).astype(BF16)
    vec[pl.ds(9 + step, 1), :] = sum_rows(up_buf[...].astype(F32))

    @pl.when(step == steps - 1)
    def _():
        clip, length, batch = place[0], place[1], place[2]
        cand = lax.broadcasted_iota(jnp.int32, (1, targets.shape[1]), 1)
        vec[8:9, :] = sum_rows(grad[...].astype(F32))
        total_hit = jnp.zeros((1, 1), F32)
        total_count = jnp.zeros((1, 1), F32)
        per_tile = tile // plan.block_rows
        for t, part in enumerate(tiles):
            result = middle[part, :] + down_sum[part, :] + row(bias_down)
            result = result.astype(BF16)
            block_out[part, :] = result
            hat, scale = normalize(middle[part, :])
            grad_second = second_sum[part, :]
            vec[6:7, :] += sum_rows(grad_second * hat)
            vec[7:8, :] += sum_rows(grad_second)
            back = normalize_back(grad_second * gain_row, hat, scale)
            back = grad[part, :].astype(F32) + back
            grad_middle[part, :] = back
            branch = back.astype(BF16)
            act_buf[part, :] = branch
            vec[5:6, :] += sum_rows(branch.astype(F32))
            grad_mixed[part, :] = mm_nt(branch, w_out[...]).astype(BF16)
            down = mm_nt(w_out[...], branch).astype(BF16)
            grad_mixed_t[:, part] = down
            product = down.astype(F32) * mixed[:, part].astype(F32)
            for h in range(HEADS):
                center[h, :, part] = sum_rows(product[h * HEAD_DIM : (h + 1) * HEAD_DIM, :])
            logits = mm_nt(result, targets[0])
            raised = jnp.exp(logits - jnp.max(logits, axis=1, keepdims=True))
            sources = range(t * per_tile, (t + 1) * per_tile)
            target_col = jnp.concatenate([columns(target[s]) for s in sources], axis=0)
            mask_col = jnp.concatenate([columns(mask[s]) for s in sources], axis=0)
            hit = jnp.sum(jnp.where(cand == target_col, raised, 0.0), axis=1, keepdims=True)
            hit = hit / jnp.sum(raised, axis=1, keepdims=True)
            ids = lax.broadcasted_iota(jnp.int32, (tile, 1), 0) + t * tile + place[3] * rows
            counted = jnp.where((plan.key_time(ids) < length) & (mask_col == 1), 1.0, 0.0)
            total_hit += jnp.sum(hit * counted, axis=0, keepdims=True)
            total_count += jnp.sum(counted, axis=0, keepdims=True)
        grad_w_out[...] = mm(mixed[...], act_buf[...])
        lane = lax.broadcasted_iota(jnp.int32, (1, D), 1)
        slot = batch * 2 * plan.clips + clip
        scores = jnp.where(lane == slot, total_hit, 0.0)
        vec[13:14, :] = scores + jnp.where(lane == slot + plan.clips, total_count, 0.0)


def feed_forward(
    plan, place, mixed, start, grad, mask, target, targets, w_out, bias_out, gain, shift,
    w_up, bias_up, w_down, bias_down,
):
    rows = plan.rows
    steps = FF // D

    def full(shape):
        return pl.BlockSpec(shape, lambda i, s: (0,) * len(shape))

    return pl.pallas_call(
        functools.partial(feed_kernel, plan),
        grid_spec=pltpu.PrefetchScalarGridSpec(
            num_scalar_prefetch=1,
            grid=(steps,),
            in_specs=[
                full((D, rows)), full((rows, D)), full((rows, D)),
                full(mask.shape), full(mask.shape),
                pl.BlockSpec((1,) + targets.shape[1:], lambda i, s: (s[0], 0, 0)),
                full((D, D)), full((D,)), full((D,)), full((D,)),
                pl.BlockSpec((D, D), lambda i, s: (0, i)),
                pl.BlockSpec((1, 1, D), lambda i, s: (i, 0, 0)),
                pl.BlockSpec((D, D), lambda i, s: (i, 0)),
                full((D,)),
            ],
            out_specs=[
                full((rows, D)), full((rows, D)), full((rows, D)), full((D, rows)),
                full((HEADS, 1, rows)),
                pl.BlockSpec((2, 1, D, D), lambda i, s: (0, i, 0, 0)),
                full((D, D)), full((VEC_ROWS, D)),
            ],
            scratch_shapes=[
                pltpu.VMEM((rows, D), F32), pltpu.VMEM((rows, D), BF16),
                pltpu.VMEM((rows, D), F32), pltpu.VMEM((rows, D), F32),
                pltpu.VMEM((rows, D), BF16), pltpu.VMEM((rows, D), BF16),
            ],
        ),
        out_shape=[
            jax.ShapeDtypeStruct((rows, D), BF16),
            jax.ShapeDtypeStruct((rows, D), F32),
            jax.ShapeDtypeStruct((rows, D), BF16),
            jax.ShapeDtypeStruct((D, rows), BF16),
            jax.ShapeDtypeStruct((HEADS, 1, rows), F32),
            jax.ShapeDtypeStruct((2, steps, D, D), BF16),
            jax.ShapeDtypeStruct((D, D), F32),
            jax.ShapeDtypeStruct((VEC_ROWS, D), F32),
        ],
        compiler_params=pltpu.CompilerParams(vmem_limit_bytes=VMEM_LIMIT),
        cost_estimate=pl.CostEstimate(
            flops=12 * rows * FF * D, bytes_accessed=20 * rows * D, transcendentals=2 * rows * FF
        ),
        name="feed_forward",
    )(
        place, mixed, start, grad, mask, target, targets, w_out, bias_out, gain, shift,
        w_up, bias_up.reshape(steps, 1, D), w_down, bias_down,
    )


class Ring:
    def __init__(self, cut, at, half_src, own_half, core_in, mine, plane_in, part_buf, depth_in, total, sems):
        self.cut, self.at = cut, at
        self.half_src, self.own_half, self.core_in, self.mine = half_src, own_half, core_in, mine
        self.plane_in, self.part_buf, self.depth_in, self.total = plane_in, part_buf, depth_in, total
        self.core_sem, self.plane_sem, self.depth_sem, self.up_sem, self.wide_sem = sems

    def core_copy(self):
        return remote(
            self.half_src, self.core_in, self.core_sem.at[0], self.core_sem.at[1], self.at.partner
        )

    def plane_copies(self):
        chunk = self.cut.chunk
        return [
            remote(
                self.mine.at[spot(self.at.planes[k] * chunk, chunk)], self.plane_in.at[k],
                self.plane_sem.at[0, k], self.plane_sem.at[1, k], self.at.in_plane[k],
            )
            for k in range(1, self.cut.n_plane)
        ]

    def depth_copies(self):
        piece, copies = self.cut.piece, []
        for k in range(1, self.cut.n_depth):
            if self.cut.scatter:
                src = self.part_buf.at[spot(self.at.depths[k] * piece, piece)]
                dst = self.depth_in.at[k]
            else:
                src = dst = self.depth_in.at[self.at.depth]
            copies.append(
                remote(
                    src, dst, self.depth_sem.at[0, k], self.depth_sem.at[1, k], self.at.in_depth[k]
                )
            )
        return copies

    def same(self, first, count, sems, k, device):
        own = spot(first, count)
        return remote(self.total.at[own], self.total.at[own], sems.at[0, k], sems.at[1, k], device)

    def home(self):
        return self.at.core * self.cut.half + self.at.plane * self.cut.chunk

    def up_copies(self):
        first = self.home() + self.at.depth * self.cut.piece
        return [
            self.same(first, self.cut.piece, self.up_sem, k, self.at.in_depth[k])
            for k in range(1, self.cut.n_depth)
        ]

    def wide_copies(self):
        return [
            self.same(self.home(), self.cut.chunk, self.wide_sem, k, self.at.in_plane[k])
            for k in range(1, self.cut.n_plane)
        ]

    def last_copy(self):
        own = spot(self.at.core * self.cut.half, self.cut.half)
        return remote(
            self.total.at[own], self.total.at[own], self.core_sem.at[2], self.core_sem.at[3],
            self.at.partner,
        )

    def begin(self):
        self.core_copy().start()

    def to_plane(self):
        self.core_copy().wait()
        own = self.own_half().astype(F32) + self.core_in[...].astype(F32)
        self.mine[...] = own.astype(BF16)
        for copy in self.plane_copies():
            copy.start()

    def to_depth(self):
        chunk = self.cut.chunk
        mine = self.mine[spot(self.at.plane * chunk, chunk), :].astype(F32)
        for k, copy in enumerate(self.plane_copies()):
            copy.wait()
            mine = mine + self.plane_in[k + 1].astype(F32)
        if self.cut.scatter:
            self.part_buf[...] = mine.astype(BF16)
        else:
            self.depth_in[self.at.depth] = mine.astype(BF16)
        for copy in self.depth_copies():
            copy.start()

    def back_up(self):
        piece, copies = self.cut.piece, self.depth_copies()
        if self.cut.scatter:
            mine = self.part_buf[spot(self.at.depth * piece, piece), :].astype(F32)
            for k, copy in enumerate(copies):
                copy.wait()
                mine = mine + self.depth_in[k + 1].astype(F32)
            self.total[spot(self.home() + self.at.depth * piece, piece), :] = mine.astype(BF16)
            for copy in self.up_copies():
                copy.start()
        else:
            for copy in copies:
                copy.wait()
            mine = self.depth_in[0].astype(F32)
            for k in range(1, self.cut.n_depth):
                mine = mine + self.depth_in[k].astype(F32)
            self.total[spot(self.home(), self.cut.chunk), :] = mine.astype(BF16)

    def back_wide(self):
        if self.cut.scatter:
            for copy in self.up_copies():
                copy.wait()
        for copy in self.wide_copies():
            copy.start()

    def back_core(self):
        for copy in self.wide_copies():
            copy.wait()
        self.last_copy().start()

    def end(self):
        self.last_copy().wait()


class Cut:
    def __init__(self, plan, rows):
        self.rows = rows
        self.n_plane = plan.freq * plan.batch
        self.n_depth = plan.tm // 2
        self.half = rows // 2
        self.chunk = self.half // self.n_plane
        self.piece = self.chunk // self.n_depth
        self.scatter = self.piece % 16 == 0 and self.piece * self.n_depth == self.chunk
        assert self.chunk * self.n_plane == self.half and self.chunk % 16 == 0

    def buffers(self):
        depth = self.piece if self.scatter else self.chunk
        return [
            pltpu.VMEM((self.half, D), BF16),
            pltpu.VMEM((self.half, D), BF16),
            pltpu.VMEM((self.half, D), BF16),
            pltpu.VMEM((self.n_plane, self.chunk, D), BF16),
            pltpu.VMEM((self.chunk, D), BF16),
            pltpu.VMEM((self.n_depth, depth, D), BF16),
            pltpu.VMEM((self.rows, D), BF16),
        ]

    def semaphores(self):
        dma = pltpu.SemaphoreType.DMA
        return [
            dma((4,)), dma((2, self.n_plane)), dma((2, self.n_depth)), dma((2, self.n_depth)),
            dma((2, self.n_plane)),
        ]


class Place:
    def __init__(self, plan):
        time_id = lax.axis_index("tm")
        n_plane, n_depth = plan.freq * plan.batch, plan.tm // 2
        self.core, self.depth = time_id % 2, time_id // 2
        self.plane = lax.axis_index("freq") * plan.batch + lax.axis_index("batch")
        self.partner = {"tm": time_id + 1 - 2 * self.core}
        self.planes = [lax.rem(self.plane + k, n_plane) for k in range(n_plane)]
        self.depths = [lax.rem(self.depth + k, n_depth) for k in range(n_depth)]
        self.in_plane = [{"freq": v // plan.batch, "batch": v % plan.batch} for v in self.planes]
        self.in_depth = [{"tm": v * 2 + self.core} for v in self.depths]


def spot(first, count):
    return pl.ds(pl.multiple_of(first, 16), count)


def back_kernel(
    plan, wide_cut, cut, lengths, block_rows_in, payload, q_ref, qt_ref, k_ref, v_ref, do_ref, dot_ref,
    log_total, center, start, grad_middle, mask, w_ref, gain, shift, dw_out, vec,
    block_grid, input_grad, wide_out, reduced, vec_out,
    kt_buf, score_a, score_b, prob_a, prob_b, dqt_sum, dk_all, dv_all, dk_in, dv_in,
    hat_buf, grad_buf, weight, rows_buf, vec_buf, vec_core, vec_plane, vec_depth,
    *rest,
):
    bufs, sems = rest[:14], rest[14:]
    wide_bufs, small_bufs = bufs[:7], bufs[7:]
    wide_sems, small_sems = sems[:5], sems[5:10]
    (grid_ss, grid_rs, kv_ss, kv_rs, rows_ss, rows_rs, local_sem, vec_core_sem,
     vec_plane_sem, vec_depth_sem) = sems[10:]
    n, rows, keys, block_rows = plan.clips, plan.rows, plan.keys, plan.block_rows
    me, part = plan.place()
    at = Place(plan)
    n_plane, n_depth = cut.n_plane, cut.n_depth
    peers = [lax.rem(me + k, n) for k in range(n)]
    sharers = [lax.rem(part + k, plan.share) for k in range(plan.share)]
    length = lengths[me]

    own_half_copy = pltpu.make_async_copy(
        payload.at[spot(at.core * wide_cut.half, wide_cut.half)], wide_bufs[0], local_sem.at[0]
    )
    wide = Ring(
        wide_cut, at, payload.at[spot((1 - at.core) * wide_cut.half, wide_cut.half)],
        lambda: wide_bufs[0][...], *wide_bufs[1:], wide_sems,
    )
    small = Ring(
        cut, at, small_bufs[0], lambda: weight[spot(at.core * cut.half, cut.half), :],
        *small_bufs[1:], small_sems,
    )
    greet(
        [plan.member(peers[k], part) for k in range(1, n)]
        + [plan.sharer(sharers[k]) for k in range(1, plan.share)]
        + [at.partner]
        + at.in_plane[1:]
        + at.in_depth[1:]
    )
    own_half_copy.start()
    wide.begin()
    home_copies = [
        pltpu.make_async_copy(block_rows_in.at[me], block_grid.at[me], local_sem.at[1])
    ]
    for k in range(1, n):
        home_copies.append(
            remote(
                block_rows_in.at[peers[k]], block_grid.at[me], grid_ss.at[k], grid_rs.at[k],
                plan.member(peers[k], part),
            )
        )
    for copy in home_copies:
        copy.start()

    def kv_copies():
        return [
            remote(
                src.at[sharers[k]], dst.at[k], kv_ss.at[i, k], kv_rs.at[i, k],
                plan.sharer(sharers[k]),
            )
            for i, (src, dst) in enumerate(((dk_all, dk_in), (dv_all, dv_in)))
            for k in range(1, plan.share)
        ]

    tile = min(256, rows)
    for i in range(keys // tile):
        span = slice(i * tile, (i + 1) * tile)
        ids = lax.broadcasted_iota(jnp.int32, (1, tile), 1) + i * tile
        turned = k_ref[span, :].T
        live = plan.key_time(ids) < length
        kt_buf[:, span] = jnp.where(live, turned, jnp.zeros_like(turned))
    dqt_sum[...] = jnp.zeros_like(dqt_sum)

    block = score_a.shape[0]
    per_part = rows // block
    lane = lax.broadcasted_iota(jnp.int32, (1, PAIR), 1)
    owns = [lane // HEAD_DIM == e for e in range(2)]
    zero = jnp.zeros((), BF16)
    bodies = PAIRS * per_part * plan.share

    def body(i, carry):
        order, pair = i // PAIRS, i % PAIRS
        owner = lax.rem(part + 1 + order // per_part, plan.share)
        begin = order % per_part * block
        span = pl.ds(pl.multiple_of(owner * rows + begin, block), block)
        inside = pl.ds(pl.multiple_of(begin, block), block)
        cols = pl.ds(pl.multiple_of(pair * PAIR, PAIR), PAIR)
        for e, (score_buf, prob_buf) in enumerate(((score_a, prob_a), (score_b, prob_b))):
            score_buf[...] = mm(jnp.where(owns[e], k_ref[span, cols], zero), qt_ref[cols, :])
            prob_buf[...] = mm(jnp.where(owns[e], v_ref[span, cols], zero), dot_ref[cols, :])
        grad_k, grad_v = [], []
        for e, (score_buf, prob_buf) in enumerate(((score_a, prob_a), (score_b, prob_b))):
            head = pl.ds(pl.multiple_of(pair * PAIR + e * HEAD_DIM, HEAD_DIM), HEAD_DIM)
            prob = jnp.exp(score_buf[...] - log_total[2 * pair + e])
            grad_scores = (prob * (prob_buf[...] - center[2 * pair + e])).astype(BF16)
            grad_v.append(mm(prob.astype(BF16), jnp.where(owns[e], do_ref[:, cols], zero)))
            grad_k.append(mm(grad_scores, jnp.where(owns[e], q_ref[:, cols], zero)))
            dqt_sum[head, :] += mm(kt_buf[head, span], grad_scores)
        dk_all[owner, inside, cols] = (grad_k[0] + grad_k[1]).astype(BF16)
        dv_all[owner, inside, cols] = (grad_v[0] + grad_v[1]).astype(BF16)

        def at_step(step, do):
            pl.when(i == step)(do)

        def to_plane():
            own_half_copy.wait()
            wide.to_plane()

        def send_keys():
            for copy in kv_copies():
                copy.start()

        at_step(1, to_plane)
        at_step(bodies - 6, wide.to_depth)
        at_step(bodies - 4, wide.back_up)
        at_step(bodies - 3, wide.back_wide)
        at_step(bodies - PAIRS * per_part - 1, send_keys)
        return carry

    lax.fori_loop(0, bodies, body, 0)

    gain_row, shift_row = row(gain), row(shift)
    dq = (dqt_sum[...] * SCALE).T.astype(BF16)
    normed = []
    for i in range(rows // tile):
        span = slice(i * tile, (i + 1) * tile)
        hat, _ = normalize(start[span, :].astype(F32))
        hat_buf[span, :] = hat
        normed.append((hat * gain_row + shift_row).astype(BF16))
    normed = jnp.concatenate(normed, axis=0)
    weight[3 * D :, :] = dw_out[...]
    weight[:D, :] = mm_tn(normed, dq)
    grad_buf[...] = mm_nt(dq, w_ref[:, :D])
    vec_buf[...] = vec[...]
    vec_buf[3:4, :] = sum_rows(dq.astype(F32))
    for copy in kv_copies():
        copy.wait()
    ids = lax.broadcasted_iota(jnp.int32, (rows, 1), 0)
    live = plan.key_time(ids + part * rows) < length
    for i, (own, buf) in enumerate(((dk_all, dk_in), (dv_all, dv_in))):
        summed = own[part].astype(F32)
        for k in range(1, plan.share):
            summed = summed + buf[k].astype(F32)
        summed = jnp.where(live, summed, 0.0).astype(BF16)
        cols = slice((1 + i) * D, (2 + i) * D)
        weight[cols, :] = mm_tn(normed, summed)
        grad_buf[...] += mm_nt(summed, w_ref[:, cols])
        if i == 1:
            vec_buf[4:5, :] = sum_rows(summed.astype(F32))
    small_bufs[0][...] = weight[spot((1 - at.core) * cut.half, cut.half), :].astype(BF16)
    small.begin()

    row_copies = []
    grad_embed = jnp.zeros((1, D), F32)
    grad_gain = jnp.zeros((1, D), F32)
    grad_shift = jnp.zeros((1, D), F32)
    for k in range(n):
        owner = peers[k]
        span = spot(owner * block_rows, block_rows)
        _, scale = normalize(start[span, :].astype(F32))
        hat = hat_buf[span, :]
        grad_normed = grad_buf[span, :]
        grad_gain += sum_rows(grad_normed * hat)
        grad_shift += sum_rows(grad_normed)
        grad_start = grad_middle[span, :] + normalize_back(grad_normed * gain_row, hat, scale)
        masked = columns(mask[owner]) == 1
        grad_embed += sum_rows(jnp.where(masked, grad_start, 0.0))
        rows_buf[owner] = jnp.where(masked, 0.0, grad_start).astype(BF16)
        if k == 0:
            copy = pltpu.make_async_copy(rows_buf.at[owner], input_grad.at[me], local_sem.at[2])
        else:
            copy = remote(
                rows_buf.at[owner], input_grad.at[me], rows_ss.at[k], rows_rs.at[k],
                plan.member(owner, part),
            )
        copy.start()
        row_copies.append(copy)
    vec_buf[0:1, :] = grad_embed
    vec_buf[1:2, :] = grad_gain
    vec_buf[2:3, :] = grad_shift
    vec_copy = remote(vec_buf, vec_core, vec_core_sem.at[0], vec_core_sem.at[1], at.partner)
    vec_copy.start()
    small.to_plane()
    wide.back_core()
    vec_copy.wait()
    vec_plane[at.plane] = vec_buf[...] + vec_core[...]
    vec_plane_copies = []
    for k in range(1, n_plane):
        copy = remote(
            vec_plane.at[at.plane], vec_plane.at[at.plane], vec_plane_sem.at[0, k],
            vec_plane_sem.at[1, k], at.in_plane[k],
        )
        copy.start()
        vec_plane_copies.append(copy)
    small.to_depth()
    wide.end()
    wide_copy = pltpu.make_async_copy(wide.total, wide_out, local_sem.at[0])
    wide_copy.start()
    for copy in vec_plane_copies:
        copy.wait()
    summed = vec_plane[0]
    for k in range(1, n_plane):
        summed = summed + vec_plane[k]
    vec_depth[at.depth] = summed
    vec_depth_copies = []
    for k in range(1, n_depth):
        copy = remote(
            vec_depth.at[at.depth], vec_depth.at[at.depth], vec_depth_sem.at[0, k],
            vec_depth_sem.at[1, k], at.in_depth[k],
        )
        copy.start()
        vec_depth_copies.append(copy)
    small.back_up()
    small.back_wide()
    for copy in vec_depth_copies:
        copy.wait()
    summed = vec_depth[0]
    for k in range(1, n_depth):
        summed = summed + vec_depth[k]
    vec_out[...] = summed
    small.back_core()
    small.end()
    copy = pltpu.make_async_copy(small.total, reduced, local_sem.at[3])
    copy.start()
    for other in row_copies + home_copies + [wide_copy, copy]:
        other.wait()


def back(
    plan, lengths, block_out, payload, queries, queries_t, key_rows, value_rows, grad_mixed,
    grad_mixed_t, log_total, center, start, grad_middle, mask, w_qkv, gain, shift, dw_out, vec,
):
    n, rows, keys = plan.clips, plan.rows, plan.keys
    wide_cut, cut = Cut(plan, 2 * FF), Cut(plan, 4 * D)
    dma = pltpu.SemaphoreType.DMA
    vec_shape = (VEC_ROWS, D)
    block = min(512, rows)
    blocks = (n, plan.block_rows, D)
    shared = pltpu.VMEM((plan.share, rows, D), BF16)
    pane = pltpu.VMEM((block, rows), F32)
    return pl.pallas_call(
        functools.partial(back_kernel, plan, wide_cut, cut),
        out_shape=[
            jax.ShapeDtypeStruct(blocks, BF16),
            jax.ShapeDtypeStruct(blocks, BF16),
            jax.ShapeDtypeStruct((wide_cut.rows, D), BF16),
            jax.ShapeDtypeStruct((cut.rows, D), BF16),
            jax.ShapeDtypeStruct(vec_shape, F32),
        ],
        in_specs=[pl.BlockSpec(memory_space=pltpu.SMEM)] + [ANY] * 2 + [VMEM] * 16,
        out_specs=[ANY] * 4 + [VMEM],
        scratch_shapes=[
            pltpu.VMEM((D, keys), BF16), pane, pane, pane, pane, pltpu.VMEM((D, rows), F32),
            shared, shared, shared, shared,
            pltpu.VMEM((rows, D), F32),
            pltpu.VMEM((rows, D), F32),
            pltpu.VMEM((cut.rows, D), F32),
            pltpu.VMEM(blocks, BF16),
            pltpu.VMEM(vec_shape, F32),
            pltpu.VMEM(vec_shape, F32),
            pltpu.VMEM((cut.n_plane,) + vec_shape, F32),
            pltpu.VMEM((cut.n_depth,) + vec_shape, F32),
            *wide_cut.buffers(), *cut.buffers(), *wide_cut.semaphores(), *cut.semaphores(),
            dma((n,)), dma((n,)), dma((2, plan.share)), dma((2, plan.share)), dma((n,)), dma((n,)),
            dma((4,)), dma((2,)), dma((2, cut.n_plane)), dma((2, cut.n_depth)),
        ],
        compiler_params=pltpu.CompilerParams(
            collective_id=1, has_side_effects=True, vmem_limit_bytes=VMEM_LIMIT
        ),
        name="back",
    )(
        lengths, block_out, payload, queries, queries_t, key_rows, value_rows, grad_mixed,
        grad_mixed_t, log_total, center, start, grad_middle, mask, w_qkv, gain, shift, dw_out, vec,
    )


def unpack_kernel(plan, place, reduced, wide, vec, *outs):
    w_qkv, w_out, w_up, w_down, bias_up, soft = outs[:6]
    step = pl.program_id(0)
    w_down[...] = wide[0, 0].astype(F32)
    w_up[...] = wide[1, 0].astype(F32)

    @pl.when(step < 3)
    def _():
        w_qkv[...] = reduced[0].astype(F32)

    @pl.when(step == 3)
    def _():
        w_out[...] = reduced[0].astype(F32)
        for i, out in enumerate(outs[6:]):
            out[...] = vec[i, :]
        for i in range(FF // D):
            bias_up[i * D : (i + 1) * D] = vec[9 + i, :]
        scores = vec[13:14, :]
        lane = lax.broadcasted_iota(jnp.int32, (plan.clips, D), 1)
        slot = place[2] * 2 * plan.clips + lax.broadcasted_iota(jnp.int32, (plan.clips, D), 0)
        hits = jnp.sum(jnp.where(lane == slot, scores, 0.0), axis=1, keepdims=True)
        counts = jnp.sum(jnp.where(lane == slot + plan.clips, scores, 0.0), axis=1, keepdims=True)
        soft[...] = hits / jnp.maximum(counts, 1.0)


def unpack(plan, place, reduced, wide, vec):
    vector = jax.ShapeDtypeStruct((D,), F32)

    def full(shape):
        return pl.BlockSpec(shape, lambda i, s: (0,) * len(shape))

    return pl.pallas_call(
        functools.partial(unpack_kernel, plan),
        grid_spec=pltpu.PrefetchScalarGridSpec(
            num_scalar_prefetch=1,
            grid=(4,),
            in_specs=[
                pl.BlockSpec((1, D, D), lambda i, s: (i, 0, 0)),
                pl.BlockSpec((2, 1, D, D), lambda i, s: (0, i, 0, 0)),
                full((VEC_ROWS, D)),
            ],
            out_specs=[
                pl.BlockSpec((D, D), lambda i, s: (0, jnp.minimum(i, 2))),
                full((D, D)),
                pl.BlockSpec((D, D), lambda i, s: (0, i)),
                pl.BlockSpec((D, D), lambda i, s: (i, 0)),
                full((FF,)),
                full((plan.clips, 1)),
            ]
            + [full((D,))] * 9,
        ),
        out_shape=[
            jax.ShapeDtypeStruct((D, 3 * D), F32),
            jax.ShapeDtypeStruct((D, D), F32),
            jax.ShapeDtypeStruct((D, FF), F32),
            jax.ShapeDtypeStruct((FF, D), F32),
            jax.ShapeDtypeStruct((FF,), F32),
            jax.ShapeDtypeStruct((plan.clips, 1), F32),
        ]
        + [vector] * 9,
        compiler_params=pltpu.CompilerParams(vmem_limit_bytes=VMEM_LIMIT),
        name="unpack",
    )(place, reduced.reshape(4, D, D), wide.reshape(2, FF // D, D, D), vec)


def per_device(
    plan,
    patches, patch_mask, clip_lengths, target_index, targets, out_grad,
    mask_embed, ln1_gain, ln1_shift, w_qkv, bias_q, bias_v, w_out, bias_out,
    ln2_gain, ln2_shift, w_up, bias_up, w_down, bias_down,
):
    n, rows, block_rows = plan.clips, plan.rows, plan.block_rows
    clip, part = plan.place()
    length = lax.dynamic_index_in_dim(clip_lengths, clip, keepdims=False)
    place = jnp.stack([clip, length, lax.axis_index("batch"), part]).astype(jnp.int32)
    (start, queries, queries_t, key_rows, value_rows, mixed, log_total, mask, target, grad) = front(
        plan, clip_lengths, patches.reshape(n, block_rows, D), patch_mask, target_index,
        out_grad.reshape(n, block_rows, D), mask_embed, ln1_gain, ln1_shift, w_qkv, bias_q, bias_v,
    )
    start = start.reshape(rows, D)
    queries = queries.reshape(rows, D)
    grad = grad.reshape(rows, D)
    block_out, grad_middle, grad_mixed, grad_mixed_t, center, payload, grad_w_out, vec = (
        feed_forward(
            plan, place, mixed, start, grad, mask, target, targets, w_out, bias_out,
            ln2_gain, ln2_shift, w_up, bias_up, w_down, bias_down,
        )
    )
    block_grid, input_grad, wide, reduced, vec = back(
        plan, clip_lengths, block_out.reshape(n, block_rows, D), payload.reshape(2 * FF, D),
        queries, queries_t, key_rows, value_rows, grad_mixed, grad_mixed_t, log_total, center,
        start, grad_middle, mask, w_qkv, ln1_gain, ln1_shift, grad_w_out, vec,
    )
    grad_w_qkv, grad_w_out, grad_w_up, grad_w_down, grad_bias_up, soft, *vectors = unpack(
        plan, place, reduced, wide, vec
    )
    block_grid = block_grid.reshape(patches.shape)
    (grad_mask_embed, grad_ln1_gain, grad_ln1_shift, grad_bias_q, grad_bias_v, grad_bias_out,
     grad_ln2_gain, grad_ln2_shift, grad_bias_down) = vectors
    return (
        block_grid, input_grad.reshape(patches.shape), grad_mask_embed, grad_ln1_gain,
        grad_ln1_shift, grad_w_qkv, grad_bias_q, grad_bias_v, grad_w_out, grad_bias_out,
        grad_ln2_gain, grad_ln2_shift, grad_w_up, grad_bias_up, grad_w_down, grad_bias_down,
        soft.reshape(n),
    )


def solution(mesh):
    rows = P("batch", "freq", "tm", None)
    whole = P()
    in_specs = (
        rows, P("batch", "freq", "tm"), P("batch"), P("batch", "freq", "tm"),
        P("batch", None, None), rows,
    ) + (whole,) * 14
    out_specs = (rows, rows) + (whole,) * 14 + (P("batch"),)

    def body(*args):
        return per_device(Plan(mesh, args[0]), *args)

    return jax.shard_map(
        body, mesh=mesh, in_specs=in_specs, out_specs=out_specs, check_vma=False
    )
```

```python
import functools

import jax
import jax.numpy as jnp
from jax import lax
from jax.experimental import pallas as pl
from jax.experimental.pallas import tpu as pltpu
from jax.sharding import PartitionSpec as P

D = 384
FF = 1536
HEADS = 6
HEAD_DIM = 64
PAIRS = HEADS // 2
PAIR = 2 * HEAD_DIM
SCALE = HEAD_DIM ** (-0.5)
DEAD = -1e9
EPS = 1e-06
VEC_ROWS = 16
LANES = 128
CHUNK = 512
TILE = 512
GRID_AT = (0, 1, 2, 4, 5, 6, 8, 9)
WAVES = (4, 6)
MESH = pl.DeviceIdType.MESH
VMEM_LIMIT = 60 * 2**20
ANY = pl.BlockSpec(memory_space=pl.ANY)
VMEM = pl.BlockSpec(memory_space=pltpu.VMEM)
BF16 = jnp.bfloat16
F32 = jnp.float32


def mm(left_mat, right_mat):
    return jnp.dot(left_mat, right_mat, preferred_element_type=F32)


def mm_nt(left_mat, right_mat):
    return lax.dot_general(
        left_mat, right_mat, (((1,), (1,)), ((), ())), preferred_element_type=F32
    )


def mm_tn(left_mat, right_mat):
    return lax.dot_general(
        left_mat, right_mat, (((0,), (0,)), ((), ())), preferred_element_type=F32
    )


def row(ref):
    return ref[...].astype(F32).reshape(1, -1)


def normalize(rows):
    center = rows - jnp.mean(rows, axis=-1, keepdims=True)
    scale = lax.rsqrt(jnp.mean(center * center, axis=-1, keepdims=True) + EPS)
    return center * scale, scale


def normalize_back(grad_hat, hat, scale):
    first = jnp.mean(grad_hat, axis=-1, keepdims=True)
    second = jnp.mean(grad_hat * hat, axis=-1, keepdims=True)
    return scale * (grad_hat - first - hat * second)


def sum_rows(rows):
    return jnp.sum(rows, axis=0, keepdims=True)


def columns(ints):
    freq_rows, time_rows = ints.shape
    shape = (time_rows, time_rows)
    eye = lax.broadcasted_iota(jnp.int32, shape, 0) == lax.broadcasted_iota(jnp.int32, shape, 1)
    parts = [
        jnp.sum(jnp.where(eye, ints[f : f + 1, :], 0), axis=1, keepdims=True)
        for f in range(freq_rows)
    ]
    return jnp.concatenate(parts, axis=0)


class Plan:
    def __init__(self, mesh, patches):
        self.freq = mesh.shape["freq"]
        self.tm = mesh.shape["tm"]
        self.batch = mesh.shape["batch"]
        self.clips, self.freq_rows, self.time_rows, _ = patches.shape
        self.share = self.freq * self.tm // self.clips
        self.blocks = self.tm // self.share
        self.block_rows = self.freq_rows * self.time_rows
        self.rows = self.clips * self.block_rows
        self.keys = self.share * self.rows
        assert self.freq * self.blocks == self.clips and self.blocks * self.share == self.tm

    def place(self):
        time_id = lax.axis_index("tm")
        return lax.axis_index("freq") * self.blocks + time_id // self.share, time_id % self.share

    def member(self, member, part):
        return {
            "freq": member // self.blocks,
            "tm": (member % self.blocks) * self.share + part,
        }

    def sharer(self, part):
        time_id = lax.axis_index("tm")
        return {"tm": time_id // self.share * self.share + part}

    def key_time(self, place):
        part = place // self.rows
        block = (place // self.block_rows) % self.clips % self.blocks
        return (block * self.share + part) * self.time_rows + place % self.time_rows


def greet(devices):
    barrier = pltpu.get_barrier_semaphore()
    for device in devices:
        pl.semaphore_signal(barrier, inc=1, device_id=device, device_id_type=MESH)
    pl.semaphore_wait(barrier, len(devices))


def remote(src, dst, send_sem, recv_sem, device):
    return pltpu.make_async_remote_copy(
        src_ref=src, dst_ref=dst, send_sem=send_sem, recv_sem=recv_sem,
        device_id=device, device_id_type=MESH,
    )


def front_kernel(
    plan, lengths, patches, mask, target, out_grad, embed, gain, shift, w_ref, bias_q, bias_v,
    start_out, q_out, qt_out, k_out, v_out, mixed_out, total_out, mask_out, target_out, grad_out,
    taken, mask_in, target_in, start_buf, q_buf, qt_buf, kv_buf, k_buf, v_buf, vt_buf,
    mixed_buf, total_buf, score_a, score_b,
    send_sem, recv_sem, local_sem, kv_send, kv_recv, grad_send, grad_recv, out_sem,
):
    me, part = plan.place()
    n, rows, keys, block_rows = plan.clips, plan.rows, plan.keys, plan.block_rows
    peers = [lax.rem(me + step, n) for step in range(n)]
    sharers = [lax.rem(part + step, plan.share) for step in range(plan.share)]
    greet(
        [plan.member(peers[step], part) for step in range(1, n)]
        + [plan.sharer(sharers[step]) for step in range(1, plan.share)]
    )
    streams = ((mask, mask_in), (target, target_in), (patches, taken))
    arrivals = []
    for step in range(n):
        copies = []
        for i, (src, dst) in enumerate(streams):
            if step == 0:
                copy = pltpu.make_async_copy(src.at[me], dst.at[me], local_sem.at[i])
            else:
                copy = remote(
                    src.at[peers[step]], dst.at[me], send_sem.at[i, step], recv_sem.at[i, step],
                    plan.member(peers[step], part),
                )
            copy.start()
            copies.append(copy)
        arrivals.append(copies)
    gain_row, shift_row, embed_row = row(gain), row(shift), row(embed)
    bias_q_row, bias_v_row = row(bias_q), row(bias_v)
    waits, shared = [], []

    def save(index, src, dst):
        copy = pltpu.make_async_copy(src, dst, out_sem.at[index])
        copy.start()
        waits.append(copy)

    for step in range(n):
        source = lax.rem(me + n - step, n)
        for copy in arrivals[step]:
            if step == 0:
                copy.wait()
            else:
                copy.wait_recv()
        masked = columns(mask_in[source]) == 1
        start = jnp.where(masked, embed_row, taken[source].astype(F32))
        start_buf[source] = start.astype(BF16)
        hat, _ = normalize(start)
        normed = (hat * gain_row + shift_row).astype(BF16)
        project = mm(normed, w_ref[...])
        queries = (project[:, :D] + bias_q_row).astype(BF16)
        q_buf[source] = (queries.astype(F32) * SCALE).astype(BF16)
        kv_buf[part, source, :, :D] = project[:, D : 2 * D].astype(BF16)
        kv_buf[part, source, :, D:] = (project[:, 2 * D :] + bias_v_row).astype(BF16)
        for other in range(1, plan.share):
            copy = remote(
                kv_buf.at[part, source], kv_buf.at[part, source], kv_send.at[other, step],
                kv_recv.at[other, step], plan.sharer(sharers[other]),
            )
            copy.start()
            shared.append(copy)
    for step in range(n):
        if step == 0:
            copy = pltpu.make_async_copy(out_grad.at[me], grad_out.at[me], local_sem.at[0])
        else:
            copy = remote(
                out_grad.at[peers[step]], grad_out.at[me], grad_send.at[step], grad_recv.at[step],
                plan.member(peers[step], part),
            )
        copy.start()
        waits.append(copy)
    save(0, start_buf, start_out)
    save(1, q_buf, q_out)
    save(2, mask_in, mask_out)
    save(3, target_in, target_out)
    for i in range(n):
        at = slice(i * block_rows, (i + 1) * block_rows)
        qt_buf[:, at] = q_buf[i].T
    save(4, qt_buf, qt_out)
    for copy in shared:
        copy.wait()
    length = lengths[me]
    first = kv_buf[0, 0, 0:1, :D]
    for i in range(plan.share):
        for b in range(n):
            begin = i * rows + b * block_rows
            at = slice(begin, begin + block_rows)
            ids = lax.broadcasted_iota(jnp.int32, (block_rows, 1), 0) + begin
            live = plan.key_time(ids) < length
            k_buf[at, :] = jnp.where(live, kv_buf[i, b, :, :D], first)
            value = kv_buf[i, b, :, D:]
            value = jnp.where(live, value, jnp.zeros_like(value))
            v_buf[at, :] = value
            turned = value.T
            ids = lax.broadcasted_iota(jnp.int32, (16, block_rows), 1) + begin
            top = lax.broadcasted_iota(jnp.int32, (16, block_rows), 0) == 0
            count = jnp.where((plan.key_time(ids) < length) & top, 1.0, 0.0).astype(BF16)
            for h in range(HEADS):
                vt_buf[h, :HEAD_DIM, at] = turned[h * HEAD_DIM : (h + 1) * HEAD_DIM, :]
                vt_buf[h, HEAD_DIM:, at] = count
    save(5, k_buf, k_out)
    save(6, v_buf, v_out)

    width = score_a.shape[1]
    spans = rows // width
    items = HEADS * spans
    lane = lax.broadcasted_iota(jnp.int32, (1, PAIR), 1)

    def score(item, buf):
        head, span = item // spans, item % spans
        pair = pl.ds(pl.multiple_of(head // 2 * PAIR, PAIR), PAIR)
        at = pl.ds(pl.multiple_of(span * width, width), width)
        k_own = jnp.where(lane // HEAD_DIM == head % 2, k_buf[:, pair], jnp.zeros((), BF16))
        scores = mm(k_own, qt_buf[pair, at])
        buf[...] = scores
        return jnp.max(scores, axis=0, keepdims=True)

    def blend(item, buf, top):
        head, span = item // spans, item % spans
        at = pl.ds(pl.multiple_of(span * width, width), width)
        raised = jnp.exp(buf[...] - top).astype(BF16)
        out = mm(vt_buf[head], raised)
        row_total = out[HEAD_DIM : HEAD_DIM + 1, :]
        into = pl.ds(pl.multiple_of(head * HEAD_DIM, HEAD_DIM), HEAD_DIM)
        mixed_buf[into, at] = (out[:HEAD_DIM, :] / row_total).astype(BF16)
        total_buf[head, :, at] = top + jnp.log(row_total)

    def two(i, top_a):
        top_b = score(2 * i + 1, score_b)
        blend(2 * i, score_a, top_a)
        top_a = score(2 * i + 2, score_a)
        blend(2 * i + 1, score_b, top_b)
        return top_a

    top_a = lax.fori_loop(0, items // 2 - 1, two, score(0, score_a))
    top_b = score(items - 1, score_b)
    blend(items - 2, score_a, top_a)
    blend(items - 1, score_b, top_b)
    save(7, mixed_buf, mixed_out)
    save(8, total_buf, total_out)
    for step in range(1, n):
        for copy in arrivals[step]:
            copy.wait_send()
    for copy in waits:
        copy.wait()


def front(plan, lengths, patches, mask, target, out_grad, embed, gain, shift, w_qkv, bias_q, bias_v):
    n, rows, keys, block_rows = plan.clips, plan.rows, plan.keys, plan.block_rows
    width = min(512, rows)
    assert HEADS * (rows // width) % 2 == 0
    dma = pltpu.SemaphoreType.DMA
    blocks = (n, block_rows, D)
    total = (HEADS, 1, rows)
    shapes = [
        (blocks, BF16), (blocks, BF16), ((D, rows), BF16), ((keys, D), BF16), ((keys, D), BF16),
        ((D, rows), BF16), (total, F32), (mask.shape, jnp.int32), (mask.shape, jnp.int32),
        (blocks, BF16),
    ]
    return pl.pallas_call(
        functools.partial(front_kernel, plan),
        out_shape=[jax.ShapeDtypeStruct(shape, kind) for shape, kind in shapes],
        in_specs=[pl.BlockSpec(memory_space=pltpu.SMEM)] + [ANY] * 4 + [VMEM] * 6,
        out_specs=[ANY] * 10,
        scratch_shapes=[
            pltpu.VMEM(blocks, BF16),
            pltpu.VMEM(mask.shape, jnp.int32),
            pltpu.VMEM(mask.shape, jnp.int32),
            pltpu.VMEM(blocks, BF16),
            pltpu.VMEM(blocks, BF16),
            pltpu.VMEM((D, rows), BF16),
            pltpu.VMEM((plan.share, n, block_rows, 2 * D), BF16),
            pltpu.VMEM((keys, D), BF16),
            pltpu.VMEM((keys, D), BF16),
            pltpu.VMEM((HEADS, HEAD_DIM + 16, keys), BF16),
            pltpu.VMEM((D, rows), BF16),
            pltpu.VMEM(total, F32),
            pltpu.VMEM((keys, width), F32),
            pltpu.VMEM((keys, width), F32),
            dma((3, n)), dma((3, n)), dma((3,)),
            dma((plan.share, n)), dma((plan.share, n)), dma((n,)), dma((n,)), dma((9,)),
        ],
        compiler_params=pltpu.CompilerParams(
            collective_id=0, has_side_effects=True, vmem_limit_bytes=VMEM_LIMIT
        ),
        name="front",
    )(lengths, patches, mask, target, out_grad, embed, gain, shift, w_qkv, bias_q, bias_v)


def gelu_parts(rows):
    lower = 0.5 * (1.0 + lax.erf(rows * 0.7071067811865476))
    slope = lower + rows * (jnp.exp(-0.5 * rows * rows) * 0.3989422804014327)
    return rows * lower, slope


class Ring:
    def __init__(self, cut, at, half_src, own_half, core_in, mine, plane_in, part_buf, depth_in, total, sems):
        self.cut, self.at = cut, at
        self.half_src, self.own_half, self.core_in, self.mine = half_src, own_half, core_in, mine
        self.plane_in, self.part_buf, self.depth_in, self.total = plane_in, part_buf, depth_in, total
        self.core_sem, self.plane_sem, self.depth_sem, self.up_sem, self.wide_sem = sems

    def core_copy(self):
        return remote(
            self.half_src, self.core_in, self.core_sem.at[0], self.core_sem.at[1], self.at.partner
        )

    def plane_copies(self):
        chunk = self.cut.chunk
        return [
            remote(
                self.mine.at[spot(self.at.planes[k] * chunk, chunk)], self.plane_in.at[k],
                self.plane_sem.at[0, k], self.plane_sem.at[1, k], self.at.in_plane[k],
            )
            for k in range(1, self.cut.n_plane)
        ]

    def depth_copies(self):
        piece, copies = self.cut.piece, []
        for k in range(1, self.cut.n_depth):
            if self.cut.scatter:
                src = self.part_buf.at[spot(self.at.depths[k] * piece, piece)]
                dst = self.depth_in.at[k]
            else:
                src = dst = self.depth_in.at[self.at.depth]
            copies.append(
                remote(
                    src, dst, self.depth_sem.at[0, k], self.depth_sem.at[1, k], self.at.in_depth[k]
                )
            )
        return copies

    def same(self, first, count, sems, k, device):
        own = spot(first, count)
        return remote(self.total.at[own], self.total.at[own], sems.at[0, k], sems.at[1, k], device)

    def home(self):
        return self.at.core * self.cut.half + self.at.plane * self.cut.chunk

    def up_copies(self):
        first = self.home() + self.at.depth * self.cut.piece
        return [
            self.same(first, self.cut.piece, self.up_sem, k, self.at.in_depth[k])
            for k in range(1, self.cut.n_depth)
        ]

    def wide_copies(self):
        return [
            self.same(self.home(), self.cut.chunk, self.wide_sem, k, self.at.in_plane[k])
            for k in range(1, self.cut.n_plane)
        ]

    def last_copy(self):
        own = spot(self.at.core * self.cut.half, self.cut.half)
        return remote(
            self.total.at[own], self.total.at[own], self.core_sem.at[2], self.core_sem.at[3],
            self.at.partner,
        )

    def begin(self):
        self.core_copy().start()

    def to_plane(self):
        self.core_copy().wait()
        own = self.own_half[...].astype(F32) + self.core_in[...].astype(F32)
        self.mine[...] = own.astype(BF16)
        for copy in self.plane_copies():
            copy.start()

    def to_depth(self):
        chunk = self.cut.chunk
        mine = self.mine[spot(self.at.plane * chunk, chunk), :].astype(F32)
        for k, copy in enumerate(self.plane_copies()):
            copy.wait()
            mine = mine + self.plane_in[k + 1].astype(F32)
        if self.cut.scatter:
            self.part_buf[...] = mine.astype(BF16)
        else:
            self.depth_in[self.at.depth] = mine.astype(BF16)
        for copy in self.depth_copies():
            copy.start()

    def back_up(self):
        piece, copies = self.cut.piece, self.depth_copies()
        if self.cut.scatter:
            mine = self.part_buf[spot(self.at.depth * piece, piece), :].astype(F32)
            for k, copy in enumerate(copies):
                copy.wait()
                mine = mine + self.depth_in[k + 1].astype(F32)
            self.total[spot(self.home() + self.at.depth * piece, piece), :] = mine.astype(BF16)
            for copy in self.up_copies():
                copy.start()
        else:
            for copy in copies:
                copy.wait()
            mine = self.depth_in[0].astype(F32)
            for k in range(1, self.cut.n_depth):
                mine = mine + self.depth_in[k].astype(F32)
            self.total[spot(self.home(), self.cut.chunk), :] = mine.astype(BF16)

    def back_wide(self):
        if self.cut.scatter:
            for copy in self.up_copies():
                copy.wait()
        for copy in self.wide_copies():
            copy.start()

    def back_core(self):
        for copy in self.wide_copies():
            copy.wait()
        self.last_copy().start()

    def turn(self):
        self.to_depth()
        self.back_up()
        self.back_wide()

    def end(self):
        self.last_copy().wait()


class Cut:
    def __init__(self, plan, rows, width, flat=False):
        self.rows, self.width = rows, width
        self.n_plane = plan.freq * plan.batch
        self.n_depth = plan.tm // 2
        self.flat = flat and rows // 2 % (16 * self.n_plane * self.n_depth) == 0
        if self.flat:
            self.n_plane, self.n_depth = self.n_plane * self.n_depth, 1
        self.half = rows // 2
        self.chunk = self.half // self.n_plane
        self.piece = self.chunk // self.n_depth
        self.scatter = self.piece % 16 == 0 and self.piece * self.n_depth == self.chunk
        assert self.chunk * self.n_plane == self.half and self.chunk % 16 == 0

    def buffers(self):
        depth = self.piece if self.scatter else self.chunk
        shapes = [
            (self.half,), (self.half,), (self.n_plane, self.chunk), (self.chunk,),
            (self.n_depth, depth), (self.rows,),
        ]
        return [pltpu.VMEM(shape + (self.width,), BF16) for shape in shapes]

    def semaphores(self):
        dma = pltpu.SemaphoreType.DMA
        return [
            dma((4,)), dma((2, self.n_plane)), dma((2, self.n_depth)), dma((2, self.n_depth)),
            dma((2, self.n_plane)),
        ]


class Place:
    def __init__(self, plan):
        time_id = lax.axis_index("tm")
        n_plane, n_depth = plan.freq * plan.batch, plan.tm // 2
        self.core, self.depth = time_id % 2, time_id // 2
        self.plane = lax.axis_index("freq") * plan.batch + lax.axis_index("batch")
        self.partner = {"tm": time_id + 1 - 2 * self.core}
        self.planes = [lax.rem(self.plane + k, n_plane) for k in range(n_plane)]
        self.depths = [lax.rem(self.depth + k, n_depth) for k in range(n_depth)]
        self.in_plane = [{"freq": v // plan.batch, "batch": v % plan.batch} for v in self.planes]
        self.in_depth = [{"tm": v * 2 + self.core} for v in self.depths]


class Flat:
    def __init__(self, plan, place):
        n_depth = plan.tm // 2
        count = plan.freq * plan.batch * n_depth
        self.core, self.partner, self.depth, self.in_depth = place.core, place.partner, 0, [None]
        self.plane = place.plane * n_depth + place.depth
        self.planes = [lax.rem(self.plane + k, count) for k in range(count)]
        self.in_plane = [
            {
                "freq": v // n_depth // plan.batch,
                "batch": v // n_depth % plan.batch,
                "tm": v % n_depth * 2 + place.core,
            }
            for v in self.planes
        ]


def spot(first, count):
    return pl.ds(pl.multiple_of(first, 16), count)


def rest_kernel(
    plan, wide_cut, small_cuts, lengths,
    mixed_in, start_in, grad_in, targets_in, w_out_in, w_up_in, w_down_in, w_qkv_in,
    q_in, qt_in, k_in, v_in, log_total, mask, target,
    ln1_gain, ln1_shift, bias_out, ln2_gain, ln2_shift, bias_up, bias_down,
    block_grid, input_grad, wide_out, small_out, vec_out,
    mixed, start, grad, targets, w_out, w_up, w_down, w_qkv, q_ref, qt_ref, k_ref, v_ref,
    middle, second, down_sum, second_sum, act_buf, up_buf, payload, small_pay, do_ref, dot_ref,
    center, block_out,
    kt_buf, score_a, score_b, prob_a, prob_b, dqt_sum, dk_all, dv_all, dk_in, dv_in,
    rows_buf, vec_buf, vec_core, vec_plane, vec_depth,
    load_sem, grid_ss, grid_rs, kv_ss, kv_rs, rows_ss, rows_rs, local_sem, out_sem,
    vec_core_sem, vec_plane_sem, vec_depth_sem,
    *rest,
):
    n, rows, keys, block_rows = plan.clips, plan.rows, plan.keys, plan.block_rows
    me, part = plan.place()
    at = Place(plan)
    last_cut = small_cuts[-1]
    flat = Flat(plan, at) if last_cut.flat else at
    n_plane, n_depth = wide_cut.n_plane, wide_cut.n_depth
    peers = [lax.rem(me + k, n) for k in range(n)]
    sharers = [lax.rem(part + k, plan.share) for k in range(plan.share)]
    length = lengths[me]

    loads = [
        pltpu.make_async_copy(src, dst, load_sem.at[i])
        for i, (src, dst) in enumerate(
            (
                (mixed_in, mixed), (w_out_in, w_out), (start_in, start), (w_up_in, w_up),
                (w_down_in, w_down), (grad_in, grad), (targets_in.at[me], targets),
                (k_in, k_ref), (qt_in, qt_ref), (v_in, v_ref), (q_in, q_ref), (w_qkv_in, w_qkv),
            )
        )
    ]
    for copy in loads:
        copy.start()
    greet(
        [plan.member(peers[k], part) for k in range(1, n)]
        + [plan.sharer(sharers[k]) for k in range(1, plan.share)]
        + [at.partner]
        + (flat.in_plane[1:] if last_cut.flat else at.in_plane[1:] + at.in_depth[1:])
    )
    steps = FF // CHUNK
    wide, small = [], []
    for i in range(steps):
        mine, rest = rest[:11], rest[11:]
        wide.append(
            Ring(
                wide_cut, at, payload.at[1 - at.core, i], payload.at[at.core, i], *mine[:6], mine[6:]
            )
        )
    for p in range(PAIRS):
        mine, rest = rest[:11], rest[11:]
        small_cut = small_cuts[p]
        away = small_pay.at[p, spot((1 - at.core) * small_cut.half, small_cut.half)]
        own = small_pay.at[p, spot(at.core * small_cut.half, small_cut.half)]
        small.append(Ring(small_cut, flat if small_cut.flat else at, away, own, *mine[:6], mine[6:]))

    tile = min(TILE, rows)
    tiles = [slice(i * tile, (i + 1) * tile) for i in range(rows // tile)]
    gain2, shift2 = row(ln2_gain), row(ln2_shift)
    bias_up_row = row(bias_up)
    vec_buf[...] = jnp.zeros_like(vec_buf)
    for copy in loads[:3]:
        copy.wait()
    for span in tiles:
        rows_in = start[span, :].astype(F32) + mm_tn(mixed[:, span], w_out[...]) + row(bias_out)
        middle[span, :] = rows_in
        hat, _ = normalize(rows_in)
        second[span, :] = (hat * gain2 + shift2).astype(BF16)
    for copy in loads[3:6]:
        copy.wait()
    up_sums = []
    for i in range(steps):
        cols = slice(i * CHUNK, (i + 1) * CHUNK)
        for t, span in enumerate(tiles):
            hidden = mm(second[span, :], w_up[:, cols]) + bias_up_row[:, cols]
            active, slope = gelu_parts(hidden)
            active = active.astype(BF16)
            act_buf[span, :] = active
            down = mm(active, w_down[cols, :])
            grad_up = (mm_nt(grad[span, :], w_down[cols, :]) * slope).astype(BF16)
            up_buf[span, :] = grad_up
            back = mm_nt(grad_up, w_up[:, cols])
            if i == 0:
                down_sum[span, :] = down
                second_sum[span, :] = back
            else:
                down_sum[span, :] += down
                second_sum[span, :] += back
            if t == 0 and i >= 1:
                wide[i - 1].to_plane()
        grad_down = mm_tn(act_buf[...], grad[...]).astype(BF16)
        for t in range(D // LANES):
            payload[0, i, t * CHUNK : (t + 1) * CHUNK, :] = grad_down[:, t * LANES : (t + 1) * LANES]
        grad_w = mm_tn(second[...], up_buf[...]).astype(BF16)
        for t in range(CHUNK // LANES):
            payload[1, i, t * D : (t + 1) * D, :] = grad_w[:, t * LANES : (t + 1) * LANES]
        up_sums.append(sum_rows(up_buf[...].astype(F32)))
        wide[i].begin()
        if i >= 2:
            wide[i - 2].to_depth()
    up_sums = jnp.concatenate(up_sums, axis=1)
    for i in range(FF // D):
        vec_buf[9 + i : 10 + i, :] = up_sums[:, i * D : (i + 1) * D]
    vec_buf[8:9, :] = sum_rows(grad[...].astype(F32))
    loads[6].wait()
    home_copies = []
    cand = lax.broadcasted_iota(jnp.int32, (1, targets.shape[0]), 1)
    total_hit = jnp.zeros((1, 1), F32)
    total_count = jnp.zeros((1, 1), F32)
    per_tile = tile // block_rows
    for t, span in enumerate(tiles):
        result = (middle[span, :] + down_sum[span, :] + row(bias_down)).astype(BF16)
        for b in range(per_tile):
            block_out[t * per_tile + b] = result[b * block_rows : (b + 1) * block_rows, :]
        hat, scale = normalize(middle[span, :])
        grad_second = second_sum[span, :]
        vec_buf[6:7, :] += sum_rows(grad_second * hat)
        vec_buf[7:8, :] += sum_rows(grad_second)
        back = grad[span, :].astype(F32) + normalize_back(grad_second * gain2, hat, scale)
        second_sum[span, :] = back
        branch = back.astype(BF16)
        up_buf[span, :D] = branch
        vec_buf[5:6, :] += sum_rows(branch.astype(F32))
        do_ref[span, :] = mm_nt(branch, w_out[...]).astype(BF16)
        down = mm_nt(w_out[...], branch).astype(BF16)
        dot_ref[:, span] = down
        product = down.astype(F32) * mixed[:, span].astype(F32)
        for h in range(HEADS):
            center[h, :, span] = sum_rows(product[h * HEAD_DIM : (h + 1) * HEAD_DIM, :])
        logits = mm_nt(result, targets[...])
        raised = jnp.exp(logits - jnp.max(logits, axis=1, keepdims=True))
        sources = range(t * per_tile, (t + 1) * per_tile)
        target_col = jnp.concatenate([columns(target[s]) for s in sources], axis=0)
        mask_col = jnp.concatenate([columns(mask[s]) for s in sources], axis=0)
        hit = jnp.sum(jnp.where(cand == target_col, raised, 0.0), axis=1, keepdims=True)
        hit = hit / jnp.sum(raised, axis=1, keepdims=True)
        ids = lax.broadcasted_iota(jnp.int32, (tile, 1), 0) + t * tile + part * rows
        counted = jnp.where((plan.key_time(ids) < length) & (mask_col == 1), 1.0, 0.0)
        total_hit += sum_rows(hit * counted)
        total_count += sum_rows(counted)
        if t == 0:
            wide[-1].to_plane()
    home_copies.append(
        pltpu.make_async_copy(block_out.at[me], block_grid.at[me], local_sem.at[0])
    )
    for k in range(1, n):
        home_copies.append(
            remote(
                block_out.at[peers[k]], block_grid.at[me], grid_ss.at[k], grid_rs.at[k],
                plan.member(peers[k], part),
            )
        )
    home_copies[0].start()
    wide[-3].back_up()
    wide[-2].to_depth()
    grad_w = mm(mixed[...], up_buf[:, :D]).astype(BF16)
    for p in range(PAIRS):
        small_pay[p, D:, :] = grad_w[p * PAIR : (p + 1) * PAIR, :]
    lane = lax.broadcasted_iota(jnp.int32, (1, D), 1)
    slot = lax.axis_index("batch") * 2 * n + me
    scores = jnp.where(lane == slot, total_hit, 0.0)
    vec_buf[13:14, :] = scores + jnp.where(lane == slot + n, total_count, 0.0)

    gain1, shift1 = row(ln1_gain), row(ln1_shift)
    hat_buf, normed, grad_buf, grad_middle = middle, second, down_sum, second_sum
    for span in tiles:
        hat, _ = normalize(start[span, :].astype(F32))
        hat_buf[span, :] = hat
        normed[span, :] = (hat * gain1 + shift1).astype(BF16)
    loads[7].wait()
    for i in range(keys // 256):
        span = slice(i * 256, (i + 1) * 256)
        ids = lax.broadcasted_iota(jnp.int32, (1, 256), 1) + i * 256
        turned = k_ref[span, :].T
        kt_buf[:, span] = jnp.where(plan.key_time(ids) < length, turned, jnp.zeros_like(turned))
    dqt_sum[...] = jnp.zeros_like(dqt_sum)
    for copy in loads[8:]:
        copy.wait()

    block = score_a.shape[0]
    per_part = rows // block
    lane = lax.broadcasted_iota(jnp.int32, (1, PAIR), 1)
    owns = [lane // HEAD_DIM == e for e in range(2)]
    zero = jnp.zeros((), BF16)
    per_pair = per_part * plan.share
    bodies = PAIRS * per_pair

    def kv_copies(p):
        return [
            remote(
                src.at[p, sharers[k]], dst.at[p, k], kv_ss.at[i, p, k], kv_rs.at[i, p, k],
                plan.sharer(sharers[k]),
            )
            for i, (src, dst) in enumerate(((dk_all, dk_in), (dv_all, dv_in)))
            for k in range(1, plan.share)
        ]

    def send_keys(p):
        for copy in kv_copies(p):
            copy.start()

    def finish_pair(p):
        for copy in kv_copies(p):
            copy.wait()
        cols = slice(p * PAIR, (p + 1) * PAIR)
        parts = [(dqt_sum[cols, :] * SCALE).T.astype(BF16)]
        ids = lax.broadcasted_iota(jnp.int32, (rows, 1), 0) + part * rows
        live = plan.key_time(ids) < length
        for own, buf in ((dk_all, dk_in), (dv_all, dv_in)):
            summed = own[p, part].astype(F32)
            for k in range(1, plan.share):
                summed = summed + buf[p, k].astype(F32)
            parts.append(jnp.where(live, summed, 0.0).astype(BF16))
        vec_buf[3:4, cols] = sum_rows(parts[0].astype(F32))
        vec_buf[4:5, cols] = sum_rows(parts[2].astype(F32))
        project = jnp.concatenate(parts, axis=1)
        small_pay[p, :D, :] = mm_tn(normed[...], project).astype(BF16)
        small[p].begin()
        weights = [w_qkv[:, i * D + p * PAIR : i * D + (p + 1) * PAIR] for i in range(3)]
        back = mm_nt(project, jnp.concatenate(weights, axis=1))
        if p == 0:
            grad_buf[...] = back
        else:
            grad_buf[...] += back

    def save(i, src, dst):
        return pltpu.make_async_copy(src, dst, out_sem.at[i])

    saves = [save(i, wide[i].total, wide_out.at[i]) for i in range(steps)]
    saves += [save(steps + p, small[p].total, small_out.at[p]) for p in range(PAIRS)]

    def wide_end(i):
        wide[i].end()
        saves[i].start()

    def small_end(p):
        small[p].end()
        saves[steps + p].start()

    last_other = per_pair - per_part - 1
    events = [
        (last_other + p * per_pair, functools.partial(send_keys, p)) for p in range(PAIRS)
    ] + [(p * per_pair + per_pair - 1, functools.partial(finish_pair, p)) for p in range(PAIRS - 1)]
    for when, event in (
        (0, wide[0].back_wide), (0, wide[2].to_depth), (1, wide[1].back_up), (2, wide[2].back_up),
        (3, wide[1].back_wide), (3, wide[0].back_core), (4, small[0].to_plane),
        (4, wide[2].back_wide), (4, functools.partial(wide_end, 0)), (6, wide[1].back_core),
        (6, small[0].to_depth), (7, wide[2].back_core), (7, functools.partial(wide_end, 1)),
        (8, small[0].back_up), (8, small[1].to_plane), (8, functools.partial(wide_end, 2)),
        (10, small[0].back_wide), (10, small[1].to_depth),
    ):
        events.append((when * bodies // 12, event))
    for k in range(1, n):
        events.append((GRID_AT[k % len(GRID_AT)] * bodies // 12, home_copies[k].start))

    def body(i, carry):
        pair, order = i // per_pair, i % per_pair
        owner = lax.rem(part + 1 + order // per_part, plan.share)
        begin = order % per_part * block
        span = pl.ds(pl.multiple_of(owner * rows + begin, block), block)
        inside = pl.ds(pl.multiple_of(begin, block), block)
        cols = pl.ds(pl.multiple_of(pair * PAIR, PAIR), PAIR)
        for e, (score_buf, prob_buf) in enumerate(((score_a, prob_a), (score_b, prob_b))):
            score_buf[...] = mm(jnp.where(owns[e], k_ref[span, cols], zero), qt_ref[cols, :])
            prob_buf[...] = mm(jnp.where(owns[e], v_ref[span, cols], zero), dot_ref[cols, :])
        grad_k, grad_v = [], []
        for e, (score_buf, prob_buf) in enumerate(((score_a, prob_a), (score_b, prob_b))):
            head = pl.ds(pl.multiple_of(pair * PAIR + e * HEAD_DIM, HEAD_DIM), HEAD_DIM)
            prob = jnp.exp(score_buf[...] - log_total[2 * pair + e])
            grad_scores = (prob * (prob_buf[...] - center[2 * pair + e])).astype(BF16)
            grad_v.append(mm(prob.astype(BF16), jnp.where(owns[e], do_ref[:, cols], zero)))
            grad_k.append(mm(grad_scores, jnp.where(owns[e], q_ref[:, cols], zero)))
            dqt_sum[head, :] += mm(kt_buf[head, span], grad_scores)
        dk_all[pair, owner, inside, :] = (grad_k[0] + grad_k[1]).astype(BF16)
        dv_all[pair, owner, inside, :] = (grad_v[0] + grad_v[1]).astype(BF16)
        for when, event in events:
            pl.when(i == when)(event)
        return carry

    lax.fori_loop(0, bodies, body, 0)
    finish_pair(PAIRS - 1)

    row_copies = []
    grad_embed = jnp.zeros((1, D), F32)
    grad_gain = jnp.zeros((1, D), F32)
    grad_shift = jnp.zeros((1, D), F32)
    for k in range(n):
        owner = peers[k]
        span = spot(owner * block_rows, block_rows)
        _, scale = normalize(start[span, :].astype(F32))
        hat = hat_buf[span, :]
        grad_normed = grad_buf[span, :]
        grad_gain += sum_rows(grad_normed * hat)
        grad_shift += sum_rows(grad_normed)
        grad_start = grad_middle[span, :] + normalize_back(grad_normed * gain1, hat, scale)
        masked = columns(mask[owner]) == 1
        grad_embed += sum_rows(jnp.where(masked, grad_start, 0.0))
        rows_buf[owner] = jnp.where(masked, 0.0, grad_start).astype(BF16)
        if k == 0:
            copy = pltpu.make_async_copy(rows_buf.at[owner], input_grad.at[me], local_sem.at[1])
        else:
            copy = remote(
                rows_buf.at[owner], input_grad.at[me], rows_ss.at[k], rows_rs.at[k],
                plan.member(owner, part),
            )
        row_copies.append(copy)
        if k < WAVES[0]:
            copy.start()
        if k == 1:
            small[2].to_plane()
        if k == 3:
            small[1].back_up()
        if k == 5:
            small[0].back_core()
    vec_buf[0:1, :] = grad_embed
    vec_buf[1:2, :] = grad_gain
    vec_buf[2:3, :] = grad_shift
    vec_copy = remote(vec_buf, vec_core, vec_core_sem.at[0], vec_core_sem.at[1], at.partner)
    vec_copy.start()
    vec_copy.wait()
    vec_plane[at.plane] = vec_buf[...] + vec_core[...]
    vec_plane_copies = []
    for k in range(1, n_plane):
        copy = remote(
            vec_plane.at[at.plane], vec_plane.at[at.plane], vec_plane_sem.at[0, k],
            vec_plane_sem.at[1, k], at.in_plane[k],
        )
        copy.start()
        vec_plane_copies.append(copy)
    small[2].turn()
    small[1].back_wide()
    for copy in row_copies[WAVES[0] : WAVES[1]]:
        copy.start()
    small_end(0)
    for copy in vec_plane_copies:
        copy.wait()
    summed = vec_plane[0]
    for k in range(1, n_plane):
        summed = summed + vec_plane[k]
    vec_depth[at.depth] = summed
    vec_depth_copies = []
    for k in range(1, n_depth):
        copy = remote(
            vec_depth.at[at.depth], vec_depth.at[at.depth], vec_depth_sem.at[0, k],
            vec_depth_sem.at[1, k], at.in_depth[k],
        )
        copy.start()
        vec_depth_copies.append(copy)
    for copy in row_copies[WAVES[1] :]:
        copy.start()
    small[1].back_core()
    small[2].back_core()
    small_end(1)
    for copy in vec_depth_copies:
        copy.wait()
    summed = vec_depth[0]
    for k in range(1, n_depth):
        summed = summed + vec_depth[k]
    vec_out[...] = summed
    small_end(2)
    for copy in row_copies + home_copies + saves:
        copy.wait()


def rest(plan, lengths, mixed, start, grad, targets, weights, q, qt, k, v, log_total, mask, target, vectors):
    n, rows, keys = plan.clips, plan.rows, plan.keys
    steps = FF // CHUNK
    wide_cut = Cut(plan, 2 * CHUNK * D // LANES, LANES)
    small_cuts = [Cut(plan, D + PAIR, D, flat=p == PAIRS - 1) for p in range(PAIRS)]
    small_cut = small_cuts[0]
    dma = pltpu.SemaphoreType.DMA
    vec_shape = (VEC_ROWS, D)
    block = min(512, rows)
    blocks = (n, plan.block_rows, D)
    shared = pltpu.VMEM((PAIRS, plan.share, rows, PAIR), BF16)
    pane = pltpu.VMEM((block, rows), F32)
    loaded = (mixed, start, grad, targets[0], *weights, q, qt, k, v)
    rings = []
    for cut in [wide_cut] * steps + small_cuts:
        rings += cut.buffers() + cut.semaphores()
    return pl.pallas_call(
        functools.partial(rest_kernel, plan, wide_cut, small_cuts),
        out_shape=[
            jax.ShapeDtypeStruct(blocks, BF16),
            jax.ShapeDtypeStruct(blocks, BF16),
            jax.ShapeDtypeStruct((steps, wide_cut.rows, LANES), BF16),
            jax.ShapeDtypeStruct((PAIRS, small_cut.rows, D), BF16),
            jax.ShapeDtypeStruct(vec_shape, F32),
        ],
        in_specs=[pl.BlockSpec(memory_space=pltpu.SMEM)] + [ANY] * 12 + [VMEM] * 10,
        out_specs=[ANY] * 4 + [VMEM],
        scratch_shapes=[pltpu.VMEM(x.shape, BF16) for x in loaded]
        + [
            pltpu.VMEM((rows, D), F32), pltpu.VMEM((rows, D), BF16),
            pltpu.VMEM((rows, D), F32), pltpu.VMEM((rows, D), F32),
            pltpu.VMEM((rows, CHUNK), BF16), pltpu.VMEM((rows, CHUNK), BF16),
            pltpu.VMEM((2, steps, CHUNK * D // LANES, LANES), BF16),
            pltpu.VMEM((PAIRS, small_cut.rows, D), BF16),
            pltpu.VMEM((rows, D), BF16), pltpu.VMEM((D, rows), BF16),
            pltpu.VMEM((HEADS, 1, rows), F32), pltpu.VMEM(blocks, BF16),
            pltpu.VMEM((D, keys), BF16), pane, pane, pane, pane, pltpu.VMEM((D, rows), F32),
            shared, shared, shared, shared,
            pltpu.VMEM(blocks, BF16),
            pltpu.VMEM(vec_shape, F32),
            pltpu.VMEM(vec_shape, F32),
            pltpu.VMEM((wide_cut.n_plane,) + vec_shape, F32),
            pltpu.VMEM((wide_cut.n_depth,) + vec_shape, F32),
            dma((12,)), dma((n,)), dma((n,)),
            dma((2, PAIRS, plan.share)), dma((2, PAIRS, plan.share)), dma((n,)), dma((n,)),
            dma((2,)), dma((steps + PAIRS,)), dma((2,)),
            dma((2, wide_cut.n_plane)), dma((2, wide_cut.n_depth)),
            *rings,
        ],
        compiler_params=pltpu.CompilerParams(
            collective_id=1, has_side_effects=True, vmem_limit_bytes=VMEM_LIMIT
        ),
        name="rest",
    )(lengths, mixed, start, grad, targets, *weights, q, qt, k, v, log_total, mask, target, *vectors)


def unpack_kernel(plan, small, wide, vec, *outs):
    w_qkv, w_out, w_up, w_down, bias_up, soft = outs[:6]
    step = pl.program_id(0)
    for t in range(D // LANES):
        at = slice(t * LANES, (t + 1) * LANES)
        w_down[:, at] = wide[0, 0, t * CHUNK : (t + 1) * CHUNK, :].astype(F32)
        part = pl.ds(pl.multiple_of(t * D + step * PAIR, PAIR), PAIR)
        w_qkv[:, part] = small[0, :D, at].astype(F32)
    for t in range(CHUNK // LANES):
        w_up[:, t * LANES : (t + 1) * LANES] = wide[0, 1, t * D : (t + 1) * D, :].astype(F32)
    w_out[...] = small[0, D:, :].astype(F32)

    @pl.when(step == 0)
    def _():
        for i, out in enumerate(outs[6:]):
            out[...] = vec[i, :]
        for i in range(FF // D):
            bias_up[i * D : (i + 1) * D] = vec[9 + i, :]
        scores = vec[13:14, :]
        n = plan.clips
        lane = lax.broadcasted_iota(jnp.int32, (n, D), 1)
        sub = lax.broadcasted_iota(jnp.int32, (n, D), 0)
        slot = lax.axis_index("batch") * 2 * n + sub
        hits = jnp.sum(jnp.where(lane == slot, scores, 0.0), axis=1, keepdims=True)
        counts = jnp.sum(jnp.where(lane == slot + n, scores, 0.0), axis=1, keepdims=True)
        means = hits / jnp.maximum(counts, 1.0)
        soft[...] = jnp.sum(jnp.where(lane == sub, means, 0.0), axis=0)[:n]


def unpack(plan, small, wide, vec):
    vector = jax.ShapeDtypeStruct((D,), F32)
    steps = FF // CHUNK
    assert steps == PAIRS

    def full(shape):
        return pl.BlockSpec(shape, lambda i: (0,) * len(shape))

    return pl.pallas_call(
        functools.partial(unpack_kernel, plan),
        grid=(steps,),
        in_specs=[
            pl.BlockSpec((1, D + PAIR, D), lambda i: (i, 0, 0)),
            pl.BlockSpec((1, 2, CHUNK * D // LANES, LANES), lambda i: (i, 0, 0, 0)),
            full((VEC_ROWS, D)),
        ],
        out_specs=[
            full((D, 3 * D)),
            pl.BlockSpec((PAIR, D), lambda i: (i, 0)),
            pl.BlockSpec((D, CHUNK), lambda i: (0, i)),
            pl.BlockSpec((CHUNK, D), lambda i: (i, 0)),
            full((FF,)),
            full((plan.clips,)),
        ]
        + [full((D,))] * 9,
        out_shape=[
            jax.ShapeDtypeStruct((D, 3 * D), F32),
            jax.ShapeDtypeStruct((D, D), F32),
            jax.ShapeDtypeStruct((D, FF), F32),
            jax.ShapeDtypeStruct((FF, D), F32),
            jax.ShapeDtypeStruct((FF,), F32),
            jax.ShapeDtypeStruct((plan.clips,), F32),
        ]
        + [vector] * 9,
        compiler_params=pltpu.CompilerParams(vmem_limit_bytes=VMEM_LIMIT),
        name="unpack",
    )(small, wide.reshape(steps, 2, CHUNK * D // LANES, LANES), vec)


def per_device(
    plan,
    patches, patch_mask, clip_lengths, target_index, targets, out_grad,
    mask_embed, ln1_gain, ln1_shift, w_qkv, bias_q, bias_v, w_out, bias_out,
    ln2_gain, ln2_shift, w_up, bias_up, w_down, bias_down,
):
    n, rows, block_rows = plan.clips, plan.rows, plan.block_rows
    (start, queries, queries_t, key_rows, value_rows, mixed, log_total, mask, target, grad) = front(
        plan, clip_lengths, patches.reshape(n, block_rows, D), patch_mask, target_index,
        out_grad.reshape(n, block_rows, D), mask_embed, ln1_gain, ln1_shift, w_qkv, bias_q, bias_v,
    )
    block_grid, input_grad, wide, small, vec = rest(
        plan, clip_lengths, mixed, start.reshape(rows, D), grad.reshape(rows, D), targets,
        (w_out, w_up, w_down, w_qkv), queries.reshape(rows, D), queries_t, key_rows, value_rows,
        log_total, mask, target,
        (ln1_gain, ln1_shift, bias_out, ln2_gain, ln2_shift, bias_up, bias_down),
    )
    grad_w_qkv, grad_w_out, grad_w_up, grad_w_down, grad_bias_up, soft_accuracy, *vectors = unpack(
        plan, small, wide, vec
    )
    (grad_mask_embed, grad_ln1_gain, grad_ln1_shift, grad_bias_q, grad_bias_v, grad_bias_out,
     grad_ln2_gain, grad_ln2_shift, grad_bias_down) = vectors
    return (
        block_grid.reshape(patches.shape), input_grad.reshape(patches.shape), grad_mask_embed,
        grad_ln1_gain, grad_ln1_shift, grad_w_qkv, grad_bias_q, grad_bias_v, grad_w_out,
        grad_bias_out, grad_ln2_gain, grad_ln2_shift, grad_w_up, grad_bias_up, grad_w_down,
        grad_bias_down, soft_accuracy,
    )


def solution(mesh):
    rows = P("batch", "freq", "tm", None)
    whole = P()
    in_specs = (
        rows, P("batch", "freq", "tm"), P("batch"), P("batch", "freq", "tm"),
        P("batch", None, None), rows,
    ) + (whole,) * 14
    out_specs = (rows, rows) + (whole,) * 14 + (P("batch"),)

    def body(*args):
        return per_device(Plan(mesh, args[0]), *args)

    return jax.shard_map(
        body, mesh=mesh, in_specs=in_specs, out_specs=out_specs, check_vma=False
    )
```

```python
import functools

import jax
import jax.numpy as jnp
from jax import lax
from jax.experimental import pallas as pl
from jax.experimental.pallas import tpu as pltpu
from jax.sharding import PartitionSpec as P

D = 384
FF = 1536
HEADS = 6
HEAD_DIM = 64
PAIRS = HEADS // 2
PAIR = 2 * HEAD_DIM
SCALE = HEAD_DIM ** (-0.5)
DEAD = -1e9
EPS = 1e-06
VEC_ROWS = 16
LANES = 128
CHUNK = 512
TILE = 1024
GRID_AT = (0, 1, 2, 4, 5, 6, 8, 9)
WAVES = (4, 6)
MESH = pl.DeviceIdType.MESH
VMEM_LIMIT = 60 * 2**20
ANY = pl.BlockSpec(memory_space=pl.ANY)
VMEM = pl.BlockSpec(memory_space=pltpu.VMEM)
BF16 = jnp.bfloat16
F32 = jnp.float32


def mm(left_mat, right_mat):
    return jnp.dot(left_mat, right_mat, preferred_element_type=F32)


def mm_nt(left_mat, right_mat):
    return lax.dot_general(
        left_mat, right_mat, (((1,), (1,)), ((), ())), preferred_element_type=F32
    )


def mm_tn(left_mat, right_mat):
    return lax.dot_general(
        left_mat, right_mat, (((0,), (0,)), ((), ())), preferred_element_type=F32
    )


def row(ref):
    return ref[...].astype(F32).reshape(1, -1)


def normalize(rows):
    center = rows - jnp.mean(rows, axis=-1, keepdims=True)
    scale = lax.rsqrt(jnp.mean(center * center, axis=-1, keepdims=True) + EPS)
    return center * scale, scale


def normalize_back(grad_hat, hat, scale):
    first = jnp.mean(grad_hat, axis=-1, keepdims=True)
    second = jnp.mean(grad_hat * hat, axis=-1, keepdims=True)
    return scale * (grad_hat - first - hat * second)


def sum_rows(rows):
    return jnp.sum(rows, axis=0, keepdims=True)


def columns(ints):
    freq_rows, time_rows = ints.shape
    shape = (time_rows, time_rows)
    eye = lax.broadcasted_iota(jnp.int32, shape, 0) == lax.broadcasted_iota(jnp.int32, shape, 1)
    parts = [
        jnp.sum(jnp.where(eye, ints[f : f + 1, :], 0), axis=1, keepdims=True)
        for f in range(freq_rows)
    ]
    return jnp.concatenate(parts, axis=0)


class Plan:
    def __init__(self, mesh, patches):
        self.freq = mesh.shape["freq"]
        self.tm = mesh.shape["tm"]
        self.batch = mesh.shape["batch"]
        self.clips, self.freq_rows, self.time_rows, _ = patches.shape
        self.share = self.freq * self.tm // self.clips
        self.blocks = self.tm // self.share
        self.block_rows = self.freq_rows * self.time_rows
        self.rows = self.clips * self.block_rows
        self.keys = self.share * self.rows
        assert self.freq * self.blocks == self.clips and self.blocks * self.share == self.tm

    def place(self):
        time_id = lax.axis_index("tm")
        return lax.axis_index("freq") * self.blocks + time_id // self.share, time_id % self.share

    def member(self, member, part):
        return {
            "freq": member // self.blocks,
            "tm": (member % self.blocks) * self.share + part,
        }

    def sharer(self, part):
        time_id = lax.axis_index("tm")
        return {"tm": time_id // self.share * self.share + part}

    def key_time(self, place):
        part = place // self.rows
        block = (place // self.block_rows) % self.clips % self.blocks
        return (block * self.share + part) * self.time_rows + place % self.time_rows


def greet(devices):
    barrier = pltpu.get_barrier_semaphore()
    for device in devices:
        pl.semaphore_signal(barrier, inc=1, device_id=device, device_id_type=MESH)
    pl.semaphore_wait(barrier, len(devices))


def remote(src, dst, send_sem, recv_sem, device):
    return pltpu.make_async_remote_copy(
        src_ref=src, dst_ref=dst, send_sem=send_sem, recv_sem=recv_sem,
        device_id=device, device_id_type=MESH,
    )


def front_kernel(
    plan, lengths, patches, mask, target, out_grad, embed, gain, shift, w_ref, bias_q, bias_v,
    start_out, q_out, qt_out, k_out, v_out, mixed_out, total_out, mask_out, target_out, grad_out,
    taken, mask_in, target_in, start_buf, q_buf, qt_buf, kv_buf, k_buf, v_buf, vt_buf,
    mixed_buf, total_buf, score_a, score_b,
    send_sem, recv_sem, local_sem, kv_send, kv_recv, grad_send, grad_recv, out_sem,
):
    me, part = plan.place()
    n, rows, keys, block_rows = plan.clips, plan.rows, plan.keys, plan.block_rows
    peers = [lax.rem(me + step, n) for step in range(n)]
    sharers = [lax.rem(part + step, plan.share) for step in range(plan.share)]
    greet(
        [plan.member(peers[step], part) for step in range(1, n)]
        + [plan.sharer(sharers[step]) for step in range(1, plan.share)]
    )
    streams = ((mask, mask_in), (target, target_in), (patches, taken))
    arrivals = []
    for step in range(n):
        copies = []
        for i, (src, dst) in enumerate(streams):
            if step == 0:
                copy = pltpu.make_async_copy(src.at[me], dst.at[me], local_sem.at[i])
            else:
                copy = remote(
                    src.at[peers[step]], dst.at[me], send_sem.at[i, step], recv_sem.at[i, step],
                    plan.member(peers[step], part),
                )
            copy.start()
            copies.append(copy)
        arrivals.append(copies)
    gain_row, shift_row, embed_row = row(gain), row(shift), row(embed)
    bias_q_row, bias_v_row = row(bias_q), row(bias_v)
    waits, shared = [], []

    def save(index, src, dst):
        copy = pltpu.make_async_copy(src, dst, out_sem.at[index])
        copy.start()
        waits.append(copy)

    for step in range(n):
        source = lax.rem(me + n - step, n)
        for copy in arrivals[step]:
            if step == 0:
                copy.wait()
            else:
                copy.wait_recv()
        masked = columns(mask_in[source]) == 1
        start = jnp.where(masked, embed_row, taken[source].astype(F32))
        start_buf[source] = start.astype(BF16)
        hat, _ = normalize(start)
        normed = (hat * gain_row + shift_row).astype(BF16)
        project = mm(normed, w_ref[...])
        queries = (project[:, :D] + bias_q_row).astype(BF16)
        q_buf[source] = (queries.astype(F32) * SCALE).astype(BF16)
        kv_buf[part, source, :, :D] = project[:, D : 2 * D].astype(BF16)
        kv_buf[part, source, :, D:] = (project[:, 2 * D :] + bias_v_row).astype(BF16)
        for other in range(1, plan.share):
            copy = remote(
                kv_buf.at[part, source], kv_buf.at[part, source], kv_send.at[other, step],
                kv_recv.at[other, step], plan.sharer(sharers[other]),
            )
            copy.start()
            shared.append(copy)
    for step in range(n):
        if step == 0:
            copy = pltpu.make_async_copy(out_grad.at[me], grad_out.at[me], local_sem.at[0])
        else:
            copy = remote(
                out_grad.at[peers[step]], grad_out.at[me], grad_send.at[step], grad_recv.at[step],
                plan.member(peers[step], part),
            )
        copy.start()
        waits.append(copy)
    save(0, start_buf, start_out)
    save(1, q_buf, q_out)
    save(2, mask_in, mask_out)
    save(3, target_in, target_out)
    for i in range(n):
        at = slice(i * block_rows, (i + 1) * block_rows)
        qt_buf[:, at] = q_buf[i].T
    save(4, qt_buf, qt_out)
    for copy in shared:
        copy.wait()
    length = lengths[me]
    first = kv_buf[0, 0, 0:1, :D]
    for i in range(plan.share):
        for b in range(n):
            begin = i * rows + b * block_rows
            at = slice(begin, begin + block_rows)
            ids = lax.broadcasted_iota(jnp.int32, (block_rows, 1), 0) + begin
            live = plan.key_time(ids) < length
            k_buf[at, :] = jnp.where(live, kv_buf[i, b, :, :D], first)
            value = kv_buf[i, b, :, D:]
            value = jnp.where(live, value, jnp.zeros_like(value))
            v_buf[at, :] = value
            turned = value.T
            ids = lax.broadcasted_iota(jnp.int32, (16, block_rows), 1) + begin
            top = lax.broadcasted_iota(jnp.int32, (16, block_rows), 0) == 0
            count = jnp.where((plan.key_time(ids) < length) & top, 1.0, 0.0).astype(BF16)
            for h in range(HEADS):
                vt_buf[h, :HEAD_DIM, at] = turned[h * HEAD_DIM : (h + 1) * HEAD_DIM, :]
                vt_buf[h, HEAD_DIM:, at] = count
    save(5, k_buf, k_out)
    save(6, v_buf, v_out)

    width = score_a.shape[1]
    spans = rows // width
    items = HEADS * spans
    lane = lax.broadcasted_iota(jnp.int32, (1, PAIR), 1)

    def score(item, buf):
        head, span = item // spans, item % spans
        pair = pl.ds(pl.multiple_of(head // 2 * PAIR, PAIR), PAIR)
        at = pl.ds(pl.multiple_of(span * width, width), width)
        k_own = jnp.where(lane // HEAD_DIM == head % 2, k_buf[:, pair], jnp.zeros((), BF16))
        scores = mm(k_own, qt_buf[pair, at])
        buf[...] = scores
        return jnp.max(scores, axis=0, keepdims=True)

    def blend(item, buf, top):
        head, span = item // spans, item % spans
        at = pl.ds(pl.multiple_of(span * width, width), width)
        raised = jnp.exp(buf[...] - top).astype(BF16)
        out = mm(vt_buf[head], raised)
        row_total = out[HEAD_DIM : HEAD_DIM + 1, :]
        into = pl.ds(pl.multiple_of(head * HEAD_DIM, HEAD_DIM), HEAD_DIM)
        mixed_buf[into, at] = (out[:HEAD_DIM, :] / row_total).astype(BF16)
        total_buf[head, :, at] = top + jnp.log(row_total)

    def two(i, top_a):
        top_b = score(2 * i + 1, score_b)
        blend(2 * i, score_a, top_a)
        top_a = score(2 * i + 2, score_a)
        blend(2 * i + 1, score_b, top_b)
        return top_a

    top_a = lax.fori_loop(0, items // 2 - 1, two, score(0, score_a))
    top_b = score(items - 1, score_b)
    blend(items - 2, score_a, top_a)
    blend(items - 1, score_b, top_b)
    save(7, mixed_buf, mixed_out)
    save(8, total_buf, total_out)
    for step in range(1, n):
        for copy in arrivals[step]:
            copy.wait_send()
    for copy in waits:
        copy.wait()


def front(plan, lengths, patches, mask, target, out_grad, embed, gain, shift, w_qkv, bias_q, bias_v):
    n, rows, keys, block_rows = plan.clips, plan.rows, plan.keys, plan.block_rows
    width = min(512, rows)
    assert HEADS * (rows // width) % 2 == 0
    dma = pltpu.SemaphoreType.DMA
    blocks = (n, block_rows, D)
    total = (HEADS, 1, rows)
    shapes = [
        (blocks, BF16), (blocks, BF16), ((D, rows), BF16), ((keys, D), BF16), ((keys, D), BF16),
        ((D, rows), BF16), (total, F32), (mask.shape, jnp.int32), (mask.shape, jnp.int32),
        (blocks, BF16),
    ]
    return pl.pallas_call(
        functools.partial(front_kernel, plan),
        out_shape=[jax.ShapeDtypeStruct(shape, kind) for shape, kind in shapes],
        in_specs=[pl.BlockSpec(memory_space=pltpu.SMEM)] + [ANY] * 4 + [VMEM] * 6,
        out_specs=[ANY] * 10,
        scratch_shapes=[
            pltpu.VMEM(blocks, BF16),
            pltpu.VMEM(mask.shape, jnp.int32),
            pltpu.VMEM(mask.shape, jnp.int32),
            pltpu.VMEM(blocks, BF16),
            pltpu.VMEM(blocks, BF16),
            pltpu.VMEM((D, rows), BF16),
            pltpu.VMEM((plan.share, n, block_rows, 2 * D), BF16),
            pltpu.VMEM((keys, D), BF16),
            pltpu.VMEM((keys, D), BF16),
            pltpu.VMEM((HEADS, HEAD_DIM + 16, keys), BF16),
            pltpu.VMEM((D, rows), BF16),
            pltpu.VMEM(total, F32),
            pltpu.VMEM((keys, width), F32),
            pltpu.VMEM((keys, width), F32),
            dma((3, n)), dma((3, n)), dma((3,)),
            dma((plan.share, n)), dma((plan.share, n)), dma((n,)), dma((n,)), dma((9,)),
        ],
        compiler_params=pltpu.CompilerParams(
            collective_id=0, has_side_effects=True, vmem_limit_bytes=VMEM_LIMIT
        ),
        name="front",
    )(lengths, patches, mask, target, out_grad, embed, gain, shift, w_qkv, bias_q, bias_v)


def gelu_parts(rows):
    lower = 0.5 * (1.0 + lax.erf(rows * 0.7071067811865476))
    slope = lower + rows * (jnp.exp(-0.5 * rows * rows) * 0.3989422804014327)
    return rows * lower, slope


class Ring:
    def __init__(self, cut, at, half_src, own_half, core_in, mine, plane_in, part_buf, depth_in, total, sems):
        self.cut, self.at = cut, at
        self.half_src, self.own_half, self.core_in, self.mine = half_src, own_half, core_in, mine
        self.plane_in, self.part_buf, self.depth_in, self.total = plane_in, part_buf, depth_in, total
        self.core_sem, self.plane_sem, self.depth_sem, self.up_sem, self.wide_sem = sems

    def core_copy(self):
        return remote(
            self.half_src, self.core_in, self.core_sem.at[0], self.core_sem.at[1], self.at.partner
        )

    def plane_copies(self):
        chunk = self.cut.chunk
        return [
            remote(
                self.mine.at[spot(self.at.planes[k] * chunk, chunk)], self.plane_in.at[k],
                self.plane_sem.at[0, k], self.plane_sem.at[1, k], self.at.in_plane[k],
            )
            for k in range(1, self.cut.n_plane)
        ]

    def depth_copies(self):
        piece, copies = self.cut.piece, []
        for k in range(1, self.cut.n_depth):
            if self.cut.scatter:
                src = self.part_buf.at[spot(self.at.depths[k] * piece, piece)]
                dst = self.depth_in.at[k]
            else:
                src = dst = self.depth_in.at[self.at.depth]
            copies.append(
                remote(
                    src, dst, self.depth_sem.at[0, k], self.depth_sem.at[1, k], self.at.in_depth[k]
                )
            )
        return copies

    def same(self, first, count, sems, k, device):
        own = spot(first, count)
        return remote(self.total.at[own], self.total.at[own], sems.at[0, k], sems.at[1, k], device)

    def home(self):
        return self.at.core * self.cut.half + self.at.plane * self.cut.chunk

    def up_copies(self):
        first = self.home() + self.at.depth * self.cut.piece
        return [
            self.same(first, self.cut.piece, self.up_sem, k, self.at.in_depth[k])
            for k in range(1, self.cut.n_depth)
        ]

    def wide_copies(self):
        return [
            self.same(self.home(), self.cut.chunk, self.wide_sem, k, self.at.in_plane[k])
            for k in range(1, self.cut.n_plane)
        ]

    def last_copy(self):
        own = spot(self.at.core * self.cut.half, self.cut.half)
        return remote(
            self.total.at[own], self.total.at[own], self.core_sem.at[2], self.core_sem.at[3],
            self.at.partner,
        )

    def begin(self):
        self.core_copy().start()

    def to_plane(self):
        self.core_copy().wait()
        own = self.own_half[...].astype(F32) + self.core_in[...].astype(F32)
        self.mine[...] = own.astype(BF16)
        for copy in self.plane_copies():
            copy.start()

    def to_depth(self):
        chunk = self.cut.chunk
        mine = self.mine[spot(self.at.plane * chunk, chunk), :].astype(F32)
        for k, copy in enumerate(self.plane_copies()):
            copy.wait()
            mine = mine + self.plane_in[k + 1].astype(F32)
        if self.cut.scatter:
            self.part_buf[...] = mine.astype(BF16)
        else:
            self.depth_in[self.at.depth] = mine.astype(BF16)
        for copy in self.depth_copies():
            copy.start()

    def back_up(self):
        piece, copies = self.cut.piece, self.depth_copies()
        if self.cut.scatter:
            mine = self.part_buf[spot(self.at.depth * piece, piece), :].astype(F32)
            for k, copy in enumerate(copies):
                copy.wait()
                mine = mine + self.depth_in[k + 1].astype(F32)
            self.total[spot(self.home() + self.at.depth * piece, piece), :] = mine.astype(BF16)
            for copy in self.up_copies():
                copy.start()
        else:
            for copy in copies:
                copy.wait()
            mine = self.depth_in[0].astype(F32)
            for k in range(1, self.cut.n_depth):
                mine = mine + self.depth_in[k].astype(F32)
            self.total[spot(self.home(), self.cut.chunk), :] = mine.astype(BF16)

    def back_wide(self):
        if self.cut.scatter:
            for copy in self.up_copies():
                copy.wait()
        for copy in self.wide_copies():
            copy.start()

    def back_core(self):
        for copy in self.wide_copies():
            copy.wait()
        self.last_copy().start()

    def turn(self):
        self.to_depth()
        self.back_up()
        self.back_wide()

    def end(self):
        self.last_copy().wait()


class Cut:
    def __init__(self, plan, rows, width, flat=False):
        self.rows, self.width = rows, width
        self.n_plane = plan.freq * plan.batch
        self.n_depth = plan.tm // 2
        self.flat = flat and rows // 2 % (16 * self.n_plane * self.n_depth) == 0
        if self.flat:
            self.n_plane, self.n_depth = self.n_plane * self.n_depth, 1
        self.half = rows // 2
        self.chunk = self.half // self.n_plane
        self.piece = self.chunk // self.n_depth
        self.scatter = self.piece % 16 == 0 and self.piece * self.n_depth == self.chunk
        assert self.chunk * self.n_plane == self.half and self.chunk % 16 == 0

    def buffers(self):
        depth = self.piece if self.scatter else self.chunk
        shapes = [
            (self.half,), (self.half,), (self.n_plane, self.chunk), (self.chunk,),
            (self.n_depth, depth), (self.rows,),
        ]
        return [pltpu.VMEM(shape + (self.width,), BF16) for shape in shapes]

    def semaphores(self):
        dma = pltpu.SemaphoreType.DMA
        return [
            dma((4,)), dma((2, self.n_plane)), dma((2, self.n_depth)), dma((2, self.n_depth)),
            dma((2, self.n_plane)),
        ]


class Place:
    def __init__(self, plan):
        time_id = lax.axis_index("tm")
        n_plane, n_depth = plan.freq * plan.batch, plan.tm // 2
        self.core, self.depth = time_id % 2, time_id // 2
        self.plane = lax.axis_index("freq") * plan.batch + lax.axis_index("batch")
        self.partner = {"tm": time_id + 1 - 2 * self.core}
        self.planes = [lax.rem(self.plane + k, n_plane) for k in range(n_plane)]
        self.depths = [lax.rem(self.depth + k, n_depth) for k in range(n_depth)]
        self.in_plane = [{"freq": v // plan.batch, "batch": v % plan.batch} for v in self.planes]
        self.in_depth = [{"tm": v * 2 + self.core} for v in self.depths]


class Flat:
    def __init__(self, plan, place):
        n_depth = plan.tm // 2
        count = plan.freq * plan.batch * n_depth
        self.core, self.partner, self.depth, self.in_depth = place.core, place.partner, 0, [None]
        self.plane = place.plane * n_depth + place.depth
        self.planes = [lax.rem(self.plane + k, count) for k in range(count)]
        self.in_plane = [
            {
                "freq": v // n_depth // plan.batch,
                "batch": v // n_depth % plan.batch,
                "tm": v % n_depth * 2 + place.core,
            }
            for v in self.planes
        ]


def spot(first, count):
    return pl.ds(pl.multiple_of(first, 16), count)


def rest_kernel(
    plan, wide_cut, small_cuts, lengths,
    mixed_in, start_in, grad_in, targets_in, w_out_in, w_up_in, w_down_in, w_qkv_in,
    q_in, qt_in, k_in, v_in, log_total, mask, target,
    ln1_gain, ln1_shift, bias_out, ln2_gain, ln2_shift, bias_up, bias_down,
    block_grid, input_grad, wide_out, small_out, vec_out,
    mixed, start, grad, targets, w_out, w_up, w_down, w_qkv, q_ref, qt_ref, k_ref, v_ref,
    middle, second, down_sum, second_sum, act_buf, up_buf, payload, small_pay, do_ref, dot_ref,
    center, block_out,
    kt_buf, score_a, score_b, prob_a, prob_b, dqt_sum, dk_all, dv_all, dk_in, dv_in,
    rows_buf, vec_buf, vec_core, vec_plane, vec_depth,
    load_sem, grid_ss, grid_rs, kv_ss, kv_rs, rows_ss, rows_rs, local_sem, out_sem,
    vec_core_sem, vec_plane_sem, vec_depth_sem,
    *rest,
):
    n, rows, keys, block_rows = plan.clips, plan.rows, plan.keys, plan.block_rows
    me, part = plan.place()
    at = Place(plan)
    last_cut = small_cuts[-1]
    flat = Flat(plan, at) if last_cut.flat else at
    n_plane, n_depth = wide_cut.n_plane, wide_cut.n_depth
    peers = [lax.rem(me + k, n) for k in range(n)]
    sharers = [lax.rem(part + k, plan.share) for k in range(plan.share)]
    length = lengths[me]

    loads = [
        pltpu.make_async_copy(src, dst, load_sem.at[i])
        for i, (src, dst) in enumerate(
            (
                (mixed_in, mixed), (w_out_in, w_out), (start_in, start), (w_up_in, w_up),
                (w_down_in, w_down), (grad_in, grad), (targets_in.at[me], targets),
                (k_in, k_ref), (qt_in, qt_ref), (v_in, v_ref), (q_in, q_ref), (w_qkv_in, w_qkv),
            )
        )
    ]
    for copy in loads:
        copy.start()
    greet(
        [plan.member(peers[k], part) for k in range(1, n)]
        + [plan.sharer(sharers[k]) for k in range(1, plan.share)]
        + [at.partner]
        + (flat.in_plane[1:] if last_cut.flat else at.in_plane[1:] + at.in_depth[1:])
    )
    steps = FF // CHUNK
    wide, small = [], []
    for i in range(steps):
        mine, rest = rest[:11], rest[11:]
        wide.append(
            Ring(
                wide_cut, at, payload.at[1 - at.core, i], payload.at[at.core, i], *mine[:6], mine[6:]
            )
        )
    for p in range(PAIRS):
        mine, rest = rest[:11], rest[11:]
        small_cut = small_cuts[p]
        away = small_pay.at[p, spot((1 - at.core) * small_cut.half, small_cut.half)]
        own = small_pay.at[p, spot(at.core * small_cut.half, small_cut.half)]
        small.append(Ring(small_cut, flat if small_cut.flat else at, away, own, *mine[:6], mine[6:]))

    tile = min(TILE, rows)
    tiles = [slice(i * tile, (i + 1) * tile) for i in range(rows // tile)]
    gain2, shift2 = row(ln2_gain), row(ln2_shift)
    bias_up_row = row(bias_up)
    vec_buf[...] = jnp.zeros_like(vec_buf)
    for copy in loads[:3]:
        copy.wait()
    for span in tiles:
        rows_in = start[span, :].astype(F32) + mm_tn(mixed[:, span], w_out[...]) + row(bias_out)
        middle[span, :] = rows_in
        hat, _ = normalize(rows_in)
        second[span, :] = (hat * gain2 + shift2).astype(BF16)
    for copy in loads[3:6]:
        copy.wait()
    up_sums = []
    for i in range(steps):
        cols = slice(i * CHUNK, (i + 1) * CHUNK)
        for t, span in enumerate(tiles):
            hidden = mm(second[span, :], w_up[:, cols]) + bias_up_row[:, cols]
            active, slope = gelu_parts(hidden)
            active = active.astype(BF16)
            act_buf[span, :] = active
            down = mm(active, w_down[cols, :])
            grad_up = (mm_nt(grad[span, :], w_down[cols, :]) * slope).astype(BF16)
            up_buf[span, :] = grad_up
            back = mm_nt(grad_up, w_up[:, cols])
            if i == 0:
                down_sum[span, :] = down
                second_sum[span, :] = back
            else:
                down_sum[span, :] += down
                second_sum[span, :] += back
            if t == 0 and i >= 1:
                wide[i - 1].to_plane()
        grad_down = mm_tn(act_buf[...], grad[...]).astype(BF16)
        for t in range(D // LANES):
            payload[0, i, t * CHUNK : (t + 1) * CHUNK, :] = grad_down[:, t * LANES : (t + 1) * LANES]
        grad_w = mm_tn(second[...], up_buf[...]).astype(BF16)
        for t in range(CHUNK // LANES):
            payload[1, i, t * D : (t + 1) * D, :] = grad_w[:, t * LANES : (t + 1) * LANES]
        up_sums.append(sum_rows(up_buf[...].astype(F32)))
        wide[i].begin()
        if i >= 2:
            wide[i - 2].to_depth()
    up_sums = jnp.concatenate(up_sums, axis=1)
    for i in range(FF // D):
        vec_buf[9 + i : 10 + i, :] = up_sums[:, i * D : (i + 1) * D]
    vec_buf[8:9, :] = sum_rows(grad[...].astype(F32))
    loads[6].wait()
    home_copies = []
    cand = lax.broadcasted_iota(jnp.int32, (1, targets.shape[0]), 1)
    total_hit = jnp.zeros((1, 1), F32)
    total_count = jnp.zeros((1, 1), F32)
    per_tile = tile // block_rows
    for t, span in enumerate(tiles):
        result = (middle[span, :] + down_sum[span, :] + row(bias_down)).astype(BF16)
        for b in range(per_tile):
            block_out[t * per_tile + b] = result[b * block_rows : (b + 1) * block_rows, :]
        hat, scale = normalize(middle[span, :])
        grad_second = second_sum[span, :]
        vec_buf[6:7, :] += sum_rows(grad_second * hat)
        vec_buf[7:8, :] += sum_rows(grad_second)
        back = grad[span, :].astype(F32) + normalize_back(grad_second * gain2, hat, scale)
        second_sum[span, :] = back
        branch = back.astype(BF16)
        up_buf[span, :D] = branch
        vec_buf[5:6, :] += sum_rows(branch.astype(F32))
        do_ref[span, :] = mm_nt(branch, w_out[...]).astype(BF16)
        down = mm_nt(w_out[...], branch).astype(BF16)
        dot_ref[:, span] = down
        product = down.astype(F32) * mixed[:, span].astype(F32)
        for h in range(HEADS):
            center[h, :, span] = sum_rows(product[h * HEAD_DIM : (h + 1) * HEAD_DIM, :])
        logits = mm_nt(result, targets[...])
        raised = jnp.exp(logits - jnp.max(logits, axis=1, keepdims=True))
        sources = range(t * per_tile, (t + 1) * per_tile)
        target_col = jnp.concatenate([columns(target[s]) for s in sources], axis=0)
        mask_col = jnp.concatenate([columns(mask[s]) for s in sources], axis=0)
        hit = jnp.sum(jnp.where(cand == target_col, raised, 0.0), axis=1, keepdims=True)
        hit = hit / jnp.sum(raised, axis=1, keepdims=True)
        ids = lax.broadcasted_iota(jnp.int32, (tile, 1), 0) + t * tile + part * rows
        counted = jnp.where((plan.key_time(ids) < length) & (mask_col == 1), 1.0, 0.0)
        total_hit += sum_rows(hit * counted)
        total_count += sum_rows(counted)
        if t == 0:
            wide[-1].to_plane()
    home_copies.append(
        pltpu.make_async_copy(block_out.at[me], block_grid.at[me], local_sem.at[0])
    )
    for k in range(1, n):
        home_copies.append(
            remote(
                block_out.at[peers[k]], block_grid.at[me], grid_ss.at[k], grid_rs.at[k],
                plan.member(peers[k], part),
            )
        )
    home_copies[0].start()
    wide[-3].back_up()
    wide[-2].to_depth()
    grad_w = mm(mixed[...], up_buf[:, :D]).astype(BF16)
    for p in range(PAIRS):
        small_pay[p, D:, :] = grad_w[p * PAIR : (p + 1) * PAIR, :]
    lane = lax.broadcasted_iota(jnp.int32, (1, D), 1)
    slot = lax.axis_index("batch") * 2 * n + me
    scores = jnp.where(lane == slot, total_hit, 0.0)
    vec_buf[13:14, :] = scores + jnp.where(lane == slot + n, total_count, 0.0)

    gain1, shift1 = row(ln1_gain), row(ln1_shift)
    hat_buf, normed, grad_buf, grad_middle = middle, second, down_sum, second_sum
    for span in tiles:
        hat, _ = normalize(start[span, :].astype(F32))
        hat_buf[span, :] = hat
        normed[span, :] = (hat * gain1 + shift1).astype(BF16)
    loads[7].wait()
    for i in range(keys // 256):
        span = slice(i * 256, (i + 1) * 256)
        ids = lax.broadcasted_iota(jnp.int32, (1, 256), 1) + i * 256
        turned = k_ref[span, :].T
        kt_buf[:, span] = jnp.where(plan.key_time(ids) < length, turned, jnp.zeros_like(turned))
    dqt_sum[...] = jnp.zeros_like(dqt_sum)
    for copy in loads[8:]:
        copy.wait()

    block = score_a.shape[0]
    per_part = rows // block
    lane = lax.broadcasted_iota(jnp.int32, (1, PAIR), 1)
    owns = [lane // HEAD_DIM == e for e in range(2)]
    zero = jnp.zeros((), BF16)
    per_pair = per_part * plan.share
    bodies = PAIRS * per_pair

    def kv_copies(p):
        return [
            remote(
                src.at[p, sharers[k]], dst.at[p, k], kv_ss.at[i, p, k], kv_rs.at[i, p, k],
                plan.sharer(sharers[k]),
            )
            for i, (src, dst) in enumerate(((dk_all, dk_in), (dv_all, dv_in)))
            for k in range(1, plan.share)
        ]

    def send_keys(p):
        for copy in kv_copies(p):
            copy.start()

    def finish_pair(p):
        for copy in kv_copies(p):
            copy.wait()
        cols = slice(p * PAIR, (p + 1) * PAIR)
        parts = [(dqt_sum[cols, :] * SCALE).T.astype(BF16)]
        ids = lax.broadcasted_iota(jnp.int32, (rows, 1), 0) + part * rows
        live = plan.key_time(ids) < length
        for own, buf in ((dk_all, dk_in), (dv_all, dv_in)):
            summed = own[p, part].astype(F32)
            for k in range(1, plan.share):
                summed = summed + buf[p, k].astype(F32)
            parts.append(jnp.where(live, summed, 0.0).astype(BF16))
        vec_buf[3:4, cols] = sum_rows(parts[0].astype(F32))
        vec_buf[4:5, cols] = sum_rows(parts[2].astype(F32))
        project = jnp.concatenate(parts, axis=1)
        small_pay[p, :D, :] = mm_tn(normed[...], project).astype(BF16)
        small[p].begin()
        weights = [w_qkv[:, i * D + p * PAIR : i * D + (p + 1) * PAIR] for i in range(3)]
        back = mm_nt(project, jnp.concatenate(weights, axis=1))
        if p == 0:
            grad_buf[...] = back
        else:
            grad_buf[...] += back

    def save(i, src, dst):
        return pltpu.make_async_copy(src, dst, out_sem.at[i])

    saves = [save(i, wide[i].total, wide_out.at[i]) for i in range(steps)]
    saves += [save(steps + p, small[p].total, small_out.at[p]) for p in range(PAIRS)]

    def wide_end(i):
        wide[i].end()
        saves[i].start()

    def small_end(p):
        small[p].end()
        saves[steps + p].start()

    last_other = per_pair - per_part - 1
    events = [
        (last_other + p * per_pair, functools.partial(send_keys, p)) for p in range(PAIRS)
    ] + [(p * per_pair + per_pair - 1, functools.partial(finish_pair, p)) for p in range(PAIRS - 1)]
    for when, event in (
        (0, wide[0].back_wide), (0, wide[2].to_depth), (1, wide[1].back_up), (2, wide[2].back_up),
        (3, wide[1].back_wide), (3, wide[0].back_core), (4, small[0].to_plane),
        (4, wide[2].back_wide), (4, functools.partial(wide_end, 0)), (6, wide[1].back_core),
        (6, small[0].to_depth), (7, wide[2].back_core), (7, functools.partial(wide_end, 1)),
        (8, small[0].back_up), (8, small[1].to_plane), (8, functools.partial(wide_end, 2)),
        (10, small[0].back_wide), (10, small[1].to_depth),
    ):
        events.append((when * bodies // 12, event))
    for k in range(1, n):
        events.append((GRID_AT[k % len(GRID_AT)] * bodies // 12, home_copies[k].start))

    def body(i, carry):
        pair, order = i // per_pair, i % per_pair
        owner = lax.rem(part + 1 + order // per_part, plan.share)
        begin = order % per_part * block
        span = pl.ds(pl.multiple_of(owner * rows + begin, block), block)
        inside = pl.ds(pl.multiple_of(begin, block), block)
        cols = pl.ds(pl.multiple_of(pair * PAIR, PAIR), PAIR)
        for e, (score_buf, prob_buf) in enumerate(((score_a, prob_a), (score_b, prob_b))):
            score_buf[...] = mm(jnp.where(owns[e], k_ref[span, cols], zero), qt_ref[cols, :])
            prob_buf[...] = mm(jnp.where(owns[e], v_ref[span, cols], zero), dot_ref[cols, :])
        grad_k, grad_v = [], []
        for e, (score_buf, prob_buf) in enumerate(((score_a, prob_a), (score_b, prob_b))):
            head = pl.ds(pl.multiple_of(pair * PAIR + e * HEAD_DIM, HEAD_DIM), HEAD_DIM)
            prob = jnp.exp(score_buf[...] - log_total[2 * pair + e])
            grad_scores = (prob * (prob_buf[...] - center[2 * pair + e])).astype(BF16)
            grad_v.append(mm(prob.astype(BF16), jnp.where(owns[e], do_ref[:, cols], zero)))
            grad_k.append(mm(grad_scores, jnp.where(owns[e], q_ref[:, cols], zero)))
            dqt_sum[head, :] += mm(kt_buf[head, span], grad_scores)
        dk_all[pair, owner, inside, :] = (grad_k[0] + grad_k[1]).astype(BF16)
        dv_all[pair, owner, inside, :] = (grad_v[0] + grad_v[1]).astype(BF16)
        for when, event in events:
            pl.when(i == when)(event)
        return carry

    lax.fori_loop(0, bodies, body, 0)
    finish_pair(PAIRS - 1)

    row_copies = []
    grad_embed = jnp.zeros((1, D), F32)
    grad_gain = jnp.zeros((1, D), F32)
    grad_shift = jnp.zeros((1, D), F32)
    for k in range(n):
        owner = peers[k]
        span = spot(owner * block_rows, block_rows)
        _, scale = normalize(start[span, :].astype(F32))
        hat = hat_buf[span, :]
        grad_normed = grad_buf[span, :]
        grad_gain += sum_rows(grad_normed * hat)
        grad_shift += sum_rows(grad_normed)
        grad_start = grad_middle[span, :] + normalize_back(grad_normed * gain1, hat, scale)
        masked = columns(mask[owner]) == 1
        grad_embed += sum_rows(jnp.where(masked, grad_start, 0.0))
        rows_buf[owner] = jnp.where(masked, 0.0, grad_start).astype(BF16)
        if k == 0:
            copy = pltpu.make_async_copy(rows_buf.at[owner], input_grad.at[me], local_sem.at[1])
        else:
            copy = remote(
                rows_buf.at[owner], input_grad.at[me], rows_ss.at[k], rows_rs.at[k],
                plan.member(owner, part),
            )
        row_copies.append(copy)
        if k < WAVES[0]:
            copy.start()
        if k == 1:
            small[2].to_plane()
        if k == 3:
            small[1].back_up()
        if k == 5:
            small[0].back_core()
    vec_buf[0:1, :] = grad_embed
    vec_buf[1:2, :] = grad_gain
    vec_buf[2:3, :] = grad_shift
    vec_copy = remote(vec_buf, vec_core, vec_core_sem.at[0], vec_core_sem.at[1], at.partner)
    vec_copy.start()
    vec_copy.wait()
    vec_plane[at.plane] = vec_buf[...] + vec_core[...]
    vec_plane_copies = []
    for k in range(1, n_plane):
        copy = remote(
            vec_plane.at[at.plane], vec_plane.at[at.plane], vec_plane_sem.at[0, k],
            vec_plane_sem.at[1, k], at.in_plane[k],
        )
        copy.start()
        vec_plane_copies.append(copy)
    small[2].to_depth()
    for copy in row_copies[WAVES[0] : WAVES[1]]:
        copy.start()
    small[1].back_wide()
    small_end(0)
    for copy in vec_plane_copies:
        copy.wait()
    summed = vec_plane[0]
    for k in range(1, n_plane):
        summed = summed + vec_plane[k]
    vec_depth[at.depth] = summed
    vec_depth_copies = []
    for k in range(1, n_depth):
        copy = remote(
            vec_depth.at[at.depth], vec_depth.at[at.depth], vec_depth_sem.at[0, k],
            vec_depth_sem.at[1, k], at.in_depth[k],
        )
        copy.start()
        vec_depth_copies.append(copy)
    small[2].back_up()
    for copy in row_copies[WAVES[1] :]:
        copy.start()
    small[1].back_core()
    small[2].back_wide()
    small_end(1)
    for copy in vec_depth_copies:
        copy.wait()
    summed = vec_depth[0]
    for k in range(1, n_depth):
        summed = summed + vec_depth[k]
    vec_out[...] = summed
    small[2].back_core()
    small_end(2)
    for copy in row_copies + home_copies + saves:
        copy.wait()


def rest(plan, lengths, mixed, start, grad, targets, weights, q, qt, k, v, log_total, mask, target, vectors):
    n, rows, keys = plan.clips, plan.rows, plan.keys
    steps = FF // CHUNK
    wide_cut = Cut(plan, 2 * CHUNK * D // LANES, LANES)
    small_cuts = [Cut(plan, D + PAIR, D, flat=False) for p in range(PAIRS)]
    small_cut = small_cuts[0]
    dma = pltpu.SemaphoreType.DMA
    vec_shape = (VEC_ROWS, D)
    block = min(512, rows)
    blocks = (n, plan.block_rows, D)
    shared = pltpu.VMEM((PAIRS, plan.share, rows, PAIR), BF16)
    pane = pltpu.VMEM((block, rows), F32)
    loaded = (mixed, start, grad, targets[0], *weights, q, qt, k, v)
    rings = []
    for cut in [wide_cut] * steps + small_cuts:
        rings += cut.buffers() + cut.semaphores()
    return pl.pallas_call(
        functools.partial(rest_kernel, plan, wide_cut, small_cuts),
        out_shape=[
            jax.ShapeDtypeStruct(blocks, BF16),
            jax.ShapeDtypeStruct(blocks, BF16),
            jax.ShapeDtypeStruct((steps, wide_cut.rows, LANES), BF16),
            jax.ShapeDtypeStruct((PAIRS, small_cut.rows, D), BF16),
            jax.ShapeDtypeStruct(vec_shape, F32),
        ],
        in_specs=[pl.BlockSpec(memory_space=pltpu.SMEM)] + [ANY] * 12 + [VMEM] * 10,
        out_specs=[ANY] * 4 + [VMEM],
        scratch_shapes=[pltpu.VMEM(x.shape, BF16) for x in loaded]
        + [
            pltpu.VMEM((rows, D), F32), pltpu.VMEM((rows, D), BF16),
            pltpu.VMEM((rows, D), F32), pltpu.VMEM((rows, D), F32),
            pltpu.VMEM((rows, CHUNK), BF16), pltpu.VMEM((rows, CHUNK), BF16),
            pltpu.VMEM((2, steps, CHUNK * D // LANES, LANES), BF16),
            pltpu.VMEM((PAIRS, small_cut.rows, D), BF16),
            pltpu.VMEM((rows, D), BF16), pltpu.VMEM((D, rows), BF16),
            pltpu.VMEM((HEADS, 1, rows), F32), pltpu.VMEM(blocks, BF16),
            pltpu.VMEM((D, keys), BF16), pane, pane, pane, pane, pltpu.VMEM((D, rows), F32),
            shared, shared, shared, shared,
            pltpu.VMEM(blocks, BF16),
            pltpu.VMEM(vec_shape, F32),
            pltpu.VMEM(vec_shape, F32),
            pltpu.VMEM((wide_cut.n_plane,) + vec_shape, F32),
            pltpu.VMEM((wide_cut.n_depth,) + vec_shape, F32),
            dma((12,)), dma((n,)), dma((n,)),
            dma((2, PAIRS, plan.share)), dma((2, PAIRS, plan.share)), dma((n,)), dma((n,)),
            dma((2,)), dma((steps + PAIRS,)), dma((2,)),
            dma((2, wide_cut.n_plane)), dma((2, wide_cut.n_depth)),
            *rings,
        ],
        compiler_params=pltpu.CompilerParams(
            collective_id=1, has_side_effects=True, vmem_limit_bytes=VMEM_LIMIT
        ),
        name="rest",
    )(lengths, mixed, start, grad, targets, *weights, q, qt, k, v, log_total, mask, target, *vectors)


def unpack_kernel(plan, small, wide, vec, *outs):
    w_qkv, w_out, w_up, w_down, bias_up, soft = outs[:6]
    step = pl.program_id(0)
    for t in range(D // LANES):
        at = slice(t * LANES, (t + 1) * LANES)
        w_down[:, at] = wide[0, 0, t * CHUNK : (t + 1) * CHUNK, :].astype(F32)
        part = pl.ds(pl.multiple_of(t * D + step * PAIR, PAIR), PAIR)
        w_qkv[:, part] = small[0, :D, at].astype(F32)
    for t in range(CHUNK // LANES):
        w_up[:, t * LANES : (t + 1) * LANES] = wide[0, 1, t * D : (t + 1) * D, :].astype(F32)
    w_out[...] = small[0, D:, :].astype(F32)

    @pl.when(step == 0)
    def _():
        for i, out in enumerate(outs[6:]):
            out[...] = vec[i, :]
        for i in range(FF // D):
            bias_up[i * D : (i + 1) * D] = vec[9 + i, :]
        scores = vec[13:14, :]
        n = plan.clips
        lane = lax.broadcasted_iota(jnp.int32, (n, D), 1)
        sub = lax.broadcasted_iota(jnp.int32, (n, D), 0)
        slot = lax.axis_index("batch") * 2 * n + sub
        hits = jnp.sum(jnp.where(lane == slot, scores, 0.0), axis=1, keepdims=True)
        counts = jnp.sum(jnp.where(lane == slot + n, scores, 0.0), axis=1, keepdims=True)
        means = hits / jnp.maximum(counts, 1.0)
        soft[...] = jnp.sum(jnp.where(lane == sub, means, 0.0), axis=0)[:n]


def unpack(plan, small, wide, vec):
    vector = jax.ShapeDtypeStruct((D,), F32)
    steps = FF // CHUNK
    assert steps == PAIRS

    def full(shape):
        return pl.BlockSpec(shape, lambda i: (0,) * len(shape))

    return pl.pallas_call(
        functools.partial(unpack_kernel, plan),
        grid=(steps,),
        in_specs=[
            pl.BlockSpec((1, D + PAIR, D), lambda i: (i, 0, 0)),
            pl.BlockSpec((1, 2, CHUNK * D // LANES, LANES), lambda i: (i, 0, 0, 0)),
            full((VEC_ROWS, D)),
        ],
        out_specs=[
            full((D, 3 * D)),
            pl.BlockSpec((PAIR, D), lambda i: (i, 0)),
            pl.BlockSpec((D, CHUNK), lambda i: (0, i)),
            pl.BlockSpec((CHUNK, D), lambda i: (i, 0)),
            full((FF,)),
            full((plan.clips,)),
        ]
        + [full((D,))] * 9,
        out_shape=[
            jax.ShapeDtypeStruct((D, 3 * D), F32),
            jax.ShapeDtypeStruct((D, D), F32),
            jax.ShapeDtypeStruct((D, FF), F32),
            jax.ShapeDtypeStruct((FF, D), F32),
            jax.ShapeDtypeStruct((FF,), F32),
            jax.ShapeDtypeStruct((plan.clips,), F32),
        ]
        + [vector] * 9,
        compiler_params=pltpu.CompilerParams(vmem_limit_bytes=VMEM_LIMIT),
        name="unpack",
    )(small, wide.reshape(steps, 2, CHUNK * D // LANES, LANES), vec)


def per_device(
    plan,
    patches, patch_mask, clip_lengths, target_index, targets, out_grad,
    mask_embed, ln1_gain, ln1_shift, w_qkv, bias_q, bias_v, w_out, bias_out,
    ln2_gain, ln2_shift, w_up, bias_up, w_down, bias_down,
):
    n, rows, block_rows = plan.clips, plan.rows, plan.block_rows
    (start, queries, queries_t, key_rows, value_rows, mixed, log_total, mask, target, grad) = front(
        plan, clip_lengths, patches.reshape(n, block_rows, D), patch_mask, target_index,
        out_grad.reshape(n, block_rows, D), mask_embed, ln1_gain, ln1_shift, w_qkv, bias_q, bias_v,
    )
    block_grid, input_grad, wide, small, vec = rest(
        plan, clip_lengths, mixed, start.reshape(rows, D), grad.reshape(rows, D), targets,
        (w_out, w_up, w_down, w_qkv), queries.reshape(rows, D), queries_t, key_rows, value_rows,
        log_total, mask, target,
        (ln1_gain, ln1_shift, bias_out, ln2_gain, ln2_shift, bias_up, bias_down),
    )
    grad_w_qkv, grad_w_out, grad_w_up, grad_w_down, grad_bias_up, soft_accuracy, *vectors = unpack(
        plan, small, wide, vec
    )
    (grad_mask_embed, grad_ln1_gain, grad_ln1_shift, grad_bias_q, grad_bias_v, grad_bias_out,
     grad_ln2_gain, grad_ln2_shift, grad_bias_down) = vectors
    return (
        block_grid.reshape(patches.shape), input_grad.reshape(patches.shape), grad_mask_embed,
        grad_ln1_gain, grad_ln1_shift, grad_w_qkv, grad_bias_q, grad_bias_v, grad_w_out,
        grad_bias_out, grad_ln2_gain, grad_ln2_shift, grad_w_up, grad_bias_up, grad_w_down,
        grad_bias_down, soft_accuracy,
    )


def solution(mesh):
    rows = P("batch", "freq", "tm", None)
    whole = P()
    in_specs = (
        rows, P("batch", "freq", "tm"), P("batch"), P("batch", "freq", "tm"),
        P("batch", None, None), rows,
    ) + (whole,) * 14
    out_specs = (rows, rows) + (whole,) * 14 + (P("batch"),)

    def body(*args):
        return per_device(Plan(mesh, args[0]), *args)

    return jax.shard_map(
        body, mesh=mesh, in_specs=in_specs, out_specs=out_specs, check_vma=False
    )
```

```python
import functools

import jax
import jax.numpy as jnp
from jax import lax
from jax.experimental import pallas as pl
from jax.experimental.pallas import tpu as pltpu
from jax.sharding import PartitionSpec as P

D = 384
FF = 1536
HEADS = 6
HEAD_DIM = 64
PAIRS = HEADS // 2
PAIR = 2 * HEAD_DIM
SCALE = HEAD_DIM ** (-0.5)
DEAD = -1e9
EPS = 1e-06
VEC_ROWS = 16
LANES = 128
CHUNK = 512
TILE = 1024
GRID_AT = (0, 1, 2, 4, 5, 6, 8, 9)
WAVES = (4, 6)
MESH = pl.DeviceIdType.MESH
VMEM_LIMIT = 60 * 2**20
ANY = pl.BlockSpec(memory_space=pl.ANY)
VMEM = pl.BlockSpec(memory_space=pltpu.VMEM)
BF16 = jnp.bfloat16
F32 = jnp.float32


def mm(left_mat, right_mat):
    return jnp.dot(left_mat, right_mat, preferred_element_type=F32)


def mm_nt(left_mat, right_mat):
    return lax.dot_general(
        left_mat, right_mat, (((1,), (1,)), ((), ())), preferred_element_type=F32
    )


def mm_tn(left_mat, right_mat):
    return lax.dot_general(
        left_mat, right_mat, (((0,), (0,)), ((), ())), preferred_element_type=F32
    )


def row(ref):
    return ref[...].astype(F32).reshape(1, -1)


def normalize(rows):
    center = rows - jnp.mean(rows, axis=-1, keepdims=True)
    scale = lax.rsqrt(jnp.mean(center * center, axis=-1, keepdims=True) + EPS)
    return center * scale, scale


def normalize_back(grad_hat, hat, scale):
    first = jnp.mean(grad_hat, axis=-1, keepdims=True)
    second = jnp.mean(grad_hat * hat, axis=-1, keepdims=True)
    return scale * (grad_hat - first - hat * second)


def sum_rows(rows):
    return jnp.sum(rows, axis=0, keepdims=True)


def columns(ints):
    freq_rows, time_rows = ints.shape
    shape = (time_rows, time_rows)
    eye = lax.broadcasted_iota(jnp.int32, shape, 0) == lax.broadcasted_iota(jnp.int32, shape, 1)
    parts = [
        jnp.sum(jnp.where(eye, ints[f : f + 1, :], 0), axis=1, keepdims=True)
        for f in range(freq_rows)
    ]
    return jnp.concatenate(parts, axis=0)


class Plan:
    def __init__(self, mesh, patches):
        self.freq = mesh.shape["freq"]
        self.tm = mesh.shape["tm"]
        self.batch = mesh.shape["batch"]
        self.clips, self.freq_rows, self.time_rows, _ = patches.shape
        self.share = self.freq * self.tm // self.clips
        self.blocks = self.tm // self.share
        self.block_rows = self.freq_rows * self.time_rows
        self.rows = self.clips * self.block_rows
        self.keys = self.share * self.rows
        assert self.freq * self.blocks == self.clips and self.blocks * self.share == self.tm

    def place(self):
        time_id = lax.axis_index("tm")
        return lax.axis_index("freq") * self.blocks + time_id // self.share, time_id % self.share

    def member(self, member, part):
        return {
            "freq": member // self.blocks,
            "tm": (member % self.blocks) * self.share + part,
        }

    def sharer(self, part):
        time_id = lax.axis_index("tm")
        return {"tm": time_id // self.share * self.share + part}

    def key_time(self, place):
        part = place // self.rows
        block = (place // self.block_rows) % self.clips % self.blocks
        return (block * self.share + part) * self.time_rows + place % self.time_rows


def greet(devices):
    barrier = pltpu.get_barrier_semaphore()
    for device in devices:
        pl.semaphore_signal(barrier, inc=1, device_id=device, device_id_type=MESH)
    pl.semaphore_wait(barrier, len(devices))


def remote(src, dst, send_sem, recv_sem, device):
    return pltpu.make_async_remote_copy(
        src_ref=src, dst_ref=dst, send_sem=send_sem, recv_sem=recv_sem,
        device_id=device, device_id_type=MESH,
    )


def front_kernel(
    plan, lengths, patches, mask, target, out_grad, embed, gain, shift, w_ref, bias_q, bias_v,
    start_out, q_out, qt_out, k_out, v_out, mixed_out, total_out, mask_out, target_out, grad_out,
    taken, mask_in, target_in, start_buf, q_buf, qt_buf, kv_buf, k_buf, v_buf, vt_buf,
    mixed_buf, total_buf, score_a, score_b,
    send_sem, recv_sem, local_sem, kv_send, kv_recv, grad_send, grad_recv, out_sem,
):
    me, part = plan.place()
    n, rows, keys, block_rows = plan.clips, plan.rows, plan.keys, plan.block_rows
    peers = [lax.rem(me + step, n) for step in range(n)]
    sharers = [lax.rem(part + step, plan.share) for step in range(plan.share)]
    greet(
        [plan.member(peers[step], part) for step in range(1, n)]
        + [plan.sharer(sharers[step]) for step in range(1, plan.share)]
    )
    streams = ((mask, mask_in), (target, target_in), (patches, taken))
    arrivals = []
    for step in range(n):
        copies = []
        for i, (src, dst) in enumerate(streams):
            if step == 0:
                copy = pltpu.make_async_copy(src.at[me], dst.at[me], local_sem.at[i])
            else:
                copy = remote(
                    src.at[peers[step]], dst.at[me], send_sem.at[i, step], recv_sem.at[i, step],
                    plan.member(peers[step], part),
                )
            copy.start()
            copies.append(copy)
        arrivals.append(copies)
    gain_row, shift_row, embed_row = row(gain), row(shift), row(embed)
    bias_q_row, bias_v_row = row(bias_q), row(bias_v)
    waits, shared = [], []

    def save(index, src, dst):
        copy = pltpu.make_async_copy(src, dst, out_sem.at[index])
        copy.start()
        waits.append(copy)

    for step in range(n):
        source = lax.rem(me + n - step, n)
        for copy in arrivals[step]:
            if step == 0:
                copy.wait()
            else:
                copy.wait_recv()
        masked = columns(mask_in[source]) == 1
        start = jnp.where(masked, embed_row, taken[source].astype(F32))
        start_buf[source] = start.astype(BF16)
        hat, _ = normalize(start)
        normed = (hat * gain_row + shift_row).astype(BF16)
        project = mm(normed, w_ref[...])
        queries = (project[:, :D] + bias_q_row).astype(BF16)
        q_buf[source] = (queries.astype(F32) * SCALE).astype(BF16)
        kv_buf[part, source, :, :D] = project[:, D : 2 * D].astype(BF16)
        kv_buf[part, source, :, D:] = (project[:, 2 * D :] + bias_v_row).astype(BF16)
        for other in range(1, plan.share):
            copy = remote(
                kv_buf.at[part, source], kv_buf.at[part, source], kv_send.at[other, step],
                kv_recv.at[other, step], plan.sharer(sharers[other]),
            )
            copy.start()
            shared.append(copy)
    for step in range(n):
        if step == 0:
            copy = pltpu.make_async_copy(out_grad.at[me], grad_out.at[me], local_sem.at[0])
        else:
            copy = remote(
                out_grad.at[peers[step]], grad_out.at[me], grad_send.at[step], grad_recv.at[step],
                plan.member(peers[step], part),
            )
        copy.start()
        waits.append(copy)
    save(0, start_buf, start_out)
    save(1, q_buf, q_out)
    save(2, mask_in, mask_out)
    save(3, target_in, target_out)
    for i in range(n):
        at = slice(i * block_rows, (i + 1) * block_rows)
        qt_buf[:, at] = q_buf[i].T
    save(4, qt_buf, qt_out)
    for copy in shared:
        copy.wait()
    length = lengths[me]
    first = kv_buf[0, 0, 0:1, :D]
    for i in range(plan.share):
        for b in range(n):
            begin = i * rows + b * block_rows
            at = slice(begin, begin + block_rows)
            ids = lax.broadcasted_iota(jnp.int32, (block_rows, 1), 0) + begin
            live = plan.key_time(ids) < length
            k_buf[at, :] = jnp.where(live, kv_buf[i, b, :, :D], first)
            value = kv_buf[i, b, :, D:]
            value = jnp.where(live, value, jnp.zeros_like(value))
            v_buf[at, :] = value
            turned = value.T
            ids = lax.broadcasted_iota(jnp.int32, (16, block_rows), 1) + begin
            top = lax.broadcasted_iota(jnp.int32, (16, block_rows), 0) == 0
            count = jnp.where((plan.key_time(ids) < length) & top, 1.0, 0.0).astype(BF16)
            for h in range(HEADS):
                vt_buf[h, :HEAD_DIM, at] = turned[h * HEAD_DIM : (h + 1) * HEAD_DIM, :]
                vt_buf[h, HEAD_DIM:, at] = count
    save(5, k_buf, k_out)
    save(6, v_buf, v_out)

    width = score_a.shape[1]
    spans = rows // width
    items = HEADS * spans
    lane = lax.broadcasted_iota(jnp.int32, (1, PAIR), 1)

    def score(item, buf):
        head, span = item // spans, item % spans
        pair = pl.ds(pl.multiple_of(head // 2 * PAIR, PAIR), PAIR)
        at = pl.ds(pl.multiple_of(span * width, width), width)
        k_own = jnp.where(lane // HEAD_DIM == head % 2, k_buf[:, pair], jnp.zeros((), BF16))
        scores = mm(k_own, qt_buf[pair, at])
        buf[...] = scores
        return jnp.max(scores, axis=0, keepdims=True)

    def blend(item, buf, top):
        head, span = item // spans, item % spans
        at = pl.ds(pl.multiple_of(span * width, width), width)
        raised = jnp.exp(buf[...] - top).astype(BF16)
        out = mm(vt_buf[head], raised)
        row_total = out[HEAD_DIM : HEAD_DIM + 1, :]
        into = pl.ds(pl.multiple_of(head * HEAD_DIM, HEAD_DIM), HEAD_DIM)
        mixed_buf[into, at] = (out[:HEAD_DIM, :] / row_total).astype(BF16)
        total_buf[head, :, at] = top + jnp.log(row_total)

    def two(i, top_a):
        top_b = score(2 * i + 1, score_b)
        blend(2 * i, score_a, top_a)
        top_a = score(2 * i + 2, score_a)
        blend(2 * i + 1, score_b, top_b)
        return top_a

    top_a = lax.fori_loop(0, items // 2 - 1, two, score(0, score_a))
    top_b = score(items - 1, score_b)
    blend(items - 2, score_a, top_a)
    blend(items - 1, score_b, top_b)
    save(7, mixed_buf, mixed_out)
    save(8, total_buf, total_out)
    for step in range(1, n):
        for copy in arrivals[step]:
            copy.wait_send()
    for copy in waits:
        copy.wait()


def front(plan, lengths, patches, mask, target, out_grad, embed, gain, shift, w_qkv, bias_q, bias_v):
    n, rows, keys, block_rows = plan.clips, plan.rows, plan.keys, plan.block_rows
    width = min(512, rows)
    assert HEADS * (rows // width) % 2 == 0
    dma = pltpu.SemaphoreType.DMA
    blocks = (n, block_rows, D)
    total = (HEADS, 1, rows)
    shapes = [
        (blocks, BF16), (blocks, BF16), ((D, rows), BF16), ((keys, D), BF16), ((keys, D), BF16),
        ((D, rows), BF16), (total, F32), (mask.shape, jnp.int32), (mask.shape, jnp.int32),
        (blocks, BF16),
    ]
    return pl.pallas_call(
        functools.partial(front_kernel, plan),
        out_shape=[jax.ShapeDtypeStruct(shape, kind) for shape, kind in shapes],
        in_specs=[pl.BlockSpec(memory_space=pltpu.SMEM)] + [ANY] * 4 + [VMEM] * 6,
        out_specs=[ANY] * 10,
        scratch_shapes=[
            pltpu.VMEM(blocks, BF16),
            pltpu.VMEM(mask.shape, jnp.int32),
            pltpu.VMEM(mask.shape, jnp.int32),
            pltpu.VMEM(blocks, BF16),
            pltpu.VMEM(blocks, BF16),
            pltpu.VMEM((D, rows), BF16),
            pltpu.VMEM((plan.share, n, block_rows, 2 * D), BF16),
            pltpu.VMEM((keys, D), BF16),
            pltpu.VMEM((keys, D), BF16),
            pltpu.VMEM((HEADS, HEAD_DIM + 16, keys), BF16),
            pltpu.VMEM((D, rows), BF16),
            pltpu.VMEM(total, F32),
            pltpu.VMEM((keys, width), F32),
            pltpu.VMEM((keys, width), F32),
            dma((3, n)), dma((3, n)), dma((3,)),
            dma((plan.share, n)), dma((plan.share, n)), dma((n,)), dma((n,)), dma((9,)),
        ],
        compiler_params=pltpu.CompilerParams(
            collective_id=0, has_side_effects=True, vmem_limit_bytes=VMEM_LIMIT
        ),
        name="front",
    )(lengths, patches, mask, target, out_grad, embed, gain, shift, w_qkv, bias_q, bias_v)


def gelu_parts(rows):
    lower = 0.5 * (1.0 + lax.erf(rows * 0.7071067811865476))
    slope = lower + rows * (jnp.exp(-0.5 * rows * rows) * 0.3989422804014327)
    return rows * lower, slope


class Ring:
    def __init__(self, cut, at, half_src, own_half, core_in, mine, plane_in, part_buf, depth_in, total, sems):
        self.cut, self.at = cut, at
        self.half_src, self.own_half, self.core_in, self.mine = half_src, own_half, core_in, mine
        self.plane_in, self.part_buf, self.depth_in, self.total = plane_in, part_buf, depth_in, total
        self.core_sem, self.plane_sem, self.depth_sem, self.up_sem, self.wide_sem = sems

    def core_copy(self):
        return remote(
            self.half_src, self.core_in, self.core_sem.at[0], self.core_sem.at[1], self.at.partner
        )

    def plane_copies(self):
        chunk = self.cut.chunk
        return [
            remote(
                self.mine.at[spot(self.at.planes[k] * chunk, chunk)], self.plane_in.at[k],
                self.plane_sem.at[0, k], self.plane_sem.at[1, k], self.at.in_plane[k],
            )
            for k in range(1, self.cut.n_plane)
        ]

    def depth_copies(self):
        piece, copies = self.cut.piece, []
        for k in range(1, self.cut.n_depth):
            if self.cut.scatter:
                src = self.part_buf.at[spot(self.at.depths[k] * piece, piece)]
                dst = self.depth_in.at[k]
            else:
                src = dst = self.depth_in.at[self.at.depth]
            copies.append(
                remote(
                    src, dst, self.depth_sem.at[0, k], self.depth_sem.at[1, k], self.at.in_depth[k]
                )
            )
        return copies

    def same(self, first, count, sems, k, device):
        own = spot(first, count)
        return remote(self.total.at[own], self.total.at[own], sems.at[0, k], sems.at[1, k], device)

    def home(self):
        return self.at.core * self.cut.half + self.at.plane * self.cut.chunk

    def up_copies(self):
        first = self.home() + self.at.depth * self.cut.piece
        return [
            self.same(first, self.cut.piece, self.up_sem, k, self.at.in_depth[k])
            for k in range(1, self.cut.n_depth)
        ]

    def wide_copies(self):
        return [
            self.same(self.home(), self.cut.chunk, self.wide_sem, k, self.at.in_plane[k])
            for k in range(1, self.cut.n_plane)
        ]

    def last_copy(self):
        own = spot(self.at.core * self.cut.half, self.cut.half)
        return remote(
            self.total.at[own], self.total.at[own], self.core_sem.at[2], self.core_sem.at[3],
            self.at.partner,
        )

    def begin(self):
        self.core_copy().start()

    def to_plane(self):
        self.core_copy().wait()
        own = self.own_half[...].astype(F32) + self.core_in[...].astype(F32)
        self.mine[...] = own.astype(BF16)
        for copy in self.plane_copies():
            copy.start()

    def to_depth(self):
        chunk = self.cut.chunk
        mine = self.mine[spot(self.at.plane * chunk, chunk), :].astype(F32)
        for k, copy in enumerate(self.plane_copies()):
            copy.wait()
            mine = mine + self.plane_in[k + 1].astype(F32)
        if self.cut.scatter:
            self.part_buf[...] = mine.astype(BF16)
        else:
            self.depth_in[self.at.depth] = mine.astype(BF16)
        for copy in self.depth_copies():
            copy.start()

    def back_up(self):
        piece, copies = self.cut.piece, self.depth_copies()
        if self.cut.scatter:
            mine = self.part_buf[spot(self.at.depth * piece, piece), :].astype(F32)
            for k, copy in enumerate(copies):
                copy.wait()
                mine = mine + self.depth_in[k + 1].astype(F32)
            self.total[spot(self.home() + self.at.depth * piece, piece), :] = mine.astype(BF16)
            for copy in self.up_copies():
                copy.start()
        else:
            for copy in copies:
                copy.wait()
            mine = self.depth_in[0].astype(F32)
            for k in range(1, self.cut.n_depth):
                mine = mine + self.depth_in[k].astype(F32)
            self.total[spot(self.home(), self.cut.chunk), :] = mine.astype(BF16)

    def back_wide(self):
        if self.cut.scatter:
            for copy in self.up_copies():
                copy.wait()
        for copy in self.wide_copies():
            copy.start()

    def back_core(self):
        for copy in self.wide_copies():
            copy.wait()
        self.last_copy().start()

    def turn(self):
        self.to_depth()
        self.back_up()
        self.back_wide()

    def end(self):
        self.last_copy().wait()


class Cut:
    def __init__(self, plan, rows, width, flat=False):
        self.rows, self.width = rows, width
        self.n_plane = plan.freq * plan.batch
        self.n_depth = plan.tm // 2
        self.flat = flat and rows // 2 % (16 * self.n_plane * self.n_depth) == 0
        if self.flat:
            self.n_plane, self.n_depth = self.n_plane * self.n_depth, 1
        self.half = rows // 2
        self.chunk = self.half // self.n_plane
        self.piece = self.chunk // self.n_depth
        self.scatter = self.piece % 16 == 0 and self.piece * self.n_depth == self.chunk
        assert self.chunk * self.n_plane == self.half and self.chunk % 16 == 0

    def buffers(self):
        depth = self.piece if self.scatter else self.chunk
        shapes = [
            (self.half,), (self.half,), (self.n_plane, self.chunk), (self.chunk,),
            (self.n_depth, depth), (self.rows,),
        ]
        return [pltpu.VMEM(shape + (self.width,), BF16) for shape in shapes]

    def semaphores(self):
        dma = pltpu.SemaphoreType.DMA
        return [
            dma((4,)), dma((2, self.n_plane)), dma((2, self.n_depth)), dma((2, self.n_depth)),
            dma((2, self.n_plane)),
        ]


class Place:
    def __init__(self, plan):
        time_id = lax.axis_index("tm")
        n_plane, n_depth = plan.freq * plan.batch, plan.tm // 2
        self.core, self.depth = time_id % 2, time_id // 2
        self.plane = lax.axis_index("freq") * plan.batch + lax.axis_index("batch")
        self.partner = {"tm": time_id + 1 - 2 * self.core}
        self.planes = [lax.rem(self.plane + k, n_plane) for k in range(n_plane)]
        self.depths = [lax.rem(self.depth + k, n_depth) for k in range(n_depth)]
        self.in_plane = [{"freq": v // plan.batch, "batch": v % plan.batch} for v in self.planes]
        self.in_depth = [{"tm": v * 2 + self.core} for v in self.depths]


class Flat:
    def __init__(self, plan, place):
        n_depth = plan.tm // 2
        count = plan.freq * plan.batch * n_depth
        self.core, self.partner, self.depth, self.in_depth = place.core, place.partner, 0, [None]
        self.plane = place.plane * n_depth + place.depth
        self.planes = [lax.rem(self.plane + k, count) for k in range(count)]
        self.in_plane = [
            {
                "freq": v // n_depth // plan.batch,
                "batch": v // n_depth % plan.batch,
                "tm": v % n_depth * 2 + place.core,
            }
            for v in self.planes
        ]


def spot(first, count):
    return pl.ds(pl.multiple_of(first, 16), count)


def rest_kernel(
    plan, wide_cut, small_cuts, lengths,
    mixed_in, start_in, grad_in, targets_in, w_out_in, w_up_in, w_down_in, w_qkv_in,
    q_in, qt_in, k_in, v_in, log_total, mask, target,
    ln1_gain, ln1_shift, bias_out, ln2_gain, ln2_shift, bias_up, bias_down,
    block_grid, input_grad, wide_out, small_out, vec_out,
    mixed, start, grad, targets, w_out, w_up, w_down, w_qkv, q_ref, qt_ref, k_ref, v_ref,
    middle, second, down_sum, second_sum, act_buf, up_buf, payload, small_pay, do_ref, dot_ref,
    center, block_out,
    kt_buf, score_a, score_b, prob_a, prob_b, dqt_sum, dk_all, dv_all, dk_in, dv_in,
    rows_buf, vec_buf, vec_core, vec_plane, vec_depth,
    load_sem, grid_ss, grid_rs, kv_ss, kv_rs, rows_ss, rows_rs, local_sem, out_sem,
    vec_core_sem, vec_plane_sem, vec_depth_sem,
    *rest,
):
    n, rows, keys, block_rows = plan.clips, plan.rows, plan.keys, plan.block_rows
    me, part = plan.place()
    at = Place(plan)
    last_cut = small_cuts[-1]
    flat = Flat(plan, at) if last_cut.flat else at
    n_plane, n_depth = wide_cut.n_plane, wide_cut.n_depth
    peers = [lax.rem(me + k, n) for k in range(n)]
    sharers = [lax.rem(part + k, plan.share) for k in range(plan.share)]
    length = lengths[me]

    loads = [
        pltpu.make_async_copy(src, dst, load_sem.at[i])
        for i, (src, dst) in enumerate(
            (
                (mixed_in, mixed), (w_out_in, w_out), (start_in, start), (w_up_in, w_up),
                (w_down_in, w_down), (grad_in, grad), (targets_in.at[me], targets),
                (k_in, k_ref), (qt_in, qt_ref), (v_in, v_ref), (q_in, q_ref), (w_qkv_in, w_qkv),
            )
        )
    ]
    for copy in loads:
        copy.start()
    greet(
        [plan.member(peers[k], part) for k in range(1, n)]
        + [plan.sharer(sharers[k]) for k in range(1, plan.share)]
        + [at.partner]
        + (flat.in_plane[1:] if last_cut.flat else at.in_plane[1:] + at.in_depth[1:])
    )
    steps = FF // CHUNK
    wide, small = [], []
    for i in range(steps):
        mine, rest = rest[:11], rest[11:]
        wide.append(
            Ring(
                wide_cut, at, payload.at[1 - at.core, i], payload.at[at.core, i], *mine[:6], mine[6:]
            )
        )
    for p in range(PAIRS):
        mine, rest = rest[:11], rest[11:]
        small_cut = small_cuts[p]
        away = small_pay.at[p, spot((1 - at.core) * small_cut.half, small_cut.half)]
        own = small_pay.at[p, spot(at.core * small_cut.half, small_cut.half)]
        small.append(Ring(small_cut, flat if small_cut.flat else at, away, own, *mine[:6], mine[6:]))

    tile = min(TILE, rows)
    tiles = [slice(i * tile, (i + 1) * tile) for i in range(rows // tile)]
    gain2, shift2 = row(ln2_gain), row(ln2_shift)
    bias_up_row = row(bias_up)
    vec_buf[...] = jnp.zeros_like(vec_buf)
    for copy in loads[:3]:
        copy.wait()
    for span in tiles:
        rows_in = start[span, :].astype(F32) + mm_tn(mixed[:, span], w_out[...]) + row(bias_out)
        middle[span, :] = rows_in
        hat, _ = normalize(rows_in)
        second[span, :] = (hat * gain2 + shift2).astype(BF16)
    for copy in loads[3:6]:
        copy.wait()
    up_sums = []
    for i in range(steps):
        cols = slice(i * CHUNK, (i + 1) * CHUNK)
        for t, span in enumerate(tiles):
            hidden = mm(second[span, :], w_up[:, cols]) + bias_up_row[:, cols]
            active, slope = gelu_parts(hidden)
            active = active.astype(BF16)
            act_buf[span, :] = active
            down = mm(active, w_down[cols, :])
            grad_up = (mm_nt(grad[span, :], w_down[cols, :]) * slope).astype(BF16)
            up_buf[span, :] = grad_up
            back = mm_nt(grad_up, w_up[:, cols])
            if i == 0:
                down_sum[span, :] = down
                second_sum[span, :] = back
            else:
                down_sum[span, :] += down
                second_sum[span, :] += back
            if t == 0 and i >= 1:
                wide[i - 1].to_plane()
        grad_down = mm_tn(act_buf[...], grad[...]).astype(BF16)
        for t in range(D // LANES):
            payload[0, i, t * CHUNK : (t + 1) * CHUNK, :] = grad_down[:, t * LANES : (t + 1) * LANES]
        grad_w = mm_tn(second[...], up_buf[...]).astype(BF16)
        for t in range(CHUNK // LANES):
            payload[1, i, t * D : (t + 1) * D, :] = grad_w[:, t * LANES : (t + 1) * LANES]
        up_sums.append(sum_rows(up_buf[...].astype(F32)))
        wide[i].begin()
        if i >= 2:
            wide[i - 2].to_depth()
    up_sums = jnp.concatenate(up_sums, axis=1)
    for i in range(FF // D):
        vec_buf[9 + i : 10 + i, :] = up_sums[:, i * D : (i + 1) * D]
    vec_buf[8:9, :] = sum_rows(grad[...].astype(F32))
    loads[6].wait()
    home_copies = []
    cand = lax.broadcasted_iota(jnp.int32, (1, targets.shape[0]), 1)
    total_hit = jnp.zeros((1, 1), F32)
    total_count = jnp.zeros((1, 1), F32)
    per_tile = tile // block_rows
    for t, span in enumerate(tiles):
        result = (middle[span, :] + down_sum[span, :] + row(bias_down)).astype(BF16)
        for b in range(per_tile):
            block_out[t * per_tile + b] = result[b * block_rows : (b + 1) * block_rows, :]
        hat, scale = normalize(middle[span, :])
        grad_second = second_sum[span, :]
        vec_buf[6:7, :] += sum_rows(grad_second * hat)
        vec_buf[7:8, :] += sum_rows(grad_second)
        back = grad[span, :].astype(F32) + normalize_back(grad_second * gain2, hat, scale)
        second_sum[span, :] = back
        branch = back.astype(BF16)
        up_buf[span, :D] = branch
        vec_buf[5:6, :] += sum_rows(branch.astype(F32))
        do_ref[span, :] = mm_nt(branch, w_out[...]).astype(BF16)
        down = mm_nt(w_out[...], branch).astype(BF16)
        dot_ref[:, span] = down
        product = down.astype(F32) * mixed[:, span].astype(F32)
        for h in range(HEADS):
            center[h, :, span] = sum_rows(product[h * HEAD_DIM : (h + 1) * HEAD_DIM, :])
        logits = mm_nt(result, targets[...])
        raised = jnp.exp(logits - jnp.max(logits, axis=1, keepdims=True))
        sources = range(t * per_tile, (t + 1) * per_tile)
        target_col = jnp.concatenate([columns(target[s]) for s in sources], axis=0)
        mask_col = jnp.concatenate([columns(mask[s]) for s in sources], axis=0)
        hit = jnp.sum(jnp.where(cand == target_col, raised, 0.0), axis=1, keepdims=True)
        hit = hit / jnp.sum(raised, axis=1, keepdims=True)
        ids = lax.broadcasted_iota(jnp.int32, (tile, 1), 0) + t * tile + part * rows
        counted = jnp.where((plan.key_time(ids) < length) & (mask_col == 1), 1.0, 0.0)
        total_hit += sum_rows(hit * counted)
        total_count += sum_rows(counted)
        if t == 0:
            wide[-1].to_plane()
    home_copies.append(
        pltpu.make_async_copy(block_out.at[me], block_grid.at[me], local_sem.at[0])
    )
    for k in range(1, n):
        home_copies.append(
            remote(
                block_out.at[peers[k]], block_grid.at[me], grid_ss.at[k], grid_rs.at[k],
                plan.member(peers[k], part),
            )
        )
    home_copies[0].start()
    wide[-3].back_up()
    wide[-2].to_depth()
    grad_w = mm(mixed[...], up_buf[:, :D]).astype(BF16)
    for p in range(PAIRS):
        small_pay[p, D:, :] = grad_w[p * PAIR : (p + 1) * PAIR, :]
    lane = lax.broadcasted_iota(jnp.int32, (1, D), 1)
    slot = lax.axis_index("batch") * 2 * n + me
    scores = jnp.where(lane == slot, total_hit, 0.0)
    vec_buf[13:14, :] = scores + jnp.where(lane == slot + n, total_count, 0.0)

    gain1, shift1 = row(ln1_gain), row(ln1_shift)
    hat_buf, normed, grad_buf, grad_middle = middle, second, down_sum, second_sum
    for span in tiles:
        hat, _ = normalize(start[span, :].astype(F32))
        hat_buf[span, :] = hat
        normed[span, :] = (hat * gain1 + shift1).astype(BF16)
    loads[7].wait()
    for i in range(keys // 256):
        span = slice(i * 256, (i + 1) * 256)
        ids = lax.broadcasted_iota(jnp.int32, (1, 256), 1) + i * 256
        turned = k_ref[span, :].T
        kt_buf[:, span] = jnp.where(plan.key_time(ids) < length, turned, jnp.zeros_like(turned))
    dqt_sum[...] = jnp.zeros_like(dqt_sum)
    for copy in loads[8:]:
        copy.wait()

    block = score_a.shape[0]
    per_part = rows // block
    lane = lax.broadcasted_iota(jnp.int32, (1, PAIR), 1)
    owns = [lane // HEAD_DIM == e for e in range(2)]
    zero = jnp.zeros((), BF16)
    per_pair = per_part * plan.share
    bodies = PAIRS * per_pair

    def kv_copies(p):
        return [
            remote(
                src.at[p, sharers[k]], dst.at[p, k], kv_ss.at[i, p, k], kv_rs.at[i, p, k],
                plan.sharer(sharers[k]),
            )
            for i, (src, dst) in enumerate(((dk_all, dk_in), (dv_all, dv_in)))
            for k in range(1, plan.share)
        ]

    def send_keys(p):
        for copy in kv_copies(p):
            copy.start()

    def finish_pair(p):
        for copy in kv_copies(p):
            copy.wait()
        cols = slice(p * PAIR, (p + 1) * PAIR)
        parts = [(dqt_sum[cols, :] * SCALE).T.astype(BF16)]
        ids = lax.broadcasted_iota(jnp.int32, (rows, 1), 0) + part * rows
        live = plan.key_time(ids) < length
        for own, buf in ((dk_all, dk_in), (dv_all, dv_in)):
            summed = own[p, part].astype(F32)
            for k in range(1, plan.share):
                summed = summed + buf[p, k].astype(F32)
            parts.append(jnp.where(live, summed, 0.0).astype(BF16))
        vec_buf[3:4, cols] = sum_rows(parts[0].astype(F32))
        vec_buf[4:5, cols] = sum_rows(parts[2].astype(F32))
        project = jnp.concatenate(parts, axis=1)
        small_pay[p, :D, :] = mm_tn(normed[...], project).astype(BF16)
        small[p].begin()
        weights = [w_qkv[:, i * D + p * PAIR : i * D + (p + 1) * PAIR] for i in range(3)]
        back = mm_nt(project, jnp.concatenate(weights, axis=1))
        if p == 0:
            grad_buf[...] = back
        else:
            grad_buf[...] += back

    def save(i, src, dst):
        return pltpu.make_async_copy(src, dst, out_sem.at[i])

    saves = [save(i, wide[i].total, wide_out.at[i]) for i in range(steps)]
    saves += [save(steps + p, small[p].total, small_out.at[p]) for p in range(PAIRS)]

    def wide_end(i):
        wide[i].end()
        saves[i].start()

    def small_end(p):
        small[p].end()
        saves[steps + p].start()

    last_other = per_pair - per_part - 1
    events = [
        (last_other + p * per_pair, functools.partial(send_keys, p)) for p in range(PAIRS)
    ] + [(p * per_pair + per_pair - 1, functools.partial(finish_pair, p)) for p in range(PAIRS - 1)]
    for when, event in (
        (0, wide[0].back_wide), (0, wide[2].to_depth), (1, wide[1].back_up), (2, wide[2].back_up),
        (3, wide[1].back_wide), (3, wide[0].back_core), (4, small[0].to_plane),
        (4, wide[2].back_wide), (4, functools.partial(wide_end, 0)), (6, wide[1].back_core),
        (6, small[0].to_depth), (7, wide[2].back_core), (7, functools.partial(wide_end, 1)),
        (8, small[0].back_up), (8, small[1].to_plane), (8, functools.partial(wide_end, 2)),
        (10, small[0].back_wide), (10, small[1].to_depth),
    ):
        events.append((when * bodies // 12, event))
    for k in range(1, n):
        events.append((GRID_AT[k % len(GRID_AT)] * bodies // 12, home_copies[k].start))

    def body(i, carry):
        pair, order = i // per_pair, i % per_pair
        owner = lax.rem(part + 1 + order // per_part, plan.share)
        begin = order % per_part * block
        span = pl.ds(pl.multiple_of(owner * rows + begin, block), block)
        inside = pl.ds(pl.multiple_of(begin, block), block)
        cols = pl.ds(pl.multiple_of(pair * PAIR, PAIR), PAIR)
        for e, (score_buf, prob_buf) in enumerate(((score_a, prob_a), (score_b, prob_b))):
            score_buf[...] = mm(jnp.where(owns[e], k_ref[span, cols], zero), qt_ref[cols, :])
            prob_buf[...] = mm(jnp.where(owns[e], v_ref[span, cols], zero), dot_ref[cols, :])
        grad_k, grad_v = [], []
        for e, (score_buf, prob_buf) in enumerate(((score_a, prob_a), (score_b, prob_b))):
            head = pl.ds(pl.multiple_of(pair * PAIR + e * HEAD_DIM, HEAD_DIM), HEAD_DIM)
            prob = jnp.exp(score_buf[...] - log_total[2 * pair + e])
            grad_scores = (prob * (prob_buf[...] - center[2 * pair + e])).astype(BF16)
            grad_v.append(mm(prob.astype(BF16), jnp.where(owns[e], do_ref[:, cols], zero)))
            grad_k.append(mm(grad_scores, jnp.where(owns[e], q_ref[:, cols], zero)))
            dqt_sum[head, :] += mm(kt_buf[head, span], grad_scores)
        dk_all[pair, owner, inside, :] = (grad_k[0] + grad_k[1]).astype(BF16)
        dv_all[pair, owner, inside, :] = (grad_v[0] + grad_v[1]).astype(BF16)
        for when, event in events:
            pl.when(i == when)(event)
        return carry

    lax.fori_loop(0, bodies, body, 0)
    finish_pair(PAIRS - 1)

    row_copies = []
    grad_embed = jnp.zeros((1, D), F32)
    grad_gain = jnp.zeros((1, D), F32)
    grad_shift = jnp.zeros((1, D), F32)
    for k in range(n):
        owner = peers[k]
        span = spot(owner * block_rows, block_rows)
        _, scale = normalize(start[span, :].astype(F32))
        hat = hat_buf[span, :]
        grad_normed = grad_buf[span, :]
        grad_gain += sum_rows(grad_normed * hat)
        grad_shift += sum_rows(grad_normed)
        grad_start = grad_middle[span, :] + normalize_back(grad_normed * gain1, hat, scale)
        masked = columns(mask[owner]) == 1
        grad_embed += sum_rows(jnp.where(masked, grad_start, 0.0))
        rows_buf[owner] = jnp.where(masked, 0.0, grad_start).astype(BF16)
        if k == 0:
            copy = pltpu.make_async_copy(rows_buf.at[owner], input_grad.at[me], local_sem.at[1])
        else:
            copy = remote(
                rows_buf.at[owner], input_grad.at[me], rows_ss.at[k], rows_rs.at[k],
                plan.member(owner, part),
            )
        row_copies.append(copy)
        if k < WAVES[0]:
            copy.start()
        if k == 0:
            small[2].to_plane()
        if k == 2:
            small[1].back_up()
        if k == 5:
            small[0].back_core()
    vec_buf[0:1, :] = grad_embed
    vec_buf[1:2, :] = grad_gain
    vec_buf[2:3, :] = grad_shift
    vec_copy = remote(vec_buf, vec_core, vec_core_sem.at[0], vec_core_sem.at[1], at.partner)
    vec_copy.start()
    vec_copy.wait()
    vec_plane[at.plane] = vec_buf[...] + vec_core[...]
    vec_plane_copies = []
    for k in range(1, n_plane):
        copy = remote(
            vec_plane.at[at.plane], vec_plane.at[at.plane], vec_plane_sem.at[0, k],
            vec_plane_sem.at[1, k], at.in_plane[k],
        )
        copy.start()
        vec_plane_copies.append(copy)
    small[2].to_depth()
    for copy in row_copies[WAVES[0] : WAVES[1]]:
        copy.start()
    small[1].back_wide()
    small_end(0)
    for copy in vec_plane_copies:
        copy.wait()
    summed = vec_plane[0]
    for k in range(1, n_plane):
        summed = summed + vec_plane[k]
    vec_depth[at.depth] = summed
    vec_depth_copies = []
    for k in range(1, n_depth):
        copy = remote(
            vec_depth.at[at.depth], vec_depth.at[at.depth], vec_depth_sem.at[0, k],
            vec_depth_sem.at[1, k], at.in_depth[k],
        )
        copy.start()
        vec_depth_copies.append(copy)
    small[2].back_up()
    for copy in row_copies[WAVES[1] :]:
        copy.start()
    small[1].back_core()
    small[2].back_wide()
    small_end(1)
    for copy in vec_depth_copies:
        copy.wait()
    summed = vec_depth[0]
    for k in range(1, n_depth):
        summed = summed + vec_depth[k]
    vec_out[...] = summed
    small[2].back_core()
    small_end(2)
    for copy in row_copies + home_copies + saves:
        copy.wait()


def rest(plan, lengths, mixed, start, grad, targets, weights, q, qt, k, v, log_total, mask, target, vectors):
    n, rows, keys = plan.clips, plan.rows, plan.keys
    steps = FF // CHUNK
    wide_cut = Cut(plan, 2 * CHUNK * D // LANES, LANES)
    small_cuts = [Cut(plan, D + PAIR, D, flat=False) for p in range(PAIRS)]
    small_cut = small_cuts[0]
    dma = pltpu.SemaphoreType.DMA
    vec_shape = (VEC_ROWS, D)
    block = min(512, rows)
    blocks = (n, plan.block_rows, D)
    shared = pltpu.VMEM((PAIRS, plan.share, rows, PAIR), BF16)
    pane = pltpu.VMEM((block, rows), F32)
    loaded = (mixed, start, grad, targets[0], *weights, q, qt, k, v)
    rings = []
    for cut in [wide_cut] * steps + small_cuts:
        rings += cut.buffers() + cut.semaphores()
    return pl.pallas_call(
        functools.partial(rest_kernel, plan, wide_cut, small_cuts),
        out_shape=[
            jax.ShapeDtypeStruct(blocks, BF16),
            jax.ShapeDtypeStruct(blocks, BF16),
            jax.ShapeDtypeStruct((steps, wide_cut.rows, LANES), BF16),
            jax.ShapeDtypeStruct((PAIRS, small_cut.rows, D), BF16),
            jax.ShapeDtypeStruct(vec_shape, F32),
        ],
        in_specs=[pl.BlockSpec(memory_space=pltpu.SMEM)] + [ANY] * 12 + [VMEM] * 10,
        out_specs=[ANY] * 4 + [VMEM],
        scratch_shapes=[pltpu.VMEM(x.shape, BF16) for x in loaded]
        + [
            pltpu.VMEM((rows, D), F32), pltpu.VMEM((rows, D), BF16),
            pltpu.VMEM((rows, D), F32), pltpu.VMEM((rows, D), F32),
            pltpu.VMEM((rows, CHUNK), BF16), pltpu.VMEM((rows, CHUNK), BF16),
            pltpu.VMEM((2, steps, CHUNK * D // LANES, LANES), BF16),
            pltpu.VMEM((PAIRS, small_cut.rows, D), BF16),
            pltpu.VMEM((rows, D), BF16), pltpu.VMEM((D, rows), BF16),
            pltpu.VMEM((HEADS, 1, rows), F32), pltpu.VMEM(blocks, BF16),
            pltpu.VMEM((D, keys), BF16), pane, pane, pane, pane, pltpu.VMEM((D, rows), F32),
            shared, shared, shared, shared,
            pltpu.VMEM(blocks, BF16),
            pltpu.VMEM(vec_shape, F32),
            pltpu.VMEM(vec_shape, F32),
            pltpu.VMEM((wide_cut.n_plane,) + vec_shape, F32),
            pltpu.VMEM((wide_cut.n_depth,) + vec_shape, F32),
            dma((12,)), dma((n,)), dma((n,)),
            dma((2, PAIRS, plan.share)), dma((2, PAIRS, plan.share)), dma((n,)), dma((n,)),
            dma((2,)), dma((steps + PAIRS,)), dma((2,)),
            dma((2, wide_cut.n_plane)), dma((2, wide_cut.n_depth)),
            *rings,
        ],
        compiler_params=pltpu.CompilerParams(
            collective_id=1, has_side_effects=True, vmem_limit_bytes=VMEM_LIMIT
        ),
        name="rest",
    )(lengths, mixed, start, grad, targets, *weights, q, qt, k, v, log_total, mask, target, *vectors)


def unpack_kernel(plan, small, wide, vec, *outs):
    w_qkv, w_out, w_up, w_down, bias_up, soft = outs[:6]
    step = pl.program_id(0)
    for t in range(D // LANES):
        at = slice(t * LANES, (t + 1) * LANES)
        w_down[:, at] = wide[0, 0, t * CHUNK : (t + 1) * CHUNK, :].astype(F32)
        part = pl.ds(pl.multiple_of(t * D + step * PAIR, PAIR), PAIR)
        w_qkv[:, part] = small[0, :D, at].astype(F32)
    for t in range(CHUNK // LANES):
        w_up[:, t * LANES : (t + 1) * LANES] = wide[0, 1, t * D : (t + 1) * D, :].astype(F32)
    w_out[...] = small[0, D:, :].astype(F32)

    @pl.when(step == 0)
    def _():
        for i, out in enumerate(outs[6:]):
            out[...] = vec[i, :]
        for i in range(FF // D):
            bias_up[i * D : (i + 1) * D] = vec[9 + i, :]
        scores = vec[13:14, :]
        n = plan.clips
        lane = lax.broadcasted_iota(jnp.int32, (n, D), 1)
        sub = lax.broadcasted_iota(jnp.int32, (n, D), 0)
        slot = lax.axis_index("batch") * 2 * n + sub
        hits = jnp.sum(jnp.where(lane == slot, scores, 0.0), axis=1, keepdims=True)
        counts = jnp.sum(jnp.where(lane == slot + n, scores, 0.0), axis=1, keepdims=True)
        means = hits / jnp.maximum(counts, 1.0)
        soft[...] = jnp.sum(jnp.where(lane == sub, means, 0.0), axis=0)[:n]


def unpack(plan, small, wide, vec):
    vector = jax.ShapeDtypeStruct((D,), F32)
    steps = FF // CHUNK
    assert steps == PAIRS

    def full(shape):
        return pl.BlockSpec(shape, lambda i: (0,) * len(shape))

    return pl.pallas_call(
        functools.partial(unpack_kernel, plan),
        grid=(steps,),
        in_specs=[
            pl.BlockSpec((1, D + PAIR, D), lambda i: (i, 0, 0)),
            pl.BlockSpec((1, 2, CHUNK * D // LANES, LANES), lambda i: (i, 0, 0, 0)),
            full((VEC_ROWS, D)),
        ],
        out_specs=[
            full((D, 3 * D)),
            pl.BlockSpec((PAIR, D), lambda i: (i, 0)),
            pl.BlockSpec((D, CHUNK), lambda i: (0, i)),
            pl.BlockSpec((CHUNK, D), lambda i: (i, 0)),
            full((FF,)),
            full((plan.clips,)),
        ]
        + [full((D,))] * 9,
        out_shape=[
            jax.ShapeDtypeStruct((D, 3 * D), F32),
            jax.ShapeDtypeStruct((D, D), F32),
            jax.ShapeDtypeStruct((D, FF), F32),
            jax.ShapeDtypeStruct((FF, D), F32),
            jax.ShapeDtypeStruct((FF,), F32),
            jax.ShapeDtypeStruct((plan.clips,), F32),
        ]
        + [vector] * 9,
        compiler_params=pltpu.CompilerParams(vmem_limit_bytes=VMEM_LIMIT),
        name="unpack",
    )(small, wide.reshape(steps, 2, CHUNK * D // LANES, LANES), vec)


def per_device(
    plan,
    patches, patch_mask, clip_lengths, target_index, targets, out_grad,
    mask_embed, ln1_gain, ln1_shift, w_qkv, bias_q, bias_v, w_out, bias_out,
    ln2_gain, ln2_shift, w_up, bias_up, w_down, bias_down,
):
    n, rows, block_rows = plan.clips, plan.rows, plan.block_rows
    (start, queries, queries_t, key_rows, value_rows, mixed, log_total, mask, target, grad) = front(
        plan, clip_lengths, patches.reshape(n, block_rows, D), patch_mask, target_index,
        out_grad.reshape(n, block_rows, D), mask_embed, ln1_gain, ln1_shift, w_qkv, bias_q, bias_v,
    )
    block_grid, input_grad, wide, small, vec = rest(
        plan, clip_lengths, mixed, start.reshape(rows, D), grad.reshape(rows, D), targets,
        (w_out, w_up, w_down, w_qkv), queries.reshape(rows, D), queries_t, key_rows, value_rows,
        log_total, mask, target,
        (ln1_gain, ln1_shift, bias_out, ln2_gain, ln2_shift, bias_up, bias_down),
    )
    grad_w_qkv, grad_w_out, grad_w_up, grad_w_down, grad_bias_up, soft_accuracy, *vectors = unpack(
        plan, small, wide, vec
    )
    (grad_mask_embed, grad_ln1_gain, grad_ln1_shift, grad_bias_q, grad_bias_v, grad_bias_out,
     grad_ln2_gain, grad_ln2_shift, grad_bias_down) = vectors
    return (
        block_grid.reshape(patches.shape), input_grad.reshape(patches.shape), grad_mask_embed,
        grad_ln1_gain, grad_ln1_shift, grad_w_qkv, grad_bias_q, grad_bias_v, grad_w_out,
        grad_bias_out, grad_ln2_gain, grad_ln2_shift, grad_w_up, grad_bias_up, grad_w_down,
        grad_bias_down, soft_accuracy,
    )


def solution(mesh):
    rows = P("batch", "freq", "tm", None)
    whole = P()
    in_specs = (
        rows, P("batch", "freq", "tm"), P("batch"), P("batch", "freq", "tm"),
        P("batch", None, None), rows,
    ) + (whole,) * 14
    out_specs = (rows, rows) + (whole,) * 14 + (P("batch"),)

    def body(*args):
        return per_device(Plan(mesh, args[0]), *args)

    return jax.shard_map(
        body, mesh=mesh, in_specs=in_specs, out_specs=out_specs, check_vma=False
    )
```
